32 devices in a mesh: groups: 2 (over y), dp: 4 (over z), mp: 2 (over x), pair: 2 (over core).
Axes of the slice: x: 2, y: 2, z: 4, core: 2. Of those that a mesh axis runs over, the one named last changes fastest.
Arguments:
- hidden_input: bfloat16 [12288, 2048], P(('groups', 'dp', 'pair'), 'mp'), parts along dimension 0, may hold values from -6 to 6
- key_weight_frozen: bfloat16 [2048, 1024], P(None, 'mp'), may hold values from -0.125 to 0.125
- adapter_down: bfloat16 [16, 2048, 64], P(('groups', 'dp'), 'mp'), parts along dimension 0, may hold values from -0.125 to 0.125
- adapter_up: bfloat16 [16, 64, 1024], P(('groups', 'dp'), None, 'mp'), parts along dimension 0, may hold values from -0.75 to 0.75
- output_cotangent: bfloat16 [12288, 1024], P(('groups', 'dp', 'pair'), 'mp'), parts along dimension 0, may hold values from -0.119628906 to 0.119628906
- block_owner_index: int32 [192], P(('groups', 'dp', 'pair')), parts along dimension 0, may hold values from 0 to 3, as said below
- send_site_table: int32 [8, 2, 4], P(('groups', 'dp')), parts along dimension 0, may hold values from 0 to 1
Outputs:
- key_projection_output: bfloat16 [12288, 1024], P(('groups', 'dp', 'pair'), 'mp'), parts along dimension 0
- input_gradient: bfloat16 [12288, 2048], P(('groups', 'dp', 'pair'), 'mp'), parts along dimension 0
- down_gradient: float32 [16, 2048, 64], P(('groups', 'dp'), 'mp'), parts along dimension 0
- up_gradient: float32 [16, 64, 1024], P(('groups', 'dp'), None, 'mp'), parts along dimension 0
The draws below stay inside these ranges and needn't reach their ends.
There are 2 independent parts, one for each index of `groups`. The reference program is written for one: setup_inputs(seed, part) draws one part's arguments, and reference() takes and returns one part's arrays. A program takes and returns all parts, laid end to end along the dimension named above; an argument that names none is the same for every part. Nothing has to cross between parts.
Inputs may be any that keep to these rules, and one draw needn't show every extreme that they name: `block_owner_index`: within the 12 blocks of one device equal values stand in consecutive runs, and exactly 4 different values occur.
All inputs are finite; a program needn't handle non-finite values.
Results may differ from the reference program's by a relative error of at most 0.014.
Values may be sent and summed in bfloat16 or wider, within the bound.
No kernel may reach another device: no remote copies, remote signals or barrier semaphores. Data moves between devices by JAX's collectives and lax.ppermute only.
A program may use at most 64 MiB of HBM per device.

```python
import jax
import jax.numpy as jnp
from jax import lax

MODEL_WIDTH = 2048
KEY_OUT_WIDTH = 1024
ADAPTER_RANK = 64
BLOCK = 64
S_DEV = 2
BLK_DEV = 12
TOKEN_TOTAL = 6144
BLOCKS = 96
SITE_TOTAL = 8
N_DP = 4
N_MP = 2
N_PAIR = 2


def draw_block_owner_index(key, part):
    key = jax.random.fold_in(key, 11)
    used_count = min(BLK_DEV, N_DP)
    device_keys = jax.random.split(key, N_DP * N_PAIR)

    def single_device_body(dev_key):
        key_perm, key_extra = jax.random.split(dev_key)
        ordering = jax.random.permutation(key_perm, N_DP).astype(jnp.int32)
        extra_picks = jax.random.randint(key_extra, (BLK_DEV - used_count,), 0, used_count).astype(jnp.int32)
        chosen = jnp.sort(jnp.concatenate([jnp.arange(used_count, dtype=jnp.int32), extra_picks]))
        return ordering[chosen]
    return jax.vmap(single_device_body)(device_keys).reshape(-1).astype(jnp.int32)


def place_ends(result, key, least, top_value):
    shape = result.shape
    index_at = [jax.random.randint(jax.random.fold_in(key, axis), (), 0, shape[axis]) for axis in range(len(shape))]
    result = result.at[tuple(index_at)].set(least)
    longest = shape.index(max(shape))
    index_at[longest] = (index_at[longest] + 1) % shape[longest]
    return result.at[tuple(index_at)].set(top_value)


def block_levels(stream_key, extent, cuts, smallest, top_value):
    def one(position, shards_of):
        steps = jax.random.uniform(jax.random.fold_in(jax.random.fold_in(stream_key, 6), position), (shards_of,), jnp.float32, smallest / len(cuts), top_value / len(cuts))
        return jnp.repeat(jnp.exp(steps), extent[position] // shards_of).reshape((-1,) + (1,) * (len(extent) - position - 1))

    loudness = one(*cuts[0])
    for cut in cuts[1:]:
        loudness = loudness * one(*cut)
    return loudness


def bell_draw(own_key, shape, scale, bound, pieces=(), held_as=jnp.bfloat16):
    level = block_levels(own_key, shape, pieces, -0.22, 0.18) if pieces else 1.0
    entries = jax.random.normal(own_key, shape, jnp.float32) * scale * level
    return jnp.minimum(jnp.maximum(entries, -bound), bound).astype(held_as)


def setup_inputs(seed: int = 0, part: int = 0) -> dict:
    keys = jax.random.split(jax.random.key(seed), 8)
    own_keys = jax.random.split(jax.random.fold_in(keys[7], part), 8)
    hidden_input = bell_draw(own_keys[0], (TOKEN_TOTAL, MODEL_WIDTH), 1.0, 6.0, ((0, 8), (1, 2)))
    key_weight_frozen = bell_draw(keys[1], (MODEL_WIDTH, KEY_OUT_WIDTH), MODEL_WIDTH ** -0.5, 0.125, ((1, 2),))
    adapter_down = bell_draw(own_keys[2], (SITE_TOTAL, MODEL_WIDTH, ADAPTER_RANK), MODEL_WIDTH ** -0.5, 0.125, ((0, 4), (1, 2)))
    adapter_up = bell_draw(own_keys[3], (SITE_TOTAL, ADAPTER_RANK, KEY_OUT_WIDTH), ADAPTER_RANK ** -0.5, 0.75, ((0, 4), (2, 2)))
    output_cotangent = bell_draw(own_keys[4], (TOKEN_TOTAL, KEY_OUT_WIDTH), 0.02, 0.119628906, ((0, 8), (1, 2)))
    block_owner_index = draw_block_owner_index(jax.random.fold_in(jax.random.fold_in(keys[7], part), 71), part)
    send_site_table = place_ends(jax.random.randint(own_keys[6], (N_DP, N_PAIR, N_DP), 0, S_DEV), jax.random.fold_in(own_keys[6], 1), 0, S_DEV - 1).astype(jnp.int32)
    return {"hidden_input": hidden_input, "key_weight_frozen": key_weight_frozen, "adapter_down": adapter_down, "adapter_up": adapter_up, "output_cotangent": output_cotangent, "block_owner_index": block_owner_index, "send_site_table": send_site_table}


adapter_scale = 2.0


def reference(hidden_input, key_weight_frozen, adapter_down, adapter_up, output_cotangent, block_owner_index, send_site_table):
    block_index = jnp.arange(BLOCKS, dtype=jnp.int32)
    device_of = block_index // BLK_DEV
    dp_index = device_of // N_PAIR
    pair_index = device_of % N_PAIR
    block_site = block_owner_index * S_DEV + send_site_table[block_owner_index, pair_index, dp_index]
    frozen_output = jnp.dot(hidden_input, key_weight_frozen, preferred_element_type=jnp.float32)
    group_width = KEY_OUT_WIDTH // N_MP
    backward_total = jnp.zeros((TOKEN_TOTAL, MODEL_WIDTH), jnp.float32)
    for group in range(N_MP):
        grad_part = output_cotangent[:, group * group_width:(group + 1) * group_width]
        weight_part = key_weight_frozen[:, group * group_width:(group + 1) * group_width]
        partial_back = lax.dot_general(grad_part, weight_part, (((1,), (1,)), ((), ())), preferred_element_type=jnp.float32)
        backward_total = backward_total + partial_back.astype(jnp.bfloat16).astype(jnp.float32)
    device_count = N_DP * N_PAIR
    device_input = hidden_input.reshape(device_count, BLK_DEV, BLOCK, MODEL_WIDTH)
    device_gradient = output_cotangent.reshape(device_count, BLK_DEV, BLOCK, KEY_OUT_WIDTH)
    device_sites = block_site.reshape(device_count, BLK_DEV)
    top_precision = lax.Precision.HIGHEST

    def single_device_body(carry, inputs):
        down_accumulator, up_accumulator = carry
        x_blk, grad_blk, resident_sites = inputs
        down_panel = adapter_down[resident_sites].astype(jnp.float32)
        up_panel = adapter_up[resident_sites].astype(jnp.float32)
        x_float = x_blk.astype(jnp.float32)
        grad_float = grad_blk.astype(jnp.float32)
        reduced_update = jnp.einsum('btd,bdr->btr', x_float, down_panel, precision=top_precision).astype(jnp.bfloat16).astype(jnp.float32)
        reduced_hidden = jnp.einsum('btc,brc->btr', grad_float, up_panel, precision=top_precision).astype(jnp.bfloat16).astype(jnp.float32)
        adapter_output = jnp.einsum('njh,nhq->njq', reduced_update, up_panel, precision=top_precision)
        adapter_backward = jnp.einsum('osp,omp->osm', reduced_hidden, down_panel, precision=top_precision)
        part_a = jnp.einsum('btd,btr->bdr', x_float, reduced_hidden, precision=top_precision)
        part_b = jnp.einsum('btr,btc->brc', reduced_update, grad_float, precision=top_precision)
        down_accumulator = down_accumulator.at[resident_sites].add(part_a)
        up_accumulator = up_accumulator.at[resident_sites].add(part_b)
        return (down_accumulator, up_accumulator), (adapter_output, adapter_backward)

    down_start = jnp.zeros((SITE_TOTAL, MODEL_WIDTH, ADAPTER_RANK), jnp.float32)
    up_start = jnp.zeros((SITE_TOTAL, ADAPTER_RANK, KEY_OUT_WIDTH), jnp.float32)
    (down_sum, up_sum), (adapter_output, adapter_backward) = lax.scan(single_device_body, (down_start, up_start), (device_input, device_gradient, device_sites))
    key_projection_output = (frozen_output + adapter_scale * adapter_output.reshape(TOKEN_TOTAL, KEY_OUT_WIDTH)).astype(jnp.bfloat16)
    input_gradient = (backward_total + adapter_scale * adapter_backward.reshape(TOKEN_TOTAL, MODEL_WIDTH)).astype(jnp.bfloat16)
    return key_projection_output, input_gradient, adapter_scale * down_sum, adapter_scale * up_sum
```

```python
import jax
import jax.numpy as jnp
from jax import lax
from jax.sharding import PartitionSpec as P

SCALE = 2.0
F32 = jnp.float32
BF16 = jnp.bfloat16


def shift(value, axis, by):
    size = lax.axis_size(axis)
    return lax.ppermute(value, axis, [(i, (i + by) % size) for i in range(size)])


def after(value, *others):
    return lax.optimization_barrier((value, *others))[0]


def nn(a, b):
    return lax.dot_general(a, b, (((1,), (0,)), ((), ())), preferred_element_type=F32)


def nt(a, b):
    return lax.dot_general(a, b, (((1,), (1,)), ((), ())), preferred_element_type=F32)


def tn(a, b):
    return lax.dot_general(a, b, (((0,), (0,)), ((), ())), preferred_element_type=F32)


def shards(x, w, down, up, gy, owner, table):
    tok, feat = x.shape
    cols = w.shape[1]
    rank = up.shape[1]
    sites = up.shape[0]
    n_dp, n_mp, n_pair = (lax.axis_size(a) for a in ("dp", "mp", "pair"))
    me_dp, me_mp, me_pair = (lax.axis_index(a) for a in ("dp", "mp", "pair"))

    part = feat // n_pair
    w_own = lax.dynamic_slice(w, (me_mp * feat, 0), (feat, cols))
    w_sent = []
    for s in range(1, n_mp):
        row = ((me_mp + s) % n_mp) * feat + me_pair * part
        w_sent.append(shift(lax.dynamic_slice(w, (row, 0), (part, cols)), "mp", s))

    wanted = lax.dynamic_index_in_dim(table[0], me_pair, 0, keepdims=False)
    maps = jnp.concatenate([down.transpose(0, 2, 1), up], axis=2)
    slots = []
    for s in range(n_dp):
        chosen = lax.dynamic_index_in_dim(maps, wanted[(me_dp + s) % n_dp], 0, keepdims=False)
        slots.append(shift(chosen, "dp", s) if s else chosen)

    w_rows = [w_own]
    for piece in w_sent:
        pieces = jnp.zeros((n_pair, part, cols), BF16)
        for q in range(n_pair):
            got = shift(piece, "pair", q) if q else piece
            pieces = lax.dynamic_update_slice(pieces, got[None], ((me_pair - q) % n_pair, 0, 0))
        w_rows.append(pieces.reshape(feat, cols))

    gy_all = [gy] + [shift(after(gy, *w_sent), "mp", s) for s in range(1, n_mp)]

    y_own = nn(x, w_own)
    y_got = [shift(nn(x, w_rows[s]).astype(BF16), "mp", n_mp - s) for s in range(1, n_mp)]

    adapters = jnp.concatenate(slots, axis=0)
    a_down, a_up = adapters[:, :feat], adapters[:, feat:]
    source = (me_dp - jnp.arange(n_dp, dtype=jnp.int32)) % n_dp
    hit = (owner[:, None] == source[None, :]).astype(BF16)
    hit = jnp.broadcast_to(
        hit[:, None, :, None], (owner.shape[0], tok // owner.shape[0], n_dp, rank)
    ).reshape(tok, n_dp * rank)
    u_part = (nt(x, a_down) * hit).astype(BF16)
    h_part = (nt(gy, a_up) * hit).astype(BF16)
    fold = lambda v: v.reshape(tok, n_dp, rank).sum(1).astype(BF16)
    uh_part = jnp.concatenate([fold(u_part), fold(h_part)], axis=1)
    uh = uh_part.astype(F32)
    for s in range(1, n_mp):
        uh = uh + shift(uh_part, "mp", s).astype(F32)
    uh = uh.astype(BF16)
    u_wide = jnp.tile(uh[:, :rank], (1, n_dp)) * hit
    h_wide = jnp.tile(uh[:, rank:], (1, n_dp)) * hit

    grads = jnp.concatenate([tn(h_wide, x), tn(u_wide, gy)], axis=1).astype(BF16)
    total = jnp.zeros((sites, rank, feat + cols), F32)
    mine = jnp.arange(sites, dtype=jnp.int32)
    for s in range(n_dp):
        sent = grads[s * rank:(s + 1) * rank]
        got = shift(sent, "dp", n_dp - s) if s else sent
        use = (mine == wanted[(me_dp + s) % n_dp]).astype(F32)
        total = total + use[:, None, None] * got.astype(F32)[None]
    total_part = total.astype(BF16)
    total = total_part.astype(F32)
    for q in range(1, n_pair):
        total = total + shift(total_part, "pair", q).astype(F32)
    total = SCALE * total
    down_grad = total[:, :, :feat].transpose(0, 2, 1)
    up_grad = total[:, :, feat:]

    back = SCALE * nn(h_wide, a_down)
    for g, rows in zip(gy_all, w_rows):
        back = back + nt(g, rows)
    y = y_own + SCALE * nn(u_wide, a_up)
    for got in y_got:
        y = y + got.astype(F32)
    return y.astype(BF16), back.astype(BF16), down_grad, up_grad


def solution(mesh):
    rows = P(("groups", "dp", "pair"), "mp")
    in_specs = (
        rows,
        P(None, "mp"),
        P(("groups", "dp"), "mp", None),
        P(("groups", "dp"), None, "mp"),
        rows,
        P(("groups", "dp", "pair")),
        P(("groups", "dp"), None, None),
    )
    out_specs = (rows, rows, P(("groups", "dp"), "mp", None), P(("groups", "dp"), None, "mp"))
    return jax.shard_map(shards, mesh=mesh, in_specs=in_specs, out_specs=out_specs, check_vma=False)
```

```python
import functools

import jax
import jax.numpy as jnp
from jax import lax
from jax.experimental import pallas as pl
from jax.experimental.pallas import tpu as pltpu
from jax.sharding import PartitionSpec as P

SCALE = 2.0
F32 = jnp.float32
BF16 = jnp.bfloat16
SMEM = pl.BlockSpec(memory_space=pltpu.SMEM)
VMEM = pl.BlockSpec(memory_space=pltpu.VMEM)
HBM = pl.BlockSpec(memory_space=pl.ANY)


def params():
    return pltpu.CompilerParams(vmem_limit_bytes=48 * 1024 * 1024)


def cost():
    return pl.CostEstimate(flops=1, bytes_accessed=1, transcendentals=0)


def shape(*dims, dtype=BF16):
    return jax.ShapeDtypeStruct(dims, dtype)


def shift(value, axis, by):
    size = lax.axis_size(axis)
    return lax.ppermute(value, axis, [(i, (i + by) % size) for i in range(size)])


def after(value, *others):
    return lax.optimization_barrier((value, *others))[0]


def nn(a, b):
    return lax.dot_general(a, b, (((1,), (0,)), ((), ())), preferred_element_type=F32)


def nt(a, b):
    return lax.dot_general(a, b, (((1,), (1,)), ((), ())), preferred_element_type=F32)


def tn(a, b):
    return lax.dot_general(a, b, (((0,), (0,)), ((), ())), preferred_element_type=F32)


def wanted_site(table, n_dp, s):
    return table[0, lax.axis_index("pair"), lax.rem(lax.axis_index("dp") + s, n_dp)]


def pack_kernel(n_dp, n_mp, n_pair, table, down, up, w, *refs):
    ups, downs, pieces, sem = refs[:n_dp], refs[n_dp:2 * n_dp], refs[2 * n_dp:-1], refs[-1]
    feat = w.shape[0] // n_mp
    part = feat // n_pair
    copies = []
    for s in range(1, n_mp):
        row = lax.rem(lax.axis_index("mp") + s, n_mp) * feat + lax.axis_index("pair") * part
        row = pl.multiple_of(row, part)
        copies.append(pltpu.make_async_copy(w.at[pl.ds(row, part)], pieces[s - 1], sem.at[s - 1]))
    for s in range(n_dp):
        site = wanted_site(table, n_dp, s)
        copies.append(pltpu.make_async_copy(up.at[site], ups[s], sem.at[n_mp - 1 + s]))
        copies.append(pltpu.make_async_copy(down.at[site], downs[s], sem.at[n_mp - 1 + n_dp + s]))
    for copy in copies:
        copy.start()
    for copy in copies:
        copy.wait()


def slot_of(owner, b, n_dp):
    return lax.rem(lax.axis_index("dp") - owner[b] + n_dp, n_dp)


def reduce_kernel(n_dp, owner, act, *refs):
    maps, out, wide = refs[:n_dp], refs[n_dp], refs[n_dp + 1]
    rank = maps[0].shape[0]
    blocks = owner.shape[0]
    rows = act.shape[0] // blocks
    for s in range(n_dp):
        wide[s * rank:(s + 1) * rank, :] = maps[s][...]
    full = nt(act[...], wide[...])
    lane_slot = lax.broadcasted_iota(jnp.int32, (rows, n_dp * rank), 1) // rank
    folded = []
    for b in range(blocks):
        kept = jnp.where(lane_slot == slot_of(owner, b, n_dp), full[b * rows:(b + 1) * rows], 0.0)
        total = kept[:, :rank]
        for s in range(1, n_dp):
            total = total + kept[:, s * rank:(s + 1) * rank]
        folded.append(total)
    for j in range(blocks // 2):
        pair = jnp.concatenate([folded[2 * j], folded[2 * j + 1]], axis=1)
        out[j * rows:(j + 1) * rows, :] = pair.astype(BF16)


def grad_kernel(n_dp, n_part, owner, act, *refs):
    parts, grads, wide = refs[:n_part], refs[n_part:n_part + n_dp], refs[n_part + n_dp]
    rank = wide.shape[1] // n_dp
    blocks = owner.shape[0]
    rows = act.shape[0] // blocks
    total = parts[0][...].astype(F32)
    for part in parts[1:]:
        total = total + part[...].astype(F32)
    lane_slot = lax.broadcasted_iota(jnp.int32, (rows, n_dp * rank), 1) // rank
    for b in range(blocks):
        one = total[(b // 2) * rows:(b // 2 + 1) * rows, (b % 2) * rank:(b % 2 + 1) * rank]
        spread = jnp.concatenate([one] * n_dp, axis=1)
        kept = jnp.where(lane_slot == slot_of(owner, b, n_dp), spread, 0.0)
        wide[b * rows:(b + 1) * rows, :] = kept.astype(BF16)
    full = tn(wide[...], act[...])
    for s in range(n_dp):
        grads[s][...] = full[s * rank:(s + 1) * rank].astype(BF16)


def send_kernel(n_pair, feat, n_mp, x, *refs):
    n_other = n_mp - 1
    pieces, outs, rows = refs[:n_other * n_pair], refs[n_other * n_pair:n_other * n_pair + n_other], refs[-n_other:]
    part = feat // n_pair

    @pl.when(pl.program_id(0) == 0)
    def _():
        for s in range(n_other):
            for q in range(n_pair):
                at = lax.rem(lax.axis_index("pair") + n_pair - q, n_pair) * part
                rows[s][pl.ds(pl.multiple_of(at, part), part), :] = pieces[s * n_pair + q][...]

    for s in range(n_other):
        outs[s][...] = nn(x[...], rows[s][...]).astype(BF16)


def back_kernel(n_dp, n_mp, *refs):
    w, gys, rows, wide, downs, out, own, maps = (
        refs[0], refs[1:1 + n_mp], refs[1 + n_mp:2 * n_mp], refs[2 * n_mp],
        refs[2 * n_mp + 1:-3], refs[-3], refs[-2], refs[-1],
    )
    rank, feat = downs[0].shape

    @pl.when(pl.program_id(0) == 0)
    def _():
        own[...] = w[pl.ds(pl.multiple_of(lax.axis_index("mp") * feat, feat), feat), :]
        for s in range(n_dp):
            maps[s * rank:(s + 1) * rank, :] = downs[s][...]

    total = nt(gys[0][...], own[...]) + SCALE * nn(wide[...], maps[...])
    for gy, row in zip(gys[1:], rows):
        total = total + nt(gy[...], row[...])
    out[...] = total.astype(BF16)


def own_kernel(n_dp, w, x, wide, *refs):
    ups, out, maps = refs[:n_dp], refs[n_dp], refs[n_dp + 1]
    rank = ups[0].shape[0]
    feat = x.shape[1]

    @pl.when(pl.program_id(0) == 0)
    def _():
        for s in range(n_dp):
            maps[s * rank:(s + 1) * rank, :] = ups[s][...]

    own = w[pl.ds(pl.multiple_of(lax.axis_index("mp") * feat, feat), feat), :]
    out[...] = nn(x[...], own) + SCALE * nn(wide[...], maps[...])


def add_kernel(*refs):
    total = refs[0][...]
    for ref in refs[1:-1]:
        total = total + ref[...].astype(F32)
    refs[-1][...] = total.astype(BF16)


def site_kernel(n_dp, feat, table, *refs):
    downs, ups, out = refs[:n_dp], refs[n_dp:2 * n_dp], refs[-1]
    for site in range(out.shape[0]):
        for grads, lo, hi in ((downs, 0, feat), (ups, feat, out.shape[2])):
            total = jnp.zeros((out.shape[1], hi - lo), F32)
            for s in range(n_dp):
                use = wanted_site(table, n_dp, s) == site
                total = total + jnp.where(use, grads[s][...].astype(F32), 0.0)
            out[site, :, lo:hi] = total.astype(BF16)


def last_kernel(feat, *refs):
    parts, down, up = refs[:-2], refs[-2], refs[-1]
    total = parts[0][...].astype(F32)
    for part in parts[1:]:
        total = total + part[...].astype(F32)
    total = SCALE * total
    down[...] = total[:, :, :feat]
    up[...] = total[:, :, feat:]


def shards(x, w, down, up, gy, owner, table):
    tok, feat = x.shape
    cols = w.shape[1]
    sites, rank = up.shape[:2]
    n_dp, n_mp, n_pair = (lax.axis_size(a) for a in ("dp", "mp", "pair"))
    down = down.transpose(0, 2, 1)
    part = feat // n_pair
    tile = tok // 3
    row_block = lambda width: pl.BlockSpec((tile, width), lambda i: (i, 0))
    whole = lambda *dims: pl.BlockSpec(dims, lambda i: (0,) * len(dims))

    gys = [gy] + [shift(gy, "mp", s) for s in range(1, n_mp)]

    packed = pl.pallas_call(
        functools.partial(pack_kernel, n_dp, n_mp, n_pair),
        out_shape=[shape(rank, cols)] * n_dp + [shape(rank, feat)] * n_dp + [shape(part, cols)] * (n_mp - 1),
        in_specs=[SMEM, HBM, HBM, HBM],
        out_specs=[HBM] * (2 * n_dp + n_mp - 1),
        scratch_shapes=[pltpu.SemaphoreType.DMA((n_mp - 1 + 2 * n_dp,))],
        compiler_params=params(), cost_estimate=cost(), name="pack",
    )(table, down, up, w)
    pieces = [shift(packed[2 * n_dp + s - 1], "mp", s) for s in range(1, n_mp)]
    ups = [packed[0]] + [shift(packed[s], "dp", s) for s in range(1, n_dp)]
    downs = [packed[n_dp]] + [shift(packed[n_dp + s], "dp", s) for s in range(1, n_dp)]

    def low_rank(act, maps, name):
        mine = pl.pallas_call(
            functools.partial(reduce_kernel, n_dp),
            out_shape=shape(tok // 2, 2 * rank),
            in_specs=[SMEM] + [VMEM] * (1 + n_dp), out_specs=VMEM,
            scratch_shapes=[pltpu.VMEM((n_dp * rank, act.shape[1]), BF16)],
            compiler_params=params(), cost_estimate=cost(), name=name + "_part",
        )(owner, act, *maps)
        return [mine] + [shift(mine, "mp", s) for s in range(1, n_mp)]

    def gradient(act, parts, name):
        *grads, wide = pl.pallas_call(
            functools.partial(grad_kernel, n_dp, n_mp),
            out_shape=[shape(rank, act.shape[1])] * n_dp + [shape(tok, n_dp * rank)],
            in_specs=[SMEM] + [VMEM] * (1 + n_mp), out_specs=[VMEM] * (n_dp + 1),
            compiler_params=params(), cost_estimate=cost(), name=name + "_grad",
        )(owner, act, *parts)
        return [grads[0]] + [shift(grads[s], "dp", n_dp - s) for s in range(1, n_dp)], wide

    h_parts = low_rank(gy, ups, "h")
    down_back, h_wide = gradient(x, h_parts, "down")
    u_parts = low_rank(x, downs, "u")
    up_back, u_wide = gradient(gy, u_parts, "up")

    parts = []
    for piece in pieces:
        parts += [piece] + [shift(piece, "pair", q) for q in range(1, n_pair)]
    sent = pl.pallas_call(
        functools.partial(send_kernel, n_pair, feat, n_mp),
        grid=(3,),
        out_shape=[shape(tok, cols)] * (n_mp - 1) + [shape(feat, cols)] * (n_mp - 1),
        in_specs=[row_block(feat)] + [whole(part, cols)] * len(parts),
        out_specs=[row_block(cols)] * (n_mp - 1) + [whole(feat, cols)] * (n_mp - 1),
        compiler_params=params(), cost_estimate=cost(), name="y_send",
    )(x, *parts)
    w_rows = sent[n_mp - 1:]
    y_got = [shift(sent[s - 1], "mp", n_mp - s) for s in range(1, n_mp)]

    y_own = pl.pallas_call(
        functools.partial(own_kernel, n_dp),
        grid=(3,),
        out_shape=shape(tok, cols, dtype=F32),
        in_specs=[whole(*w.shape), row_block(feat), row_block(n_dp * rank)] + [whole(rank, cols)] * n_dp,
        out_specs=row_block(cols),
        scratch_shapes=[pltpu.VMEM((n_dp * rank, cols), BF16)],
        compiler_params=params(), cost_estimate=cost(), name="y_own",
    )(w, x, u_wide, *ups)

    back = pl.pallas_call(
        functools.partial(back_kernel, n_dp, n_mp),
        grid=(3,),
        out_shape=shape(tok, feat),
        in_specs=[whole(*w.shape)] + [row_block(cols)] * n_mp + [whole(feat, cols)] * (n_mp - 1)
        + [row_block(n_dp * rank)] + [whole(rank, feat)] * n_dp,
        out_specs=row_block(feat),
        scratch_shapes=[pltpu.VMEM((feat, cols), BF16), pltpu.VMEM((n_dp * rank, feat), BF16)],
        compiler_params=params(), cost_estimate=cost(), name="back",
    )(w, *gys, *w_rows, h_wide, *downs)

    summed = pl.pallas_call(
        functools.partial(site_kernel, n_dp, feat),
        out_shape=shape(sites, rank, feat + cols),
        in_specs=[SMEM] + [VMEM] * (2 * n_dp), out_specs=VMEM,
        compiler_params=params(), cost_estimate=cost(), name="sites",
    )(table, *down_back, *up_back)
    both = [summed] + [shift(summed, "pair", q) for q in range(1, n_pair)]
    down_grad, up_grad = pl.pallas_call(
        functools.partial(last_kernel, feat),
        out_shape=[shape(sites, rank, feat, dtype=F32), shape(sites, rank, cols, dtype=F32)],
        in_specs=[VMEM] * n_pair, out_specs=[VMEM] * 2,
        compiler_params=params(), cost_estimate=cost(), name="gradients",
    )(*both)

    y = pl.pallas_call(
        add_kernel,
        grid=(3,),
        out_shape=shape(tok, cols),
        in_specs=[row_block(cols)] * n_mp, out_specs=row_block(cols),
        compiler_params=params(), cost_estimate=cost(), name="y_add",
    )(y_own, *y_got)
    return y, back, down_grad.transpose(0, 2, 1), up_grad


def solution(mesh):
    rows = P(("groups", "dp", "pair"), "mp")
    in_specs = (
        rows,
        P(None, "mp"),
        P(("groups", "dp"), "mp", None),
        P(("groups", "dp"), None, "mp"),
        rows,
        P(("groups", "dp", "pair")),
        P(("groups", "dp"), None, None),
    )
    out_specs = (rows, rows, P(("groups", "dp"), "mp", None), P(("groups", "dp"), None, "mp"))
    return jax.shard_map(shards, mesh=mesh, in_specs=in_specs, out_specs=out_specs, check_vma=False)
```

```python
import functools

import jax
import jax.numpy as jnp
from jax import lax
from jax.experimental import pallas as pl
from jax.experimental.pallas import tpu as pltpu
from jax.sharding import PartitionSpec as P

SCALE = 2.0
TILES = 3
UHCOST = 1
F32 = jnp.float32
BF16 = jnp.bfloat16
SMEM = pl.BlockSpec(memory_space=pltpu.SMEM)
VMEM = pl.BlockSpec(memory_space=pltpu.VMEM)
ANY = pl.BlockSpec(memory_space=pl.ANY)


def shape(*dims, dtype=BF16):
    return jax.ShapeDtypeStruct(dims, dtype)


def call(kernel, name, out_shape, in_specs, out_specs, scratch=(), grid=(), flops=1):
    return pl.pallas_call(
        kernel, name=name, out_shape=out_shape, grid=grid, in_specs=in_specs, out_specs=out_specs,
        scratch_shapes=scratch,
        compiler_params=pltpu.CompilerParams(vmem_limit_bytes=64 * 1024 * 1024),
        cost_estimate=pl.CostEstimate(flops=flops, bytes_accessed=1, transcendentals=0),
    )


def shift(value, axis, by):
    size = lax.axis_size(axis)
    return lax.ppermute(value, axis, [(i, (i + by) % size) for i in range(size)])


def after(value, *others):
    return lax.optimization_barrier((value, *others))[0]


def nn(a, b):
    return lax.dot_general(a, b, (((1,), (0,)), ((), ())), preferred_element_type=F32)


def nt(a, b):
    return lax.dot_general(a, b, (((1,), (1,)), ((), ())), preferred_element_type=F32)


def tn(a, b):
    return lax.dot_general(a, b, (((0,), (0,)), ((), ())), preferred_element_type=F32)


def run(copies):
    for copy in copies:
        copy.start()
    for copy in copies:
        copy.wait()


def wanted_site(table, n_dp, s):
    return table[0, lax.axis_index("pair"), lax.rem(lax.axis_index("dp") + s, n_dp)]


def slot_of(owner, b, n_dp):
    return lax.rem(lax.axis_index("dp") - owner[b] + n_dp, n_dp)


def first_kernel(n_mp, n_share, w, *refs):
    pieces, sem = refs[:-1], refs[-1]
    feat = w.shape[0] // n_mp
    part = feat // n_share
    place = lax.axis_index("groups") * lax.axis_size("pair") + lax.axis_index("pair")
    copies = []
    for s in range(1, n_mp):
        row = pl.multiple_of(lax.rem(lax.axis_index("mp") + s, n_mp) * feat + place * part, part)
        copies.append(pltpu.make_async_copy(w.at[pl.ds(row, part)], pieces[s - 1], sem.at[s - 1]))
    run(copies)


def pack_kernel(n_dp, table, down, up, _, *refs):
    maps, sem = refs[:n_dp], refs[-1]
    feat, cols = down.shape[2], up.shape[2]
    copies = []
    for s in range(n_dp):
        site = wanted_site(table, n_dp, s)
        copies.append(pltpu.make_async_copy(down.at[site], maps[s].at[:, pl.ds(0, feat)], sem.at[s]))
        copies.append(pltpu.make_async_copy(up.at[site], maps[s].at[:, pl.ds(feat, cols)], sem.at[n_dp + s]))
    run(copies)


def reduce_kernel(n_dp, owner, x, gy, *refs):
    maps, out, wide = refs[:n_dp], refs[n_dp], refs[n_dp + 1]
    rank = maps[0].shape[0]
    feat = x.shape[1]
    blocks = owner.shape[0]
    rows = x.shape[0] // blocks
    for s in range(n_dp):
        wide[s * rank:(s + 1) * rank, :] = maps[s][...]
    lane_slot = lax.broadcasted_iota(jnp.int32, (rows, n_dp * rank), 1) // rank
    full = nt(x[...], wide[:, :feat]), nt(gy[...], wide[:, feat:])
    for b in range(blocks):
        mine = lane_slot == slot_of(owner, b, n_dp)
        halves = []
        for one in full:
            kept = jnp.where(mine, one[b * rows:(b + 1) * rows], 0.0)
            total = kept[:, :rank]
            for s in range(1, n_dp):
                total = total + kept[:, s * rank:(s + 1) * rank]
            halves.append(total)
        out[b * rows:(b + 1) * rows, :] = jnp.concatenate(halves, axis=1).astype(BF16)


def send_kernel(n_groups, n_pair, feat, n_mp, _, x, *refs):
    n_other, n_share = n_mp - 1, n_groups * n_pair
    pieces, outs, rows = refs[:n_other * n_share], refs[-2 * n_other:-n_other], refs[-n_other:]
    part = feat // n_share

    @pl.when(pl.program_id(0) == 0)
    def _():
        for s in range(n_other):
            for k in range(n_share):
                group = lax.rem(lax.axis_index("groups") + n_groups - k // n_pair, n_groups)
                core = lax.rem(lax.axis_index("pair") + n_pair - k % n_pair, n_pair)
                at = pl.multiple_of((group * n_pair + core) * part, part)
                rows[s][pl.ds(at, part), :] = pieces[s * n_share + k][...]

    for s in range(n_other):
        outs[s][...] = nn(x[...], rows[s][...]).astype(BF16)


def grad_kernel(n_dp, n_mp, owner, _, x, gy, *refs):
    parts, grads, u_wide, h_wide = refs[:n_mp], refs[n_mp:n_mp + n_dp], refs[-2], refs[-1]
    rank = u_wide.shape[1] // n_dp
    feat = x.shape[1]
    blocks = owner.shape[0]
    rows = x.shape[0] // blocks
    total = parts[0][...].astype(F32)
    for part in parts[1:]:
        total = total + part[...].astype(F32)
    lane_slot = lax.broadcasted_iota(jnp.int32, (rows, n_dp * rank), 1) // rank
    for b in range(blocks):
        mine = lane_slot == slot_of(owner, b, n_dp)
        for k, wide in enumerate((u_wide, h_wide)):
            one = total[b * rows:(b + 1) * rows, k * rank:(k + 1) * rank]
            spread = jnp.concatenate([one] * n_dp, axis=1)
            wide[b * rows:(b + 1) * rows, :] = jnp.where(mine, spread, 0.0).astype(BF16)
    for wide, act, lo in ((h_wide, x, 0), (u_wide, gy, feat)):
        full = tn(wide[...], act[...])
        for s in range(n_dp):
            grads[s][:, lo:lo + full.shape[1]] = full[s * rank:(s + 1) * rank].astype(BF16)


def back_kernel(n_dp, n_mp, w, gy, wide, *refs):
    n_other = n_mp - 1
    gots, rows = refs[:n_other], refs[n_other:2 * n_other]
    maps, out, own, downs = refs[2 * n_other:-3], refs[-3], refs[-2], refs[-1]
    rank = maps[0].shape[0]
    feat = out.shape[1]

    @pl.when(pl.program_id(0) == 0)
    def _():
        own[...] = w[pl.ds(pl.multiple_of(lax.axis_index("mp") * feat, feat), feat), :]
        for s in range(n_dp):
            downs[s * rank:(s + 1) * rank, :] = maps[s][:, :feat]

    total = nt(gy[...], own[...]) + SCALE * nn(wide[...], downs[...])
    for got, row in zip(gots, rows):
        total = total + nt(got[...], row[...])
    out[...] = total.astype(BF16)


def own_kernel(n_dp, w, x, wide, *refs):
    maps, out, ups = refs[:n_dp], refs[n_dp], refs[n_dp + 1]
    rank = maps[0].shape[0]
    feat = x.shape[1]

    @pl.when(pl.program_id(0) == 0)
    def _():
        for s in range(n_dp):
            ups[s * rank:(s + 1) * rank, :] = maps[s][:, feat:]

    own = w[pl.ds(pl.multiple_of(lax.axis_index("mp") * feat, feat), feat), :]
    out[...] = nn(x[...], own) + SCALE * nn(wide[...], ups[...])


def add_kernel(*refs):
    total = refs[0][...]
    for ref in refs[1:-1]:
        total = total + ref[...].astype(F32)
    refs[-1][...] = total.astype(BF16)


def site_kernel(n_dp, table, _, *refs):
    grads, out = refs[:n_dp], refs[-1]
    for site in range(out.shape[0]):
        total = jnp.zeros(out.shape[1:], F32)
        for s in range(n_dp):
            use = wanted_site(table, n_dp, s) == site
            total = total + jnp.where(use, grads[s][...].astype(F32), 0.0)
        out[site] = total.astype(BF16)


def last_kernel(feat, *refs):
    parts, down, up = refs[:-2], refs[-2], refs[-1]
    total = parts[0][...].astype(F32)
    for part in parts[1:]:
        total = total + part[...].astype(F32)
    total = SCALE * total
    down[...] = total[:, :, :feat]
    up[...] = total[:, :, feat:]


def shards(x, w, down, up, gy, owner, table):
    tok, feat = x.shape
    cols = w.shape[1]
    sites, rank = up.shape[:2]
    n_groups, n_dp, n_mp, n_pair = (lax.axis_size(a) for a in ("groups", "dp", "mp", "pair"))
    n_other, n_share = n_mp - 1, n_groups * n_pair
    down = down.transpose(0, 2, 1)
    part = feat // n_share
    both = feat + cols
    tile = tok // TILES
    row_block = lambda width: pl.BlockSpec((tile, width), lambda i: (i, 0))
    whole = lambda *dims: pl.BlockSpec(dims, lambda i: (0,) * len(dims))

    pieces = call(
        functools.partial(first_kernel, n_mp, n_share), "first",
        [shape(part, cols)] * n_other, [ANY], [ANY] * n_other, [pltpu.SemaphoreType.DMA((n_other,))],
    )(w)
    maps = call(
        functools.partial(pack_kernel, n_dp), "pack",
        [shape(rank, both)] * n_dp, [SMEM, ANY, ANY, ANY], [ANY] * n_dp,
        [pltpu.SemaphoreType.DMA((2 * n_dp,))],
    )(table, down, up, pieces[0])
    maps = [maps[0]] + [shift(maps[s], "dp", s) for s in range(1, n_dp)]
    pieces = [shift(pieces[s - 1], "mp", s) for s in range(1, n_mp)]
    gy_got = [shift(after(gy, maps[0], *pieces), "mp", s) for s in range(1, n_mp)]
    pieces = [after(piece, maps[0]) for piece in pieces]
    parts = []
    for piece in pieces:
        for j in range(n_groups):
            one = shift(piece, "groups", j) if j else piece
            parts += [shift(one, "pair", q) if q else one for q in range(n_pair)]

    uh = call(
        functools.partial(reduce_kernel, n_dp), "uh",
        shape(tok, 2 * rank), [SMEM] + [VMEM] * (2 + n_dp), VMEM,
        [pltpu.VMEM((n_dp * rank, both), BF16)], flops=UHCOST,
    )(owner, x, gy, *maps)
    uhs = [uh] + [shift(uh, "mp", s) for s in range(1, n_mp)]

    *grads, u_wide, h_wide = call(
        functools.partial(grad_kernel, n_dp, n_mp), "grads",
        [shape(rank, both)] * n_dp + [shape(tok, n_dp * rank)] * 2,
        [SMEM, ANY] + [VMEM] * (2 + n_mp), [VMEM] * (n_dp + 2),
    )(owner, gy_got[0], x, gy, *uhs)
    grads = [grads[0]] + [shift(grads[s], "dp", n_dp - s) for s in range(1, n_dp)]

    sent = call(
        functools.partial(send_kernel, n_groups, n_pair, feat, n_mp), "y_send",
        [shape(tok, cols)] * n_other + [shape(feat, cols)] * n_other,
        [ANY, row_block(feat)] + [whole(part, cols)] * len(parts),
        [row_block(cols)] * n_other + [whole(feat, cols)] * n_other,
        grid=(TILES,),
    )(u_wide, x, *parts)
    w_rows = sent[n_other:]
    y_got = [shift(sent[s - 1], "mp", n_mp - s) for s in range(1, n_mp)]

    y_own = call(
        functools.partial(own_kernel, n_dp), "y_own",
        shape(tok, cols, dtype=F32),
        [whole(*w.shape), row_block(feat), row_block(n_dp * rank)] + [whole(rank, both)] * n_dp,
        row_block(cols), [pltpu.VMEM((n_dp * rank, cols), BF16)], grid=(TILES,),
    )(w, x, u_wide, *maps)

    back = call(
        functools.partial(back_kernel, n_dp, n_mp), "back",
        shape(tok, feat),
        [whole(*w.shape), row_block(cols), row_block(n_dp * rank)] + [row_block(cols)] * n_other
        + [whole(feat, cols)] * n_other + [whole(rank, both)] * n_dp,
        row_block(feat), [pltpu.VMEM((feat, cols), BF16), pltpu.VMEM((n_dp * rank, feat), BF16)], grid=(TILES,),
    )(w, gy, h_wide, *gy_got, *w_rows, *maps)

    summed = call(
        functools.partial(site_kernel, n_dp), "sites",
        shape(sites, rank, both), [SMEM, ANY] + [VMEM] * n_dp, VMEM,
    )(table, back, *grads)
    halves = [summed] + [shift(summed, "pair", q) for q in range(1, n_pair)]
    down_grad, up_grad = call(
        functools.partial(last_kernel, feat), "gradients",
        [shape(sites, rank, feat, dtype=F32), shape(sites, rank, cols, dtype=F32)],
        [VMEM] * n_pair, [VMEM] * 2,
    )(*halves)

    y = call(
        add_kernel, "y_add", shape(tok, cols), [row_block(cols)] * n_mp, row_block(cols), grid=(TILES,),
    )(y_own, *y_got)
    return y, back, down_grad.transpose(0, 2, 1), up_grad


def solution(mesh):
    rows = P(("groups", "dp", "pair"), "mp")
    in_specs = (
        rows,
        P(None, "mp"),
        P(("groups", "dp"), "mp", None),
        P(("groups", "dp"), None, "mp"),
        rows,
        P(("groups", "dp", "pair")),
        P(("groups", "dp"), None, None),
    )
    out_specs = (rows, rows, P(("groups", "dp"), "mp", None), P(("groups", "dp"), None, "mp"))
    return jax.shard_map(shards, mesh=mesh, in_specs=in_specs, out_specs=out_specs, check_vma=False)
```

```python
import functools

import jax
import jax.numpy as jnp
from jax import lax
from jax.experimental import pallas as pl
from jax.experimental.pallas import tpu as pltpu
from jax.sharding import PartitionSpec as P

SCALE = 2.0
TILES = 3
GRAD_COST = 15_000_000_000
F32 = jnp.float32
BF16 = jnp.bfloat16
SMEM = pl.BlockSpec(memory_space=pltpu.SMEM)
VMEM = pl.BlockSpec(memory_space=pltpu.VMEM)
ANY = pl.BlockSpec(memory_space=pl.ANY)


def shape(*dims, dtype=BF16):
    return jax.ShapeDtypeStruct(dims, dtype)


def call(kernel, name, out_shape, in_specs, out_specs, scratch=(), grid=(), mib=32, flops=1):
    return pl.pallas_call(
        kernel, name=name, out_shape=out_shape, grid=grid, in_specs=in_specs, out_specs=out_specs,
        scratch_shapes=scratch,
        compiler_params=pltpu.CompilerParams(vmem_limit_bytes=mib * 1024 * 1024),
        cost_estimate=pl.CostEstimate(flops=flops, bytes_accessed=1, transcendentals=0),
    )


def shift(value, axis, by):
    size = lax.axis_size(axis)
    return lax.ppermute(value, axis, [(i, (i + by) % size) for i in range(size)])


def after(value, *others):
    return lax.optimization_barrier((value, *others))[0]


def nn(a, b):
    return lax.dot_general(a, b, (((1,), (0,)), ((), ())), preferred_element_type=F32)


def nt(a, b):
    return lax.dot_general(a, b, (((1,), (1,)), ((), ())), preferred_element_type=F32)


def tn(a, b):
    return lax.dot_general(a, b, (((0,), (0,)), ((), ())), preferred_element_type=F32)


def run(copies):
    for copy in copies:
        copy.start()
    for copy in copies:
        copy.wait()


def wanted_site(table, n_dp, s):
    return table[0, lax.axis_index("pair"), lax.rem(lax.axis_index("dp") + s, n_dp)]


def slot_of(owner, b, n_dp):
    return lax.rem(lax.axis_index("dp") - owner[b] + n_dp, n_dp)


def pack_kernel(n_dp, n_mp, n_pair, table, down, up, w, *refs):
    ups, downs, pieces, sem = refs[:n_dp], refs[n_dp:2 * n_dp], refs[2 * n_dp:-1], refs[-1]
    feat = w.shape[0] // n_mp
    part = feat // n_pair
    copies = []
    for s in range(n_dp):
        site = wanted_site(table, n_dp, s)
        copies.append(pltpu.make_async_copy(up.at[site], ups[s], sem.at[s]))
        copies.append(pltpu.make_async_copy(down.at[site], downs[s], sem.at[n_dp + s]))
    for s in range(1, n_mp):
        row = lax.rem(lax.axis_index("mp") + s, n_mp) * feat + lax.axis_index("pair") * part
        row = pl.multiple_of(row, part)
        copies.append(pltpu.make_async_copy(w.at[pl.ds(row, part)], pieces[s - 1], sem.at[2 * n_dp + s - 1]))
    run(copies)


def reduce_kernel(n_dp, owner, act, _, *refs):
    maps, out, wide = refs[:n_dp], refs[n_dp], refs[n_dp + 1]
    rank = maps[0].shape[0]
    blocks = owner.shape[0]
    rows = act.shape[0] // blocks
    for s in range(n_dp):
        wide[s * rank:(s + 1) * rank, :] = maps[s][...]
    full = nt(act[...], wide[...])
    lane_slot = lax.broadcasted_iota(jnp.int32, (rows, n_dp * rank), 1) // rank
    folded = []
    for b in range(blocks):
        kept = jnp.where(lane_slot == slot_of(owner, b, n_dp), full[b * rows:(b + 1) * rows], 0.0)
        total = kept[:, :rank]
        for s in range(1, n_dp):
            total = total + kept[:, s * rank:(s + 1) * rank]
        folded.append(total)
    for j in range(blocks // 2):
        pair = jnp.concatenate([folded[2 * j], folded[2 * j + 1]], axis=1)
        out[j * rows:(j + 1) * rows, :] = pair.astype(BF16)


def grad_kernel(n_dp, n_part, n_behind, owner, act, *refs):
    refs = refs[n_behind:]
    parts, grads, wide = refs[:n_part], refs[n_part:n_part + n_dp], refs[n_part + n_dp]
    rank = wide.shape[1] // n_dp
    blocks = owner.shape[0]
    rows = act.shape[0] // blocks
    total = parts[0][...].astype(F32)
    for part in parts[1:]:
        total = total + part[...].astype(F32)
    lane_slot = lax.broadcasted_iota(jnp.int32, (rows, n_dp * rank), 1) // rank
    for b in range(blocks):
        one = total[(b // 2) * rows:(b // 2 + 1) * rows, (b % 2) * rank:(b % 2 + 1) * rank]
        spread = jnp.concatenate([one] * n_dp, axis=1)
        kept = jnp.where(lane_slot == slot_of(owner, b, n_dp), spread, 0.0)
        wide[b * rows:(b + 1) * rows, :] = kept.astype(BF16)
    full = tn(wide[...], act[...])
    for s in range(n_dp):
        grads[s][...] = full[s * rank:(s + 1) * rank].astype(BF16)


def send_kernel(n_pair, feat, n_mp, _, __, x, *refs):
    n_other = n_mp - 1
    pieces, outs, rows = refs[:n_other * n_pair], refs[n_other * n_pair:n_other * n_pair + n_other], refs[-n_other:]
    part = feat // n_pair

    @pl.when(pl.program_id(0) == 0)
    def _():
        for s in range(n_other):
            for q in range(n_pair):
                at = lax.rem(lax.axis_index("pair") + n_pair - q, n_pair) * part
                rows[s][pl.ds(pl.multiple_of(at, part), part), :] = pieces[s * n_pair + q][...]

    for s in range(n_other):
        outs[s][...] = nn(x[...], rows[s][...]).astype(BF16)


def back_kernel(n_dp, n_mp, _, *refs):
    w, gys, rows, wide, downs, out, own, maps = (
        refs[0], refs[1:1 + n_mp], refs[1 + n_mp:2 * n_mp], refs[2 * n_mp],
        refs[2 * n_mp + 1:-3], refs[-3], refs[-2], refs[-1],
    )
    rank, feat = downs[0].shape

    @pl.when(pl.program_id(0) == 0)
    def _():
        own[...] = w[pl.ds(pl.multiple_of(lax.axis_index("mp") * feat, feat), feat), :]
        for s in range(n_dp):
            maps[s * rank:(s + 1) * rank, :] = downs[s][...]

    total = nt(gys[0][...], own[...]) + SCALE * nn(wide[...], maps[...])
    for gy, row in zip(gys[1:], rows):
        total = total + nt(gy[...], row[...])
    out[...] = total.astype(BF16)


def own_kernel(n_dp, w, x, wide, *refs):
    ups, out, maps = refs[:n_dp], refs[n_dp], refs[n_dp + 1]
    rank = ups[0].shape[0]
    feat = x.shape[1]

    @pl.when(pl.program_id(0) == 0)
    def _():
        for s in range(n_dp):
            maps[s * rank:(s + 1) * rank, :] = ups[s][...]

    own = w[pl.ds(pl.multiple_of(lax.axis_index("mp") * feat, feat), feat), :]
    out[...] = nn(x[...], own) + SCALE * nn(wide[...], maps[...])


def add_kernel(*refs):
    total = refs[0][...]
    for ref in refs[1:-1]:
        total = total + ref[...].astype(F32)
    refs[-1][...] = total.astype(BF16)


def site_kernel(n_dp, feat, table, *refs):
    downs, ups, out = refs[:n_dp], refs[n_dp:2 * n_dp], refs[-1]
    for site in range(out.shape[0]):
        for grads, lo, hi in ((downs, 0, feat), (ups, feat, out.shape[2])):
            total = jnp.zeros((out.shape[1], hi - lo), F32)
            for s in range(n_dp):
                use = wanted_site(table, n_dp, s) == site
                total = total + jnp.where(use, grads[s][...].astype(F32), 0.0)
            out[site, :, lo:hi] = total.astype(BF16)


def last_kernel(feat, *refs):
    parts, down, up = refs[:-2], refs[-2], refs[-1]
    total = parts[0][...].astype(F32)
    for part in parts[1:]:
        total = total + part[...].astype(F32)
    total = SCALE * total
    down[...] = total[:, :, :feat]
    up[...] = total[:, :, feat:]


def shards(x, w, down, up, gy, owner, table):
    tok, feat = x.shape
    cols = w.shape[1]
    sites, rank = up.shape[:2]
    n_dp, n_mp, n_pair = (lax.axis_size(a) for a in ("dp", "mp", "pair"))
    n_other = n_mp - 1
    down = down.transpose(0, 2, 1)
    part = feat // n_pair
    tile = tok // TILES
    row_block = lambda width: pl.BlockSpec((tile, width), lambda i: (i, 0))
    whole = lambda *dims: pl.BlockSpec(dims, lambda i: (0,) * len(dims))

    packed = call(
        functools.partial(pack_kernel, n_dp, n_mp, n_pair), "pack",
        [shape(rank, cols)] * n_dp + [shape(rank, feat)] * n_dp + [shape(part, cols)] * n_other,
        [SMEM, ANY, ANY, ANY], [VMEM] * (2 * n_dp + n_other),
        [pltpu.SemaphoreType.DMA((2 * n_dp + n_other,))], mib=64,
    )(table, down, up, w)
    pieces = [shift(packed[2 * n_dp + s - 1], "mp", s) for s in range(1, n_mp)]
    ups = [packed[0]] + [shift(packed[s], "dp", s) for s in range(1, n_dp)]
    downs = [packed[n_dp]] + [shift(packed[n_dp + s], "dp", s) for s in range(1, n_dp)]

    def low_rank(act, maps, behind, name):
        mine = call(
            functools.partial(reduce_kernel, n_dp), name + "_part",
            shape(tok // 2, 2 * rank), [SMEM, VMEM, ANY] + [VMEM] * n_dp, VMEM,
            [pltpu.VMEM((n_dp * rank, act.shape[1]), BF16)],
        )(owner, act, behind, *maps)
        return [mine] + [shift(mine, "mp", s) for s in range(1, n_mp)]

    def gradient(act, parts, behind, name, flops):
        *grads, wide = call(
            functools.partial(grad_kernel, n_dp, n_mp, len(behind)), name + "_grad",
            [shape(rank, act.shape[1])] * n_dp + [shape(tok, n_dp * rank)],
            [SMEM, VMEM] + [ANY] * len(behind) + [VMEM] * n_mp, [VMEM] * (n_dp + 1), flops=flops,
        )(owner, act, *behind, *parts)
        return [grads[0]] + [shift(grads[s], "dp", n_dp - s) for s in range(1, n_dp)], wide

    h_parts = low_rank(gy, ups, packed[0], "h")
    gy_got = [shift(after(gy, h_parts[0], *pieces), "mp", s) for s in range(1, n_mp)]
    down_back, h_wide = gradient(x, h_parts, downs[1:], "down", GRAD_COST)
    u_parts = low_rank(x, downs, h_wide, "u")

    parts = []
    for piece in pieces:
        parts += [piece] + [shift(after(piece, h_parts[0]), "pair", q) for q in range(1, n_pair)]
    sent = call(
        functools.partial(send_kernel, n_pair, feat, n_mp), "y_send",
        [shape(tok, cols)] * n_other + [shape(feat, cols)] * n_other,
        [ANY, ANY, row_block(feat)] + [whole(part, cols)] * len(parts),
        [row_block(cols)] * n_other + [whole(feat, cols)] * n_other,
        grid=(TILES,),
    )(u_parts[0], down_back[1], x, *parts)
    w_rows = sent[n_other:]
    y_got = [shift(sent[s - 1], "mp", n_mp - s) for s in range(1, n_mp)]
    up_back, u_wide = gradient(gy, u_parts, down_back[2:] + gy_got, "up", GRAD_COST)

    y_own = call(
        functools.partial(own_kernel, n_dp), "y_own",
        shape(tok, cols, dtype=F32),
        [whole(*w.shape), row_block(feat), row_block(n_dp * rank)] + [whole(rank, cols)] * n_dp,
        row_block(cols), [pltpu.VMEM((n_dp * rank, cols), BF16)], grid=(TILES,),
    )(w, x, u_wide, *ups)

    back = call(
        functools.partial(back_kernel, n_dp, n_mp), "back",
        shape(tok, feat),
        [ANY, whole(*w.shape)] + [row_block(cols)] * n_mp + [whole(feat, cols)] * n_other
        + [row_block(n_dp * rank)] + [whole(rank, feat)] * n_dp,
        row_block(feat), [pltpu.VMEM((feat, cols), BF16), pltpu.VMEM((n_dp * rank, feat), BF16)], grid=(TILES,),
    )(u_wide, w, gy, *gy_got, *w_rows, h_wide, *downs)

    summed = call(
        functools.partial(site_kernel, n_dp, feat), "sites",
        shape(sites, rank, feat + cols), [SMEM] + [VMEM] * (2 * n_dp), VMEM,
    )(table, *down_back, *up_back)
    both = [summed] + [shift(summed, "pair", q) for q in range(1, n_pair)]
    down_grad, up_grad = call(
        functools.partial(last_kernel, feat), "gradients",
        [shape(sites, rank, feat, dtype=F32), shape(sites, rank, cols, dtype=F32)],
        [VMEM] * n_pair, [VMEM] * 2,
    )(*both)

    y = call(
        add_kernel, "y_add", shape(tok, cols), [row_block(cols)] * n_mp, row_block(cols), grid=(TILES,),
    )(y_own, *y_got)
    return y, back, down_grad.transpose(0, 2, 1), up_grad


def solution(mesh):
    rows = P(("groups", "dp", "pair"), "mp")
    in_specs = (
        rows,
        P(None, "mp"),
        P(("groups", "dp"), "mp", None),
        P(("groups", "dp"), None, "mp"),
        rows,
        P(("groups", "dp", "pair")),
        P(("groups", "dp"), None, None),
    )
    out_specs = (rows, rows, P(("groups", "dp"), "mp", None), P(("groups", "dp"), None, "mp"))
    return jax.shard_map(shards, mesh=mesh, in_specs=in_specs, out_specs=out_specs, check_vma=False)
```

```python
import functools

import jax
import jax.numpy as jnp
from jax import lax
from jax.experimental import pallas as pl
from jax.experimental.pallas import tpu as pltpu
from jax.sharding import PartitionSpec as P

SCALE = 2.0
TILES = 3
LONG = 7000000000
F32 = jnp.float32
BF16 = jnp.bfloat16
SMEM = pl.BlockSpec(memory_space=pltpu.SMEM)
VMEM = pl.BlockSpec(memory_space=pltpu.VMEM)
ANY = pl.BlockSpec(memory_space=pl.ANY)


def shape(*dims, dtype=BF16):
    return jax.ShapeDtypeStruct(dims, dtype)


def call(kernel, name, out_shape, in_specs, out_specs, scratch=(), grid=(), mib=32, flops=1):
    return pl.pallas_call(
        kernel, name=name, out_shape=out_shape, grid=grid, in_specs=in_specs, out_specs=out_specs,
        scratch_shapes=scratch,
        compiler_params=pltpu.CompilerParams(vmem_limit_bytes=mib * 1024 * 1024),
        cost_estimate=pl.CostEstimate(flops=flops, bytes_accessed=1, transcendentals=0),
    )


def shift(value, axis, by):
    size = lax.axis_size(axis)
    return lax.ppermute(value, axis, [(i, (i + by) % size) for i in range(size)])


def after(value, *others):
    return lax.optimization_barrier((value, *others))[0]


def nn(a, b):
    return lax.dot_general(a, b, (((1,), (0,)), ((), ())), preferred_element_type=F32)


def nt(a, b):
    return lax.dot_general(a, b, (((1,), (1,)), ((), ())), preferred_element_type=F32)


def tn(a, b):
    return lax.dot_general(a, b, (((0,), (0,)), ((), ())), preferred_element_type=F32)


def run(copies):
    for copy in copies:
        copy.start()
    for copy in copies:
        copy.wait()


def wanted_site(table, n_dp, s):
    return table[0, lax.axis_index("pair"), lax.rem(lax.axis_index("dp") + s, n_dp)]


def slot_of(owner, b, n_dp):
    return lax.rem(lax.axis_index("dp") - owner[b] + n_dp, n_dp)


def pack_kernel(n_dp, n_mp, n_share, table, down, up, w, *refs):
    maps, pieces, sem = refs[:n_dp], refs[n_dp:-1], refs[-1]
    feat, cols = down.shape[2], up.shape[2]
    part = feat // n_share
    place = lax.axis_index("groups") * lax.axis_size("pair") + lax.axis_index("pair")
    copies = []
    for s in range(n_dp):
        site = wanted_site(table, n_dp, s)
        copies.append(pltpu.make_async_copy(down.at[site], maps[s].at[:, pl.ds(0, feat)], sem.at[s]))
        copies.append(pltpu.make_async_copy(up.at[site], maps[s].at[:, pl.ds(feat, cols)], sem.at[n_dp + s]))
    for s in range(1, n_mp):
        row = pl.multiple_of(lax.rem(lax.axis_index("mp") + s, n_mp) * feat + place * part, part)
        copies.append(pltpu.make_async_copy(w.at[pl.ds(row, part)], pieces[s - 1], sem.at[2 * n_dp + s - 1]))
    run(copies)


def reduce_kernel(n_dp, owner, _, x, gy, *refs):
    maps, out, wide = refs[:n_dp], refs[n_dp], refs[n_dp + 1]
    rank = maps[0].shape[0]
    feat = x.shape[1]
    blocks = owner.shape[0]
    rows = x.shape[0] // blocks
    for s in range(n_dp):
        wide[s * rank:(s + 1) * rank, :] = maps[s][...]
    lane_slot = lax.broadcasted_iota(jnp.int32, (rows, n_dp * rank), 1) // rank
    full = nt(x[...], wide[:, :feat]), nt(gy[...], wide[:, feat:])
    for b in range(blocks):
        mine = lane_slot == slot_of(owner, b, n_dp)
        halves = []
        for one in full:
            kept = jnp.where(mine, one[b * rows:(b + 1) * rows], 0.0)
            total = kept[:, :rank]
            for s in range(1, n_dp):
                total = total + kept[:, s * rank:(s + 1) * rank]
            halves.append(total)
        out[b * rows:(b + 1) * rows, :] = jnp.concatenate(halves, axis=1).astype(BF16)


def send_kernel(n_groups, n_pair, feat, n_mp, _, x, *refs):
    n_other, n_share = n_mp - 1, n_groups * n_pair
    pieces, outs, rows = refs[:n_other * n_share], refs[-2 * n_other:-n_other], refs[-n_other:]
    part = feat // n_share

    @pl.when(pl.program_id(0) == 0)
    def _():
        for s in range(n_other):
            for k in range(n_share):
                group = lax.rem(lax.axis_index("groups") + n_groups - k // n_pair, n_groups)
                core = lax.rem(lax.axis_index("pair") + n_pair - k % n_pair, n_pair)
                at = pl.multiple_of((group * n_pair + core) * part, part)
                rows[s][pl.ds(at, part), :] = pieces[s * n_share + k][...]

    for s in range(n_other):
        outs[s][...] = nn(x[...], rows[s][...]).astype(BF16)


def grad_kernel(n_dp, n_mp, owner, x, gy, *refs):
    parts, grads, u_wide, h_wide = refs[:n_mp], refs[n_mp:n_mp + n_dp], refs[-2], refs[-1]
    rank = u_wide.shape[1] // n_dp
    feat = x.shape[1]
    blocks = owner.shape[0]
    rows = x.shape[0] // blocks
    total = parts[0][...].astype(F32)
    for part in parts[1:]:
        total = total + part[...].astype(F32)
    lane_slot = lax.broadcasted_iota(jnp.int32, (rows, n_dp * rank), 1) // rank
    for b in range(blocks):
        mine = lane_slot == slot_of(owner, b, n_dp)
        for k, wide in enumerate((u_wide, h_wide)):
            one = total[b * rows:(b + 1) * rows, k * rank:(k + 1) * rank]
            spread = jnp.concatenate([one] * n_dp, axis=1)
            wide[b * rows:(b + 1) * rows, :] = jnp.where(mine, spread, 0.0).astype(BF16)
    for wide, act, lo in ((h_wide, x, 0), (u_wide, gy, feat)):
        full = tn(wide[...], act[...])
        for s in range(n_dp):
            grads[s][:, lo:lo + full.shape[1]] = full[s * rank:(s + 1) * rank].astype(BF16)


def back_kernel(n_dp, n_mp, w, gy, wide, *refs):
    n_other = n_mp - 1
    gots, rows = refs[:n_other], refs[n_other:2 * n_other]
    maps, out, own, downs = refs[2 * n_other:-3], refs[-3], refs[-2], refs[-1]
    rank = maps[0].shape[0]
    feat = out.shape[1]

    @pl.when(pl.program_id(0) == 0)
    def _():
        own[...] = w[pl.ds(pl.multiple_of(lax.axis_index("mp") * feat, feat), feat), :]
        for s in range(n_dp):
            downs[s * rank:(s + 1) * rank, :] = maps[s][:, :feat]

    total = nt(gy[...], own[...]) + SCALE * nn(wide[...], downs[...])
    for got, row in zip(gots, rows):
        total = total + nt(got[...], row[...])
    out[...] = total.astype(BF16)


def own_kernel(n_dp, w, x, wide, *refs):
    maps, out, ups = refs[:n_dp], refs[n_dp], refs[n_dp + 1]
    rank = maps[0].shape[0]
    feat = x.shape[1]

    @pl.when(pl.program_id(0) == 0)
    def _():
        for s in range(n_dp):
            ups[s * rank:(s + 1) * rank, :] = maps[s][:, feat:]

    own = w[pl.ds(pl.multiple_of(lax.axis_index("mp") * feat, feat), feat), :]
    out[...] = nn(x[...], own) + SCALE * nn(wide[...], ups[...])


def add_kernel(*refs):
    total = refs[0][...]
    for ref in refs[1:-1]:
        total = total + ref[...].astype(F32)
    refs[-1][...] = total.astype(BF16)


def site_kernel(n_dp, table, _, __, *refs):
    grads, out = refs[:n_dp], refs[-1]
    for site in range(out.shape[0]):
        total = jnp.zeros(out.shape[1:], F32)
        for s in range(n_dp):
            use = wanted_site(table, n_dp, s) == site
            total = total + jnp.where(use, grads[s][...].astype(F32), 0.0)
        out[site] = total.astype(BF16)


def last_kernel(feat, *refs):
    parts, down, up = refs[:-2], refs[-2], refs[-1]
    total = parts[0][...].astype(F32)
    for part in parts[1:]:
        total = total + part[...].astype(F32)
    total = SCALE * total
    down[...] = total[:, :, :feat]
    up[...] = total[:, :, feat:]


def shards(x, w, down, up, gy, owner, table):
    tok, feat = x.shape
    cols = w.shape[1]
    sites, rank = up.shape[:2]
    n_groups, n_dp, n_mp, n_pair = (lax.axis_size(a) for a in ("groups", "dp", "mp", "pair"))
    n_other, n_share = n_mp - 1, n_groups * n_pair
    down = down.transpose(0, 2, 1)
    part = feat // n_share
    both = feat + cols
    tile = tok // TILES
    row_block = lambda width: pl.BlockSpec((tile, width), lambda i: (i, 0))
    whole = lambda *dims: pl.BlockSpec(dims, lambda i: (0,) * len(dims))

    packed = call(
        functools.partial(pack_kernel, n_dp, n_mp, n_share), "pack",
        [shape(rank, both)] * n_dp + [shape(part, cols)] * n_other,
        [SMEM, ANY, ANY, ANY], [VMEM] * (n_dp + n_other),
        [pltpu.SemaphoreType.DMA((2 * n_dp + n_other,))], mib=60,
    )(table, down, up, w)
    gy_got = [shift(gy, "mp", s) for s in range(1, n_mp)]
    maps = [packed[0]] + [shift(packed[s], "dp", s) for s in range(1, n_dp)]
    pieces = [shift(packed[n_dp + s - 1], "mp", s) for s in range(1, n_mp)]

    uh = call(
        functools.partial(reduce_kernel, n_dp), "uh",
        shape(tok, 2 * rank), [SMEM, ANY] + [VMEM] * (2 + n_dp), VMEM,
        [pltpu.VMEM((n_dp * rank, both), BF16)],
    )(owner, gy_got[0], x, gy, *maps)
    uhs = [uh] + [shift(uh, "mp", s) for s in range(1, n_mp)]

    *grads, u_wide, h_wide = call(
        functools.partial(grad_kernel, n_dp, n_mp), "grads",
        [shape(rank, both)] * n_dp + [shape(tok, n_dp * rank)] * 2,
        [SMEM] + [VMEM] * (2 + n_mp), [VMEM] * (n_dp + 2),
    )(owner, x, gy, *uhs)
    grads = [grads[0]] + [shift(grads[s], "dp", n_dp - s) for s in range(1, n_dp)]

    parts = []
    for piece in pieces:
        for j in range(n_groups):
            one = shift(after(piece, uh), "groups", j) if j else piece
            parts += [shift(after(one, h_wide), "pair", q) if q else one for q in range(n_pair)]

    sent = call(
        functools.partial(send_kernel, n_groups, n_pair, feat, n_mp), "y_send",
        [shape(tok, cols)] * n_other + [shape(feat, cols)] * n_other,
        [ANY, row_block(feat)] + [whole(part, cols)] * len(parts),
        [row_block(cols)] * n_other + [whole(feat, cols)] * n_other,
        grid=(TILES,),
    )(u_wide, x, *parts)
    w_rows = sent[n_other:]
    y_got = [shift(sent[s - 1], "mp", n_mp - s) for s in range(1, n_mp)]

    y_own = call(
        functools.partial(own_kernel, n_dp), "y_own",
        shape(tok, cols, dtype=F32),
        [whole(*w.shape), row_block(feat), row_block(n_dp * rank)] + [whole(rank, both)] * n_dp,
        row_block(cols), [pltpu.VMEM((n_dp * rank, cols), BF16)], grid=(TILES,), flops=LONG,
    )(w, x, u_wide, *maps)

    back = call(
        functools.partial(back_kernel, n_dp, n_mp), "back",
        shape(tok, feat),
        [whole(*w.shape), row_block(cols), row_block(n_dp * rank)] + [row_block(cols)] * n_other
        + [whole(feat, cols)] * n_other + [whole(rank, both)] * n_dp,
        row_block(feat), [pltpu.VMEM((feat, cols), BF16), pltpu.VMEM((n_dp * rank, feat), BF16)], grid=(TILES,),
    )(w, gy, h_wide, *gy_got, *w_rows, *maps)

    summed = call(
        functools.partial(site_kernel, n_dp), "sites",
        shape(sites, rank, both), [SMEM, ANY, ANY] + [VMEM] * n_dp, VMEM,
    )(table, back, y_own, *grads)
    halves = [summed] + [shift(summed, "pair", q) for q in range(1, n_pair)]
    down_grad, up_grad = call(
        functools.partial(last_kernel, feat), "gradients",
        [shape(sites, rank, feat, dtype=F32), shape(sites, rank, cols, dtype=F32)],
        [VMEM] * n_pair, [VMEM] * 2,
    )(*halves)

    y = call(
        add_kernel, "y_add", shape(tok, cols), [row_block(cols)] * n_mp, row_block(cols), grid=(TILES,),
    )(y_own, *y_got)
    return y, back, down_grad.transpose(0, 2, 1), up_grad


def solution(mesh):
    rows = P(("groups", "dp", "pair"), "mp")
    in_specs = (
        rows,
        P(None, "mp"),
        P(("groups", "dp"), "mp", None),
        P(("groups", "dp"), None, "mp"),
        rows,
        P(("groups", "dp", "pair")),
        P(("groups", "dp"), None, None),
    )
    out_specs = (rows, rows, P(("groups", "dp"), "mp", None), P(("groups", "dp"), None, "mp"))
    return jax.shard_map(shards, mesh=mesh, in_specs=in_specs, out_specs=out_specs, check_vma=False)
```

```python
import functools

import jax
import jax.numpy as jnp
from jax import lax
from jax.experimental import pallas as pl
from jax.experimental.pallas import tpu as pltpu
from jax.sharding import PartitionSpec as P

SCALE = 2.0
TILES = 3
GRAD_COST = 15_000_000_000
F32 = jnp.float32
BF16 = jnp.bfloat16
SMEM = pl.BlockSpec(memory_space=pltpu.SMEM)
VMEM = pl.BlockSpec(memory_space=pltpu.VMEM)
ANY = pl.BlockSpec(memory_space=pl.ANY)


def shape(*dims, dtype=BF16):
    return jax.ShapeDtypeStruct(dims, dtype)


def call(kernel, name, out_shape, in_specs, out_specs, scratch=(), grid=(), mib=32, flops=1):
    return pl.pallas_call(
        kernel, name=name, out_shape=out_shape, grid=grid, in_specs=in_specs, out_specs=out_specs,
        scratch_shapes=scratch,
        compiler_params=pltpu.CompilerParams(vmem_limit_bytes=mib * 1024 * 1024),
        cost_estimate=pl.CostEstimate(flops=flops, bytes_accessed=1, transcendentals=0),
    )


def shift(value, axis, by):
    size = lax.axis_size(axis)
    return lax.ppermute(value, axis, [(i, (i + by) % size) for i in range(size)])


def after(value, *others):
    return lax.optimization_barrier((value, *others))[0]


def nn(a, b):
    return lax.dot_general(a, b, (((1,), (0,)), ((), ())), preferred_element_type=F32)


def nt(a, b):
    return lax.dot_general(a, b, (((1,), (1,)), ((), ())), preferred_element_type=F32)


def tn(a, b):
    return lax.dot_general(a, b, (((0,), (0,)), ((), ())), preferred_element_type=F32)


def run(copies):
    for copy in copies:
        copy.start()
    for copy in copies:
        copy.wait()


def wanted_site(table, n_dp, s):
    return table[0, lax.axis_index("pair"), lax.rem(lax.axis_index("dp") + s, n_dp)]


def slot_of(owner, b, n_dp):
    return lax.rem(lax.axis_index("dp") - owner[b] + n_dp, n_dp)


def pack_kernel(n_dp, n_mp, n_pair, table, down, up, w, *refs):
    away = n_dp - 1
    ups, downs, pieces, sem = refs[:away], refs[away:2 * away], refs[2 * away:-1], refs[-1]
    feat = w.shape[0] // n_mp
    part = feat // n_pair
    copies = []
    for s in range(away):
        site = wanted_site(table, n_dp, s + 1)
        copies.append(pltpu.make_async_copy(up.at[site], ups[s], sem.at[s]))
        copies.append(pltpu.make_async_copy(down.at[site], downs[s], sem.at[away + s]))
    for s in range(1, n_mp):
        row = lax.rem(lax.axis_index("mp") + s, n_mp) * feat + lax.axis_index("pair") * part
        row = pl.multiple_of(row, part)
        copies.append(pltpu.make_async_copy(w.at[pl.ds(row, part)], pieces[s - 1], sem.at[2 * away + s - 1]))
    run(copies)


def gather_maps(n_dp, table, own, gots, wide):
    rank = own.shape[1]
    wide[:rank, :] = own[wanted_site(table, n_dp, 0)]
    for s in range(1, n_dp):
        wide[s * rank:(s + 1) * rank, :] = gots[s - 1][...]


def reduce_kernel(n_dp, owner, table, act, _, own, *refs):
    gots, out, wide = refs[:n_dp - 1], refs[n_dp - 1], refs[n_dp]
    rank = own.shape[1]
    blocks = owner.shape[0]
    rows = act.shape[0] // blocks
    gather_maps(n_dp, table, own, gots, wide)
    full = nt(act[...], wide[...])
    lane_slot = lax.broadcasted_iota(jnp.int32, (rows, n_dp * rank), 1) // rank
    folded = []
    for b in range(blocks):
        kept = jnp.where(lane_slot == slot_of(owner, b, n_dp), full[b * rows:(b + 1) * rows], 0.0)
        total = kept[:, :rank]
        for s in range(1, n_dp):
            total = total + kept[:, s * rank:(s + 1) * rank]
        folded.append(total)
    for j in range(blocks // 2):
        pair = jnp.concatenate([folded[2 * j], folded[2 * j + 1]], axis=1)
        out[j * rows:(j + 1) * rows, :] = pair.astype(BF16)


def grad_kernel(n_dp, n_part, n_behind, owner, act, *refs):
    refs = refs[n_behind:]
    parts, grads, wide = refs[:n_part], refs[n_part:n_part + n_dp], refs[n_part + n_dp]
    rank = wide.shape[1] // n_dp
    blocks = owner.shape[0]
    rows = act.shape[0] // blocks
    total = parts[0][...].astype(F32)
    for part in parts[1:]:
        total = total + part[...].astype(F32)
    lane_slot = lax.broadcasted_iota(jnp.int32, (rows, n_dp * rank), 1) // rank
    for b in range(blocks):
        one = total[(b // 2) * rows:(b // 2 + 1) * rows, (b % 2) * rank:(b % 2 + 1) * rank]
        spread = jnp.concatenate([one] * n_dp, axis=1)
        kept = jnp.where(lane_slot == slot_of(owner, b, n_dp), spread, 0.0)
        wide[b * rows:(b + 1) * rows, :] = kept.astype(BF16)
    full = tn(wide[...], act[...])
    for s in range(n_dp):
        grads[s][...] = full[s * rank:(s + 1) * rank].astype(BF16)


def send_kernel(n_pair, feat, n_mp, _, __, x, *refs):
    n_other = n_mp - 1
    pieces, outs, rows = refs[:n_other * n_pair], refs[n_other * n_pair:n_other * n_pair + n_other], refs[-n_other:]
    part = feat // n_pair

    @pl.when(pl.program_id(0) == 0)
    def _():
        for s in range(n_other):
            for q in range(n_pair):
                at = lax.rem(lax.axis_index("pair") + n_pair - q, n_pair) * part
                rows[s][pl.ds(pl.multiple_of(at, part), part), :] = pieces[s * n_pair + q][...]

    for s in range(n_other):
        outs[s][...] = nn(x[...], rows[s][...]).astype(BF16)


def back_kernel(n_dp, n_mp, table, _, *refs):
    w, gys, rows, wide, own_down, downs, out, token, own, maps = (
        refs[0], refs[1:1 + n_mp], refs[1 + n_mp:2 * n_mp], refs[2 * n_mp], refs[2 * n_mp + 1],
        refs[2 * n_mp + 2:-4], refs[-4], refs[-3], refs[-2], refs[-1],
    )
    feat = out.shape[1]

    @pl.when(pl.program_id(0) == 0)
    def _():
        token[...] = jnp.zeros_like(token)
        own[...] = w[pl.ds(pl.multiple_of(lax.axis_index("mp") * feat, feat), feat), :]
        gather_maps(n_dp, table, own_down, downs, maps)

    total = nt(gys[0][...], own[...]) + SCALE * nn(wide[...], maps[...])
    for gy, row in zip(gys[1:], rows):
        total = total + nt(gy[...], row[...])
    out[...] = total.astype(BF16)


def own_kernel(n_dp, table, w, x, wide, own_up, *refs):
    ups, out, picks, maps = refs[:n_dp - 1], refs[n_dp - 1], refs[n_dp], refs[n_dp + 1]
    feat = x.shape[1]

    @pl.when(pl.program_id(0) == 0)
    def _():
        gather_maps(n_dp, table, own_up, ups, maps)
        row = lax.broadcasted_iota(jnp.int32, picks.shape, 0)
        total = jnp.zeros(picks.shape, jnp.int32)
        for s in range(n_dp):
            total = jnp.where(row == s, wanted_site(table, n_dp, s), total)
        picks[...] = total

    own = w[pl.ds(pl.multiple_of(lax.axis_index("mp") * feat, feat), feat), :]
    out[...] = nn(x[...], own) + SCALE * nn(wide[...], maps[...])


def add_kernel(*refs):
    total = refs[0][...]
    for ref in refs[1:-1]:
        total = total + ref[...].astype(F32)
    refs[-1][...] = total.astype(BF16)


def site_kernel(n_dp, feat, picks, _, *refs):
    downs, ups, out = refs[:n_dp], refs[n_dp:2 * n_dp], refs[-1]
    for site in range(out.shape[0]):
        for grads, lo, hi in ((downs, 0, feat), (ups, feat, out.shape[2])):
            total = jnp.zeros((out.shape[1], hi - lo), F32)
            for s in range(n_dp):
                use = picks[s:s + 1, :1] == site
                total = total + jnp.where(use, grads[s][...].astype(F32), 0.0)
            out[site, :, lo:hi] = total.astype(BF16)


def last_kernel(feat, *refs):
    parts, down, up = refs[:-2], refs[-2], refs[-1]
    total = parts[0][...].astype(F32)
    for part in parts[1:]:
        total = total + part[...].astype(F32)
    total = SCALE * total
    down[...] = total[:, :, :feat]
    up[...] = total[:, :, feat:]


def shards(x, w, down, up, gy, owner, table):
    tok, feat = x.shape
    cols = w.shape[1]
    sites, rank = up.shape[:2]
    n_dp, n_mp, n_pair = (lax.axis_size(a) for a in ("dp", "mp", "pair"))
    n_other = n_mp - 1
    down = down.transpose(0, 2, 1)
    part = feat // n_pair
    tile = tok // TILES
    row_block = lambda width: pl.BlockSpec((tile, width), lambda i: (i, 0))
    whole = lambda *dims: pl.BlockSpec(dims, lambda i: (0,) * len(dims))

    away = n_dp - 1
    packed = call(
        functools.partial(pack_kernel, n_dp, n_mp, n_pair), "pack",
        [shape(rank, cols)] * away + [shape(rank, feat)] * away + [shape(part, cols)] * n_other,
        [SMEM, ANY, ANY, ANY], [VMEM] * (2 * away + n_other),
        [pltpu.SemaphoreType.DMA((2 * away + n_other,))], mib=60,
    )(table, down, up, w)
    pieces = [shift(packed[2 * away + s - 1], "mp", s) for s in range(1, n_mp)]
    ups = [shift(packed[s - 1], "dp", s) for s in range(1, n_dp)]
    downs = [shift(after(packed[away + s - 1], ups[1 % away]), "dp", s) for s in range(1, n_dp)]

    def low_rank(act, own, maps, behind, name):
        mine = call(
            functools.partial(reduce_kernel, n_dp), name + "_part",
            shape(tok // 2, 2 * rank), [SMEM, SMEM, VMEM, ANY] + [VMEM] * n_dp, VMEM,
            [pltpu.VMEM((n_dp * rank, act.shape[1]), BF16)],
        )(owner, table, act, behind, own, *maps)
        return [mine] + [shift(mine, "mp", s) for s in range(1, n_mp)]

    def gradient(act, parts, behind, name, flops):
        *grads, wide = call(
            functools.partial(grad_kernel, n_dp, n_mp, len(behind)), name + "_grad",
            [shape(rank, act.shape[1])] * n_dp + [shape(tok, n_dp * rank)],
            [SMEM, VMEM] + [ANY] * len(behind) + [VMEM] * n_mp, [VMEM] * (n_dp + 1), flops=flops,
        )(owner, act, *behind, *parts)
        return [grads[0]] + [shift(grads[s], "dp", n_dp - s) for s in range(1, n_dp)], wide

    h_parts = low_rank(gy, up, ups, ups[0], "h")
    gy_got = [shift(after(gy, *pieces), "mp", s) for s in range(1, n_mp)]
    down_back, h_wide = gradient(x, h_parts, downs, "down", GRAD_COST)
    u_parts = low_rank(x, down, downs, h_wide, "u")

    parts = []
    for piece in pieces:
        parts += [piece] + [shift(after(piece, h_wide), "pair", q) for q in range(1, n_pair)]
    sent = call(
        functools.partial(send_kernel, n_pair, feat, n_mp), "y_send",
        [shape(tok, cols)] * n_other + [shape(feat, cols)] * n_other,
        [ANY, ANY, row_block(feat)] + [whole(part, cols)] * len(parts),
        [row_block(cols)] * n_other + [whole(feat, cols)] * n_other,
        grid=(TILES,),
    )(u_parts[0], down_back[1], x, *parts)
    w_rows = sent[n_other:]
    y_got = [shift(sent[s - 1], "mp", n_mp - s) for s in range(1, n_mp)]
    up_back, u_wide = gradient(gy, u_parts, down_back[2:] + gy_got, "up", GRAD_COST)

    y_own, picks = call(
        functools.partial(own_kernel, n_dp), "y_own",
        [shape(tok, cols, dtype=F32), shape(-(-n_dp // 8) * 8, 128, dtype=jnp.int32)],
        [SMEM, whole(*w.shape), row_block(feat), row_block(n_dp * rank), whole(*up.shape)]
        + [whole(rank, cols)] * away,
        [row_block(cols), whole(-(-n_dp // 8) * 8, 128)],
        [pltpu.VMEM((n_dp * rank, cols), BF16)], grid=(TILES,),
    )(table, w, x, u_wide, up, *ups)

    back, token = call(
        functools.partial(back_kernel, n_dp, n_mp), "back",
        [shape(tok, feat), shape(8, 128, dtype=F32)],
        [SMEM, ANY, whole(*w.shape)] + [row_block(cols)] * n_mp + [whole(feat, cols)] * n_other
        + [row_block(n_dp * rank), whole(*down.shape)] + [whole(rank, feat)] * away,
        [row_block(feat), whole(8, 128)],
        [pltpu.VMEM((feat, cols), BF16), pltpu.VMEM((n_dp * rank, feat), BF16)], grid=(TILES,),
    )(table, u_wide, w, gy, *gy_got, *w_rows, h_wide, down, *downs)

    summed = call(
        functools.partial(site_kernel, n_dp, feat), "sites",
        shape(sites, rank, feat + cols), [VMEM, ANY] + [VMEM] * (2 * n_dp), VMEM,
    )(picks, token, *down_back, *up_back)
    both = [summed] + [shift(summed, "pair", q) for q in range(1, n_pair)]
    down_grad, up_grad = call(
        functools.partial(last_kernel, feat), "gradients",
        [shape(sites, rank, feat, dtype=F32), shape(sites, rank, cols, dtype=F32)],
        [VMEM] * n_pair, [VMEM] * 2,
    )(*both)

    y = call(
        add_kernel, "y_add", shape(tok, cols), [row_block(cols)] * n_mp, row_block(cols), grid=(TILES,),
    )(y_own, *y_got)
    return y, back, down_grad.transpose(0, 2, 1), up_grad


def solution(mesh):
    rows = P(("groups", "dp", "pair"), "mp")
    in_specs = (
        rows,
        P(None, "mp"),
        P(("groups", "dp"), "mp", None),
        P(("groups", "dp"), None, "mp"),
        rows,
        P(("groups", "dp", "pair")),
        P(("groups", "dp"), None, None),
    )
    out_specs = (rows, rows, P(("groups", "dp"), "mp", None), P(("groups", "dp"), None, "mp"))
    return jax.shard_map(shards, mesh=mesh, in_specs=in_specs, out_specs=out_specs, check_vma=False)
```

```python
import functools

import jax
import jax.numpy as jnp
from jax import lax
from jax.experimental import pallas as pl
from jax.experimental.pallas import tpu as pltpu
from jax.sharding import PartitionSpec as P

SCALE = 2.0
TILES = 3
GRAD_COST = 15_000_000_000
F32 = jnp.float32
BF16 = jnp.bfloat16
SMEM = pl.BlockSpec(memory_space=pltpu.SMEM)
VMEM = pl.BlockSpec(memory_space=pltpu.VMEM)
ANY = pl.BlockSpec(memory_space=pl.ANY)


def shape(*dims, dtype=BF16):
    return jax.ShapeDtypeStruct(dims, dtype)


def call(kernel, name, out_shape, in_specs, out_specs, scratch=(), grid=(), mib=32, flops=1):
    return pl.pallas_call(
        kernel, name=name, out_shape=out_shape, grid=grid, in_specs=in_specs, out_specs=out_specs,
        scratch_shapes=scratch,
        compiler_params=pltpu.CompilerParams(vmem_limit_bytes=mib * 1024 * 1024),
        cost_estimate=pl.CostEstimate(flops=flops, bytes_accessed=1, transcendentals=0),
    )


def shift(value, axis, by):
    size = lax.axis_size(axis)
    return lax.ppermute(value, axis, [(i, (i + by) % size) for i in range(size)])


def after(value, *others):
    return lax.optimization_barrier((value, *others))[0]


def nn(a, b):
    return lax.dot_general(a, b, (((1,), (0,)), ((), ())), preferred_element_type=F32)


def nt(a, b):
    return lax.dot_general(a, b, (((1,), (1,)), ((), ())), preferred_element_type=F32)


def tn(a, b):
    return lax.dot_general(a, b, (((0,), (0,)), ((), ())), preferred_element_type=F32)


def run(copies):
    for copy in copies:
        copy.start()
    for copy in copies:
        copy.wait()


def wanted_site(table, n_dp, s):
    return table[0, lax.axis_index("pair"), lax.rem(lax.axis_index("dp") + s, n_dp)]


def slot_of(owner, b, n_dp):
    return lax.rem(lax.axis_index("dp") - owner[b] + n_dp, n_dp)


def pack_kernel(n_dp, n_mp, n_pair, table, down, up, w, *refs):
    away = n_dp - 1
    ups, downs, pieces, sem = refs[:away], refs[away:2 * away], refs[2 * away:-1], refs[-1]
    feat = w.shape[0] // n_mp
    part = feat // n_pair
    copies = []
    for s in range(away):
        site = wanted_site(table, n_dp, s + 1)
        copies.append(pltpu.make_async_copy(up.at[site], ups[s], sem.at[s]))
        copies.append(pltpu.make_async_copy(down.at[site], downs[s], sem.at[away + s]))
    for s in range(1, n_mp):
        row = lax.rem(lax.axis_index("mp") + s, n_mp) * feat + lax.axis_index("pair") * part
        row = pl.multiple_of(row, part)
        copies.append(pltpu.make_async_copy(w.at[pl.ds(row, part)], pieces[s - 1], sem.at[2 * away + s - 1]))
    run(copies)


def gather_maps(n_dp, table, own, gots, wide):
    rank = own.shape[1]
    wide[:rank, :] = own[wanted_site(table, n_dp, 0)]
    for s in range(1, n_dp):
        wide[s * rank:(s + 1) * rank, :] = gots[s - 1][...]


def reduce_kernel(n_dp, owner, table, act, _, own, *refs):
    gots, out, wide = refs[:n_dp - 1], refs[n_dp - 1], refs[n_dp]
    rank = own.shape[1]
    blocks = owner.shape[0]
    rows = act.shape[0] // blocks
    gather_maps(n_dp, table, own, gots, wide)
    full = nt(act[...], wide[...])
    lane_slot = lax.broadcasted_iota(jnp.int32, (rows, n_dp * rank), 1) // rank
    folded = []
    for b in range(blocks):
        kept = jnp.where(lane_slot == slot_of(owner, b, n_dp), full[b * rows:(b + 1) * rows], 0.0)
        total = kept[:, :rank]
        for s in range(1, n_dp):
            total = total + kept[:, s * rank:(s + 1) * rank]
        folded.append(total)
    for j in range(blocks // 2):
        pair = jnp.concatenate([folded[2 * j], folded[2 * j + 1]], axis=1)
        out[j * rows:(j + 1) * rows, :] = pair.astype(BF16)


def grad_kernel(n_dp, n_part, n_behind, owner, act, *refs):
    refs = refs[n_behind:]
    parts, grads, wide = refs[:n_part], refs[n_part:n_part + n_dp], refs[n_part + n_dp]
    rank = wide.shape[1] // n_dp
    blocks = owner.shape[0]
    rows = act.shape[0] // blocks
    total = parts[0][...].astype(F32)
    for part in parts[1:]:
        total = total + part[...].astype(F32)
    lane_slot = lax.broadcasted_iota(jnp.int32, (rows, n_dp * rank), 1) // rank
    for b in range(blocks):
        one = total[(b // 2) * rows:(b // 2 + 1) * rows, (b % 2) * rank:(b % 2 + 1) * rank]
        spread = jnp.concatenate([one] * n_dp, axis=1)
        kept = jnp.where(lane_slot == slot_of(owner, b, n_dp), spread, 0.0)
        wide[b * rows:(b + 1) * rows, :] = kept.astype(BF16)
    full = tn(wide[...], act[...])
    for s in range(n_dp):
        grads[s][...] = full[s * rank:(s + 1) * rank].astype(BF16)


def send_kernel(n_pair, feat, n_mp, _, __, x, *refs):
    n_other = n_mp - 1
    pieces, outs, rows = refs[:n_other * n_pair], refs[n_other * n_pair:n_other * n_pair + n_other], refs[-n_other:]
    part = feat // n_pair

    @pl.when(pl.program_id(0) == 0)
    def _():
        for s in range(n_other):
            for q in range(n_pair):
                at = lax.rem(lax.axis_index("pair") + n_pair - q, n_pair) * part
                rows[s][pl.ds(pl.multiple_of(at, part), part), :] = pieces[s * n_pair + q][...]

    for s in range(n_other):
        outs[s][...] = nn(x[...], rows[s][...]).astype(BF16)


def back_kernel(n_dp, n_mp, table, w, gy, wide, own_down, *refs):
    n_other = n_mp - 1
    gots, rows = refs[:n_other], refs[n_other:2 * n_other]
    downs, out, picks, own, maps = refs[2 * n_other:-4], refs[-4], refs[-3], refs[-2], refs[-1]
    feat = out.shape[1]

    @pl.when(pl.program_id(0) == 0)
    def _():
        own[...] = w[pl.ds(pl.multiple_of(lax.axis_index("mp") * feat, feat), feat), :]
        gather_maps(n_dp, table, own_down, downs, maps)
        row = lax.broadcasted_iota(jnp.int32, picks.shape, 0)
        sites = jnp.zeros(picks.shape, jnp.int32)
        for s in range(n_dp):
            sites = jnp.where(row == s, wanted_site(table, n_dp, s), sites)
        picks[...] = sites

    total = nt(gy[...], own[...]) + SCALE * nn(wide[...], maps[...])
    for got, row in zip(gots, rows):
        total = total + nt(got[...], row[...])
    out[...] = total.astype(BF16)


def base_kernel(_, w, x, out):
    feat = x.shape[1]
    out[...] = nn(x[...], w[pl.ds(pl.multiple_of(lax.axis_index("mp") * feat, feat), feat), :])


def add_kernel(n_dp, table, base, wide, own_up, *refs):
    ups, gots, out, maps = refs[:n_dp - 1], refs[n_dp - 1:-2], refs[-2], refs[-1]

    @pl.when(pl.program_id(0) == 0)
    def _():
        gather_maps(n_dp, table, own_up, ups, maps)

    total = base[...] + SCALE * nn(wide[...], maps[...])
    for got in gots:
        total = total + got[...].astype(F32)
    out[...] = total.astype(BF16)


def site_kernel(n_dp, feat, picks, *refs):
    downs, ups, out = refs[:n_dp], refs[n_dp:2 * n_dp], refs[-1]
    for site in range(out.shape[0]):
        for grads, lo, hi in ((downs, 0, feat), (ups, feat, out.shape[2])):
            total = jnp.zeros((out.shape[1], hi - lo), F32)
            for s in range(n_dp):
                use = picks[s:s + 1, :1] == site
                total = total + jnp.where(use, grads[s][...].astype(F32), 0.0)
            out[site, :, lo:hi] = total.astype(BF16)


def last_kernel(feat, *refs):
    parts, down, up = refs[:-2], refs[-2], refs[-1]
    total = parts[0][...].astype(F32)
    for part in parts[1:]:
        total = total + part[...].astype(F32)
    total = SCALE * total
    down[...] = total[:, :, :feat]
    up[...] = total[:, :, feat:]


def shards(x, w, down, up, gy, owner, table):
    tok, feat = x.shape
    cols = w.shape[1]
    sites, rank = up.shape[:2]
    n_dp, n_mp, n_pair = (lax.axis_size(a) for a in ("dp", "mp", "pair"))
    n_other = n_mp - 1
    down = down.transpose(0, 2, 1)
    part = feat // n_pair
    tile = tok // TILES
    row_block = lambda width: pl.BlockSpec((tile, width), lambda i: (i, 0))
    whole = lambda *dims: pl.BlockSpec(dims, lambda i: (0,) * len(dims))

    away = n_dp - 1
    packed = call(
        functools.partial(pack_kernel, n_dp, n_mp, n_pair), "pack",
        [shape(rank, cols)] * away + [shape(rank, feat)] * away + [shape(part, cols)] * n_other,
        [SMEM, ANY, ANY, ANY], [VMEM] * (2 * away + n_other),
        [pltpu.SemaphoreType.DMA((2 * away + n_other,))], mib=60,
    )(table, down, up, w)
    pieces = [shift(packed[2 * away + s - 1], "mp", s) for s in range(1, n_mp)]
    ups = [shift(packed[s - 1], "dp", s) for s in range(1, n_dp)]
    downs = [shift(after(packed[away + s - 1], ups[1 % away]), "dp", s) for s in range(1, n_dp)]

    def low_rank(act, own, maps, behind, name):
        mine = call(
            functools.partial(reduce_kernel, n_dp), name + "_part",
            shape(tok // 2, 2 * rank), [SMEM, SMEM, VMEM, ANY] + [VMEM] * n_dp, VMEM,
            [pltpu.VMEM((n_dp * rank, act.shape[1]), BF16)],
        )(owner, table, act, behind, own, *maps)
        return [mine] + [shift(mine, "mp", s) for s in range(1, n_mp)]

    def gradient(act, parts, behind, name, flops):
        *grads, wide = call(
            functools.partial(grad_kernel, n_dp, n_mp, len(behind)), name + "_grad",
            [shape(rank, act.shape[1])] * n_dp + [shape(tok, n_dp * rank)],
            [SMEM, VMEM] + [ANY] * len(behind) + [VMEM] * n_mp, [VMEM] * (n_dp + 1), flops=flops,
        )(owner, act, *behind, *parts)
        return [grads[0]] + [shift(grads[s], "dp", n_dp - s) for s in range(1, n_dp)], wide

    h_parts = low_rank(gy, up, ups, ups[0], "h")
    gy_got = [shift(after(gy, *pieces), "mp", s) for s in range(1, n_mp)]
    base = call(
        base_kernel, "base", shape(tok, cols, dtype=F32),
        [ANY, whole(*w.shape), row_block(feat)], row_block(cols), grid=(TILES,),
    )(h_parts[1 % n_mp], w, x)
    down_back, h_wide = gradient(x, h_parts, [base] + downs, "down", GRAD_COST)
    u_parts = low_rank(x, down, downs, h_wide, "u")

    parts = []
    for piece in pieces:
        parts += [piece] + [shift(after(piece, h_wide), "pair", q) for q in range(1, n_pair)]
    sent = call(
        functools.partial(send_kernel, n_pair, feat, n_mp), "y_send",
        [shape(tok, cols)] * n_other + [shape(feat, cols)] * n_other,
        [ANY, ANY, row_block(feat)] + [whole(part, cols)] * len(parts),
        [row_block(cols)] * n_other + [whole(feat, cols)] * n_other,
        grid=(TILES,),
    )(u_parts[0], down_back[1], x, *parts)
    w_rows = sent[n_other:]
    y_got = [shift(sent[s - 1], "mp", n_mp - s) for s in range(1, n_mp)]
    back, picks = call(
        functools.partial(back_kernel, n_dp, n_mp), "back",
        [shape(tok, feat), shape(-(-n_dp // 8) * 8, 128, dtype=jnp.int32)],
        [SMEM, whole(*w.shape), row_block(cols), row_block(n_dp * rank), whole(*down.shape)]
        + [row_block(cols)] * n_other + [whole(feat, cols)] * n_other + [whole(rank, feat)] * away,
        [row_block(feat), whole(-(-n_dp // 8) * 8, 128)],
        [pltpu.VMEM((feat, cols), BF16), pltpu.VMEM((n_dp * rank, feat), BF16)], grid=(TILES,),
    )(table, w, gy, h_wide, down, *gy_got, *w_rows, *downs)
    up_back, u_wide = gradient(gy, u_parts, [picks] + down_back[2:], "up", GRAD_COST)

    summed = call(
        functools.partial(site_kernel, n_dp, feat), "sites",
        shape(sites, rank, feat + cols), [VMEM] + [VMEM] * (2 * n_dp), VMEM,
    )(picks, *down_back, *up_back)
    both = [summed] + [shift(summed, "pair", q) for q in range(1, n_pair)]
    down_grad, up_grad = call(
        functools.partial(last_kernel, feat), "gradients",
        [shape(sites, rank, feat, dtype=F32), shape(sites, rank, cols, dtype=F32)],
        [VMEM] * n_pair, [VMEM] * 2,
    )(*both)

    y = call(
        functools.partial(add_kernel, n_dp), "y_add", shape(tok, cols),
        [SMEM, row_block(cols), row_block(n_dp * rank), whole(*up.shape)] + [whole(rank, cols)] * away
        + [row_block(cols)] * n_other,
        row_block(cols), [pltpu.VMEM((n_dp * rank, cols), BF16)], grid=(TILES,),
    )(table, base, u_wide, up, *ups, *y_got)
    return y, back, down_grad.transpose(0, 2, 1), up_grad


def solution(mesh):
    rows = P(("groups", "dp", "pair"), "mp")
    in_specs = (
        rows,
        P(None, "mp"),
        P(("groups", "dp"), "mp", None),
        P(("groups", "dp"), None, "mp"),
        rows,
        P(("groups", "dp", "pair")),
        P(("groups", "dp"), None, None),
    )
    out_specs = (rows, rows, P(("groups", "dp"), "mp", None), P(("groups", "dp"), None, "mp"))
    return jax.shard_map(shards, mesh=mesh, in_specs=in_specs, out_specs=out_specs, check_vma=False)
```

```python
import functools

import jax
import jax.numpy as jnp
from jax import lax
from jax.experimental import pallas as pl
from jax.experimental.pallas import tpu as pltpu
from jax.sharding import PartitionSpec as P

SCALE = 2.0
TILES = 3
GRAD_COST = 15_000_000_000
F32 = jnp.float32
BF16 = jnp.bfloat16
SMEM = pl.BlockSpec(memory_space=pltpu.SMEM)
VMEM = pl.BlockSpec(memory_space=pltpu.VMEM)
ANY = pl.BlockSpec(memory_space=pl.ANY)


def shape(*dims, dtype=BF16):
    return jax.ShapeDtypeStruct(dims, dtype)


def call(kernel, name, out_shape, in_specs, out_specs, scratch=(), grid=(), mib=32, flops=1):
    return pl.pallas_call(
        kernel, name=name, out_shape=out_shape, grid=grid, in_specs=in_specs, out_specs=out_specs,
        scratch_shapes=scratch,
        compiler_params=pltpu.CompilerParams(vmem_limit_bytes=mib * 1024 * 1024),
        cost_estimate=pl.CostEstimate(flops=flops, bytes_accessed=1, transcendentals=0),
    )


def shift(value, axis, by):
    size = lax.axis_size(axis)
    return lax.ppermute(value, axis, [(i, (i + by) % size) for i in range(size)])


def after(value, *others):
    return lax.optimization_barrier((value, *others))[0]


def nn(a, b):
    return lax.dot_general(a, b, (((1,), (0,)), ((), ())), preferred_element_type=F32)


def nt(a, b):
    return lax.dot_general(a, b, (((1,), (1,)), ((), ())), preferred_element_type=F32)


def tn(a, b):
    return lax.dot_general(a, b, (((0,), (0,)), ((), ())), preferred_element_type=F32)


def run(copies):
    for copy in copies:
        copy.start()
    for copy in copies:
        copy.wait()


def wanted_site(table, n_dp, s):
    return table[0, lax.axis_index("pair"), lax.rem(lax.axis_index("dp") + s, n_dp)]


def slot_of(owner, b, n_dp):
    return lax.rem(lax.axis_index("dp") - owner[b] + n_dp, n_dp)


def pack_kernel(n_dp, n_mp, n_pair, table, down, up, w, *refs):
    away = n_dp - 1
    ups, downs, pieces, sem = refs[:away], refs[away:2 * away], refs[2 * away:-1], refs[-1]
    feat = w.shape[0] // n_mp
    part = feat // n_pair
    copies = []
    for s in range(away):
        site = wanted_site(table, n_dp, s + 1)
        copies.append(pltpu.make_async_copy(up.at[site], ups[s], sem.at[s]))
        copies.append(pltpu.make_async_copy(down.at[site], downs[s], sem.at[away + s]))
    for s in range(1, n_mp):
        row = lax.rem(lax.axis_index("mp") + s, n_mp) * feat + lax.axis_index("pair") * part
        row = pl.multiple_of(row, part)
        copies.append(pltpu.make_async_copy(w.at[pl.ds(row, part)], pieces[s - 1], sem.at[2 * away + s - 1]))
    run(copies)


def gather_maps(n_dp, table, own, gots, wide):
    rank = own.shape[1]
    wide[:rank, :] = own[wanted_site(table, n_dp, 0)]
    for s in range(1, n_dp):
        wide[s * rank:(s + 1) * rank, :] = gots[s - 1][...]


def reduce_kernel(n_dp, owner, table, act, _, own, *refs):
    gots, out, wide = refs[:n_dp - 1], refs[n_dp - 1], refs[n_dp]
    rank = own.shape[1]
    blocks = owner.shape[0]
    rows = act.shape[0] // blocks
    gather_maps(n_dp, table, own, gots, wide)
    full = nt(act[...], wide[...])
    lane_slot = lax.broadcasted_iota(jnp.int32, (rows, n_dp * rank), 1) // rank
    folded = []
    for b in range(blocks):
        kept = jnp.where(lane_slot == slot_of(owner, b, n_dp), full[b * rows:(b + 1) * rows], 0.0)
        total = kept[:, :rank]
        for s in range(1, n_dp):
            total = total + kept[:, s * rank:(s + 1) * rank]
        folded.append(total)
    for j in range(blocks // 2):
        pair = jnp.concatenate([folded[2 * j], folded[2 * j + 1]], axis=1)
        out[j * rows:(j + 1) * rows, :] = pair.astype(BF16)


def grad_kernel(n_dp, n_part, n_behind, owner, act, *refs):
    refs = refs[n_behind:]
    parts, grads, wide = refs[:n_part], refs[n_part:n_part + n_dp], refs[n_part + n_dp]
    rank = wide.shape[1] // n_dp
    blocks = owner.shape[0]
    rows = act.shape[0] // blocks
    total = parts[0][...].astype(F32)
    for part in parts[1:]:
        total = total + part[...].astype(F32)
    lane_slot = lax.broadcasted_iota(jnp.int32, (rows, n_dp * rank), 1) // rank
    for b in range(blocks):
        one = total[(b // 2) * rows:(b // 2 + 1) * rows, (b % 2) * rank:(b % 2 + 1) * rank]
        spread = jnp.concatenate([one] * n_dp, axis=1)
        kept = jnp.where(lane_slot == slot_of(owner, b, n_dp), spread, 0.0)
        wide[b * rows:(b + 1) * rows, :] = kept.astype(BF16)
    full = tn(wide[...], act[...])
    for s in range(n_dp):
        grads[s][...] = full[s * rank:(s + 1) * rank].astype(BF16)


def send_kernel(n_pair, feat, n_mp, _, __, x, *refs):
    n_other = n_mp - 1
    pieces, outs, rows = refs[:n_other * n_pair], refs[n_other * n_pair:n_other * n_pair + n_other], refs[-n_other:]
    part = feat // n_pair

    @pl.when(pl.program_id(0) == 0)
    def _():
        for s in range(n_other):
            for q in range(n_pair):
                at = lax.rem(lax.axis_index("pair") + n_pair - q, n_pair) * part
                rows[s][pl.ds(pl.multiple_of(at, part), part), :] = pieces[s * n_pair + q][...]

    for s in range(n_other):
        outs[s][...] = nn(x[...], rows[s][...]).astype(BF16)


def back_kernel(n_dp, n_mp, table, *refs):
    w, gys, rows, wide, own_down, downs, out, picks, own, maps = (
        refs[0], refs[1:1 + n_mp], refs[1 + n_mp:2 * n_mp], refs[2 * n_mp], refs[2 * n_mp + 1],
        refs[2 * n_mp + 2:-4], refs[-4], refs[-3], refs[-2], refs[-1],
    )
    feat = out.shape[1]

    @pl.when(pl.program_id(0) == 0)
    def _():
        row = lax.broadcasted_iota(jnp.int32, picks.shape, 0)
        sites = jnp.zeros(picks.shape, jnp.int32)
        for s in range(n_dp):
            sites = jnp.where(row == s, wanted_site(table, n_dp, s), sites)
        picks[...] = sites
        own[...] = w[pl.ds(pl.multiple_of(lax.axis_index("mp") * feat, feat), feat), :]
        gather_maps(n_dp, table, own_down, downs, maps)

    total = nt(gys[0][...], own[...]) + SCALE * nn(wide[...], maps[...])
    for gy, row in zip(gys[1:], rows):
        total = total + nt(gy[...], row[...])
    out[...] = total.astype(BF16)


def own_kernel(n_dp, table, w, x, wide, own_up, *refs):
    ups, out, maps = refs[:n_dp - 1], refs[n_dp - 1], refs[n_dp]
    feat = x.shape[1]

    @pl.when(pl.program_id(0) == 0)
    def _():
        gather_maps(n_dp, table, own_up, ups, maps)

    own = w[pl.ds(pl.multiple_of(lax.axis_index("mp") * feat, feat), feat), :]
    out[...] = nn(x[...], own) + SCALE * nn(wide[...], maps[...])


def add_kernel(*refs):
    total = refs[0][...]
    for ref in refs[1:-1]:
        total = total + ref[...].astype(F32)
    refs[-1][...] = total.astype(BF16)


def site_kernel(n_dp, feat, picks, _, *refs):
    downs, ups, out = refs[:n_dp], refs[n_dp:2 * n_dp], refs[-1]
    for site in range(out.shape[0]):
        for grads, lo, hi in ((downs, 0, feat), (ups, feat, out.shape[2])):
            total = jnp.zeros((out.shape[1], hi - lo), F32)
            for s in range(n_dp):
                use = picks[s:s + 1, :1] == site
                total = total + jnp.where(use, grads[s][...].astype(F32), 0.0)
            out[site, :, lo:hi] = total.astype(BF16)


def last_kernel(feat, *refs):
    parts, down, up = refs[:-2], refs[-2], refs[-1]
    total = parts[0][...].astype(F32)
    for part in parts[1:]:
        total = total + part[...].astype(F32)
    total = SCALE * total
    down[...] = total[:, :, :feat]
    up[...] = total[:, :, feat:]


def shards(x, w, down, up, gy, owner, table):
    tok, feat = x.shape
    cols = w.shape[1]
    sites, rank = up.shape[:2]
    n_dp, n_mp, n_pair = (lax.axis_size(a) for a in ("dp", "mp", "pair"))
    n_other = n_mp - 1
    down = down.transpose(0, 2, 1)
    part = feat // n_pair
    tile = tok // TILES
    row_block = lambda width: pl.BlockSpec((tile, width), lambda i: (i, 0))
    whole = lambda *dims: pl.BlockSpec(dims, lambda i: (0,) * len(dims))

    away = n_dp - 1
    packed = call(
        functools.partial(pack_kernel, n_dp, n_mp, n_pair), "pack",
        [shape(rank, cols)] * away + [shape(rank, feat)] * away + [shape(part, cols)] * n_other,
        [SMEM, ANY, ANY, ANY], [VMEM] * (2 * away + n_other),
        [pltpu.SemaphoreType.DMA((2 * away + n_other,))], mib=60,
    )(table, down, up, w)
    pieces = [shift(packed[2 * away + s - 1], "mp", s) for s in range(1, n_mp)]
    ups = [shift(packed[s - 1], "dp", s) for s in range(1, n_dp)]
    downs = [shift(after(packed[away + s - 1], ups[1 % away]), "dp", s) for s in range(1, n_dp)]

    def low_rank(act, own, maps, behind, name):
        mine = call(
            functools.partial(reduce_kernel, n_dp), name + "_part",
            shape(tok // 2, 2 * rank), [SMEM, SMEM, VMEM, ANY] + [VMEM] * n_dp, VMEM,
            [pltpu.VMEM((n_dp * rank, act.shape[1]), BF16)],
        )(owner, table, act, behind, own, *maps)
        return [mine] + [shift(mine, "mp", s) for s in range(1, n_mp)]

    def gradient(act, parts, behind, name, flops):
        *grads, wide = call(
            functools.partial(grad_kernel, n_dp, n_mp, len(behind)), name + "_grad",
            [shape(rank, act.shape[1])] * n_dp + [shape(tok, n_dp * rank)],
            [SMEM, VMEM] + [ANY] * len(behind) + [VMEM] * n_mp, [VMEM] * (n_dp + 1), flops=flops,
        )(owner, act, *behind, *parts)
        return [grads[0]] + [shift(grads[s], "dp", n_dp - s) for s in range(1, n_dp)], wide

    h_parts = low_rank(gy, up, ups, ups[0], "h")
    gy_got = [shift(after(gy, *pieces), "mp", s) for s in range(1, n_mp)]
    down_back, h_wide = gradient(x, h_parts, downs, "down", GRAD_COST)
    u_parts = low_rank(x, down, downs, h_wide, "u")

    parts = []
    for piece in pieces:
        parts += [piece] + [shift(after(piece, h_wide), "pair", q) for q in range(1, n_pair)]
    sent = call(
        functools.partial(send_kernel, n_pair, feat, n_mp), "y_send",
        [shape(tok, cols)] * n_other + [shape(feat, cols)] * n_other,
        [ANY, ANY, row_block(feat)] + [whole(part, cols)] * len(parts),
        [row_block(cols)] * n_other + [whole(feat, cols)] * n_other,
        grid=(TILES,),
    )(u_parts[0], down_back[1], x, *parts)
    w_rows = sent[n_other:]
    y_got = [shift(sent[s - 1], "mp", n_mp - s) for s in range(1, n_mp)]
    back, picks = call(
        functools.partial(back_kernel, n_dp, n_mp), "back",
        [shape(tok, feat), shape(-(-n_dp // 8) * 8, 128, dtype=jnp.int32)],
        [SMEM, whole(*w.shape)] + [row_block(cols)] * n_mp + [whole(feat, cols)] * n_other
        + [row_block(n_dp * rank), whole(*down.shape)] + [whole(rank, feat)] * away,
        [row_block(feat), whole(-(-n_dp // 8) * 8, 128)],
        [pltpu.VMEM((feat, cols), BF16), pltpu.VMEM((n_dp * rank, feat), BF16)], grid=(TILES,),
    )(table, w, gy, *gy_got, *w_rows, h_wide, down, *downs)
    up_back, u_wide = gradient(gy, u_parts, [picks] + down_back[2:] + gy_got, "up", GRAD_COST)

    y_own = call(
        functools.partial(own_kernel, n_dp), "y_own", shape(tok, cols, dtype=F32),
        [SMEM, whole(*w.shape), row_block(feat), row_block(n_dp * rank), whole(*up.shape)]
        + [whole(rank, cols)] * away,
        row_block(cols), [pltpu.VMEM((n_dp * rank, cols), BF16)], grid=(TILES,),
    )(table, w, x, u_wide, up, *ups)

    summed = call(
        functools.partial(site_kernel, n_dp, feat), "sites",
        shape(sites, rank, feat + cols), [VMEM, ANY] + [VMEM] * (2 * n_dp), VMEM,
    )(picks, y_own, *down_back, *up_back)
    both = [summed] + [shift(summed, "pair", q) for q in range(1, n_pair)]
    down_grad, up_grad = call(
        functools.partial(last_kernel, feat), "gradients",
        [shape(sites, rank, feat, dtype=F32), shape(sites, rank, cols, dtype=F32)],
        [VMEM] * n_pair, [VMEM] * 2,
    )(*both)

    y = call(
        add_kernel, "y_add", shape(tok, cols), [row_block(cols)] * n_mp, row_block(cols), grid=(TILES,),
    )(y_own, *y_got)
    return y, back, down_grad.transpose(0, 2, 1), up_grad


def solution(mesh):
    rows = P(("groups", "dp", "pair"), "mp")
    in_specs = (
        rows,
        P(None, "mp"),
        P(("groups", "dp"), "mp", None),
        P(("groups", "dp"), None, "mp"),
        rows,
        P(("groups", "dp", "pair")),
        P(("groups", "dp"), None, None),
    )
    out_specs = (rows, rows, P(("groups", "dp"), "mp", None), P(("groups", "dp"), None, "mp"))
    return jax.shard_map(shards, mesh=mesh, in_specs=in_specs, out_specs=out_specs, check_vma=False)
```

```python
import functools

import jax
import jax.numpy as jnp
from jax import lax
from jax.experimental import pallas as pl
from jax.experimental.pallas import tpu as pltpu
from jax.sharding import PartitionSpec as P

SCALE = 2.0
TILES = 3
GRAD_COST = 15_000_000_000
F32 = jnp.float32
BF16 = jnp.bfloat16
SMEM = pl.BlockSpec(memory_space=pltpu.SMEM)
VMEM = pl.BlockSpec(memory_space=pltpu.VMEM)
ANY = pl.BlockSpec(memory_space=pl.ANY)


def shape(*dims, dtype=BF16):
    return jax.ShapeDtypeStruct(dims, dtype)


def call(kernel, name, out_shape, in_specs, out_specs, scratch=(), grid=(), mib=32, flops=1):
    return pl.pallas_call(
        kernel, name=name, out_shape=out_shape, grid=grid, in_specs=in_specs, out_specs=out_specs,
        scratch_shapes=scratch,
        compiler_params=pltpu.CompilerParams(vmem_limit_bytes=mib * 1024 * 1024),
        cost_estimate=pl.CostEstimate(flops=flops, bytes_accessed=1, transcendentals=0),
    )


def shift(value, axis, by):
    size = lax.axis_size(axis)
    return lax.ppermute(value, axis, [(i, (i + by) % size) for i in range(size)])


def after(value, *others):
    return lax.optimization_barrier((value, *others))[0]


def nn(a, b):
    return lax.dot_general(a, b, (((1,), (0,)), ((), ())), preferred_element_type=F32)


def nt(a, b):
    return lax.dot_general(a, b, (((1,), (1,)), ((), ())), preferred_element_type=F32)


def tn(a, b):
    return lax.dot_general(a, b, (((0,), (0,)), ((), ())), preferred_element_type=F32)


def run(copies):
    for copy in copies:
        copy.start()
    for copy in copies:
        copy.wait()


def wanted_site(table, n_dp, s, q=0):
    n_pair = lax.axis_size("pair")
    core = lax.rem(lax.axis_index("pair") + n_pair - q, n_pair)
    return table[0, core, lax.rem(lax.axis_index("dp") + s, n_dp)]


def slot_of(owner, b, n_dp):
    return lax.rem(lax.axis_index("dp") - owner[b] + n_dp, n_dp)


def pack_kernel(n_dp, n_mp, n_pair, table, down, up, w, *refs):
    away = n_dp - 1
    ups, downs, pieces, sem = refs[:away], refs[away:2 * away], refs[2 * away:-1], refs[-1]
    feat = w.shape[0] // n_mp
    part = feat // n_pair
    copies = []
    for s in range(away):
        site = wanted_site(table, n_dp, s + 1)
        copies.append(pltpu.make_async_copy(up.at[site], ups[s], sem.at[s]))
        copies.append(pltpu.make_async_copy(down.at[site], downs[s], sem.at[away + s]))
    for s in range(1, n_mp):
        row = lax.rem(lax.axis_index("mp") + s, n_mp) * feat + lax.axis_index("pair") * part
        row = pl.multiple_of(row, part)
        copies.append(pltpu.make_async_copy(w.at[pl.ds(row, part)], pieces[s - 1], sem.at[2 * away + s - 1]))
    run(copies)


def gather_maps(n_dp, table, own, gots, wide):
    rank = own.shape[1]
    wide[:rank, :] = own[wanted_site(table, n_dp, 0)]
    for s in range(1, n_dp):
        wide[s * rank:(s + 1) * rank, :] = gots[s - 1][...]


def reduce_kernel(n_dp, owner, table, act, _, own, *refs):
    gots, out, wide = refs[:n_dp - 1], refs[n_dp - 1], refs[n_dp]
    rank = own.shape[1]
    blocks = owner.shape[0]
    rows = act.shape[0] // blocks
    gather_maps(n_dp, table, own, gots, wide)
    full = nt(act[...], wide[...])
    lane_slot = lax.broadcasted_iota(jnp.int32, (rows, n_dp * rank), 1) // rank
    folded = []
    for b in range(blocks):
        kept = jnp.where(lane_slot == slot_of(owner, b, n_dp), full[b * rows:(b + 1) * rows], 0.0)
        total = kept[:, :rank]
        for s in range(1, n_dp):
            total = total + kept[:, s * rank:(s + 1) * rank]
        folded.append(total)
    for j in range(blocks // 2):
        pair = jnp.concatenate([folded[2 * j], folded[2 * j + 1]], axis=1)
        out[j * rows:(j + 1) * rows, :] = pair.astype(BF16)


def grad_kernel(n_dp, n_part, n_behind, owner, act, *refs):
    refs = refs[n_behind:]
    parts, grads, wide = refs[:n_part], refs[n_part:n_part + n_dp], refs[n_part + n_dp]
    rank = wide.shape[1] // n_dp
    blocks = owner.shape[0]
    rows = act.shape[0] // blocks
    total = parts[0][...].astype(F32)
    for part in parts[1:]:
        total = total + part[...].astype(F32)
    lane_slot = lax.broadcasted_iota(jnp.int32, (rows, n_dp * rank), 1) // rank
    for b in range(blocks):
        one = total[(b // 2) * rows:(b // 2 + 1) * rows, (b % 2) * rank:(b % 2 + 1) * rank]
        spread = jnp.concatenate([one] * n_dp, axis=1)
        kept = jnp.where(lane_slot == slot_of(owner, b, n_dp), spread, 0.0)
        wide[b * rows:(b + 1) * rows, :] = kept.astype(BF16)
    full = tn(wide[...], act[...])
    for s in range(n_dp):
        grads[s][...] = full[s * rank:(s + 1) * rank].astype(BF16)


def send_kernel(n_pair, feat, n_mp, _, __, x, *refs):
    n_other = n_mp - 1
    pieces, outs, rows = refs[:n_other * n_pair], refs[n_other * n_pair:n_other * n_pair + n_other], refs[-n_other:]
    part = feat // n_pair

    @pl.when(pl.program_id(0) == 0)
    def _():
        for s in range(n_other):
            for q in range(n_pair):
                at = lax.rem(lax.axis_index("pair") + n_pair - q, n_pair) * part
                rows[s][pl.ds(pl.multiple_of(at, part), part), :] = pieces[s * n_pair + q][...]

    for s in range(n_other):
        outs[s][...] = nn(x[...], rows[s][...]).astype(BF16)


def back_kernel(n_dp, n_mp, table, *refs):
    w, gys, rows, wide, own_down, downs, out, picks, own, maps = (
        refs[0], refs[1:1 + n_mp], refs[1 + n_mp:2 * n_mp], refs[2 * n_mp], refs[2 * n_mp + 1],
        refs[2 * n_mp + 2:-4], refs[-4], refs[-3], refs[-2], refs[-1],
    )
    feat = out.shape[1]

    @pl.when(pl.program_id(0) == 0)
    def _():
        row = lax.broadcasted_iota(jnp.int32, picks.shape, 0)
        sites = jnp.zeros(picks.shape, jnp.int32)
        for k in range(n_dp * lax.axis_size("pair")):
            sites = jnp.where(row == k, wanted_site(table, n_dp, k % n_dp, k // n_dp), sites)
        picks[...] = sites
        own[...] = w[pl.ds(pl.multiple_of(lax.axis_index("mp") * feat, feat), feat), :]
        gather_maps(n_dp, table, own_down, downs, maps)

    total = nt(gys[0][...], own[...]) + SCALE * nn(wide[...], maps[...])
    for gy, row in zip(gys[1:], rows):
        total = total + nt(gy[...], row[...])
    out[...] = total.astype(BF16)


def own_kernel(n_dp, table, w, x, wide, own_up, *refs):
    ups, out, maps = refs[:n_dp - 1], refs[n_dp - 1], refs[n_dp]
    feat = x.shape[1]

    @pl.when(pl.program_id(0) == 0)
    def _():
        gather_maps(n_dp, table, own_up, ups, maps)

    own = w[pl.ds(pl.multiple_of(lax.axis_index("mp") * feat, feat), feat), :]
    out[...] = nn(x[...], own) + SCALE * nn(wide[...], maps[...])


def pick_sum(grads, picks, site):
    total = jnp.zeros(grads[0].shape, F32)
    for k, grad in enumerate(grads):
        total = total + jnp.where(picks[k:k + 1, :1] == site, grad[...].astype(F32), 0.0)
    return total


def site_kernel(picks, _, *refs):
    grads, out = refs[:-1], refs[-1]
    for site in range(out.shape[0]):
        out[site] = pick_sum(grads, picks, site).astype(BF16)


def last_kernel(n_pair, n_ups, n_mp, picks, *refs):
    downs, ups, parts = refs[:n_pair], refs[n_pair:n_pair + n_ups], refs[n_pair + n_ups:n_pair + n_ups + n_mp]
    down, up, y = refs[-3:]
    total = downs[0][0].astype(F32)
    for part in downs[1:]:
        total = total + part[0].astype(F32)
    down[0] = SCALE * total
    up[0] = SCALE * pick_sum(ups, picks, pl.program_id(0))
    total = parts[0][...]
    for part in parts[1:]:
        total = total + part[...].astype(F32)
    y[...] = total.astype(BF16)


def shards(x, w, down, up, gy, owner, table):
    tok, feat = x.shape
    cols = w.shape[1]
    sites, rank = up.shape[:2]
    n_dp, n_mp, n_pair = (lax.axis_size(a) for a in ("dp", "mp", "pair"))
    n_other = n_mp - 1
    down = down.transpose(0, 2, 1)
    part = feat // n_pair
    tile = tok // TILES
    row_block = lambda width: pl.BlockSpec((tile, width), lambda i: (i, 0))
    whole = lambda *dims: pl.BlockSpec(dims, lambda i: (0,) * len(dims))

    away = n_dp - 1
    packed = call(
        functools.partial(pack_kernel, n_dp, n_mp, n_pair), "pack",
        [shape(rank, cols)] * away + [shape(rank, feat)] * away + [shape(part, cols)] * n_other,
        [SMEM, ANY, ANY, ANY], [VMEM] * (2 * away + n_other),
        [pltpu.SemaphoreType.DMA((2 * away + n_other,))], mib=60,
    )(table, down, up, w)
    pieces = [shift(packed[2 * away + s - 1], "mp", s) for s in range(1, n_mp)]
    ups = [shift(packed[s - 1], "dp", s) for s in range(1, n_dp)]
    downs = [shift(after(packed[away + s - 1], ups[1 % away]), "dp", s) for s in range(1, n_dp)]

    def low_rank(act, own, maps, behind, name):
        mine = call(
            functools.partial(reduce_kernel, n_dp), name + "_part",
            shape(tok // 2, 2 * rank), [SMEM, SMEM, VMEM, ANY] + [VMEM] * n_dp, VMEM,
            [pltpu.VMEM((n_dp * rank, act.shape[1]), BF16)],
        )(owner, table, act, behind, own, *maps)
        return [mine] + [shift(mine, "mp", s) for s in range(1, n_mp)]

    def gradient(act, parts, behind, name, flops):
        *grads, wide = call(
            functools.partial(grad_kernel, n_dp, n_mp, len(behind)), name + "_grad",
            [shape(rank, act.shape[1])] * n_dp + [shape(tok, n_dp * rank)],
            [SMEM, VMEM] + [ANY] * len(behind) + [VMEM] * n_mp, [VMEM] * (n_dp + 1), flops=flops,
        )(owner, act, *behind, *parts)
        return [grads[0]] + [shift(grads[s], "dp", n_dp - s) for s in range(1, n_dp)], wide

    h_parts = low_rank(gy, up, ups, ups[0], "h")
    gy_got = [shift(after(gy, *pieces), "mp", s) for s in range(1, n_mp)]
    down_back, h_wide = gradient(x, h_parts, downs, "down", GRAD_COST)
    u_parts = low_rank(x, down, downs, h_wide, "u")

    parts = []
    for piece in pieces:
        parts += [piece] + [shift(after(piece, h_wide), "pair", q) for q in range(1, n_pair)]
    sent = call(
        functools.partial(send_kernel, n_pair, feat, n_mp), "y_send",
        [shape(tok, cols)] * n_other + [shape(feat, cols)] * n_other,
        [ANY, ANY, row_block(feat)] + [whole(part, cols)] * len(parts),
        [row_block(cols)] * n_other + [whole(feat, cols)] * n_other,
        grid=(TILES,),
    )(u_parts[0], down_back[1], x, *parts)
    w_rows = sent[n_other:]
    y_got = [shift(sent[s - 1], "mp", n_mp - s) for s in range(1, n_mp)]
    back, picks = call(
        functools.partial(back_kernel, n_dp, n_mp), "back",
        [shape(tok, feat), shape(-(-n_dp * n_pair // 8) * 8, 128, dtype=jnp.int32)],
        [SMEM, whole(*w.shape)] + [row_block(cols)] * n_mp + [whole(feat, cols)] * n_other
        + [row_block(n_dp * rank), whole(*down.shape)] + [whole(rank, feat)] * away,
        [row_block(feat), whole(-(-n_dp * n_pair // 8) * 8, 128)],
        [pltpu.VMEM((feat, cols), BF16), pltpu.VMEM((n_dp * rank, feat), BF16)], grid=(TILES,),
    )(table, w, gy, *gy_got, *w_rows, h_wide, down, *downs)
    up_back, u_wide = gradient(gy, u_parts, [picks] + down_back[2:] + gy_got, "up", GRAD_COST)

    y_own = call(
        functools.partial(own_kernel, n_dp), "y_own", shape(tok, cols, dtype=F32),
        [SMEM, whole(*w.shape), row_block(feat), row_block(n_dp * rank), whole(*up.shape)]
        + [whole(rank, cols)] * away,
        row_block(cols), [pltpu.VMEM((n_dp * rank, cols), BF16)], grid=(TILES,), flops=GRAD_COST,
    )(table, w, x, u_wide, up, *ups)

    summed = call(
        site_kernel, "sites", shape(sites, rank, feat), [VMEM, ANY] + [VMEM] * n_dp, VMEM,
    )(picks, up_back[0], *down_back)
    both = [summed] + [shift(summed, "pair", q) for q in range(1, n_pair)]
    up_all = [shift(after(one, y_own), "pair", q) if q else one for q in range(n_pair) for one in up_back]
    rows = tok // sites
    of_site = lambda width: pl.BlockSpec((1, rank, width), lambda i: (i, 0, 0))
    out_rows = pl.BlockSpec((rows, cols), lambda i: (i, 0))
    down_grad, up_grad, y = call(
        functools.partial(last_kernel, n_pair, n_pair * n_dp, n_mp), "last",
        [shape(sites, rank, feat, dtype=F32), shape(sites, rank, cols, dtype=F32), shape(tok, cols)],
        [whole(*picks.shape)] + [of_site(feat)] * n_pair + [whole(rank, cols)] * (n_pair * n_dp) + [out_rows] * n_mp,
        [of_site(feat), of_site(cols), out_rows], grid=(sites,),
    )(picks, *both, *up_all, y_own, *y_got)
    return y, back, down_grad.transpose(0, 2, 1), up_grad


def solution(mesh):
    rows = P(("groups", "dp", "pair"), "mp")
    in_specs = (
        rows,
        P(None, "mp"),
        P(("groups", "dp"), "mp", None),
        P(("groups", "dp"), None, "mp"),
        rows,
        P(("groups", "dp", "pair")),
        P(("groups", "dp"), None, None),
    )
    out_specs = (rows, rows, P(("groups", "dp"), "mp", None), P(("groups", "dp"), None, "mp"))
    return jax.shard_map(shards, mesh=mesh, in_specs=in_specs, out_specs=out_specs, check_vma=False)
```

```python
import functools

import jax
import jax.numpy as jnp
from jax import lax
from jax.experimental import pallas as pl
from jax.experimental.pallas import tpu as pltpu
from jax.sharding import PartitionSpec as P

SCALE = 2.0
TILES = 3
GRAD_COST = 15_000_000_000
F32 = jnp.float32
BF16 = jnp.bfloat16
SMEM = pl.BlockSpec(memory_space=pltpu.SMEM)
VMEM = pl.BlockSpec(memory_space=pltpu.VMEM)
ANY = pl.BlockSpec(memory_space=pl.ANY)


def shape(*dims, dtype=BF16):
    return jax.ShapeDtypeStruct(dims, dtype)


def call(kernel, name, out_shape, in_specs, out_specs, scratch=(), grid=(), mib=32, flops=1):
    return pl.pallas_call(
        kernel, name=name, out_shape=out_shape, grid=grid, in_specs=in_specs, out_specs=out_specs,
        scratch_shapes=scratch,
        compiler_params=pltpu.CompilerParams(vmem_limit_bytes=mib * 1024 * 1024),
        cost_estimate=pl.CostEstimate(flops=flops, bytes_accessed=1, transcendentals=0),
    )


def shift(value, axis, by):
    size = lax.axis_size(axis)
    return lax.ppermute(value, axis, [(i, (i + by) % size) for i in range(size)])


def swap(value, axis, mask):
    return lax.ppermute(value, axis, [(i, i ^ mask) for i in range(lax.axis_size(axis))])


def after(value, *others):
    return lax.optimization_barrier((value, *others))[0]


def nn(a, b):
    return lax.dot_general(a, b, (((1,), (0,)), ((), ())), preferred_element_type=F32)


def nt(a, b):
    return lax.dot_general(a, b, (((1,), (1,)), ((), ())), preferred_element_type=F32)


def tn(a, b):
    return lax.dot_general(a, b, (((0,), (0,)), ((), ())), preferred_element_type=F32)


def run(copies):
    for copy in copies:
        copy.start()
    for copy in copies:
        copy.wait()


def wanted_site(table, n_dp, s, q=0):
    n_pair = lax.axis_size("pair")
    core = lax.rem(lax.axis_index("pair") + n_pair - q, n_pair)
    return table[0, core, lax.bitwise_xor(lax.axis_index("dp"), s)]


def slot_of(owner, b, n_dp):
    return lax.bitwise_xor(lax.axis_index("dp"), owner[b])


def pack_kernel(n_dp, n_mp, n_pair, table, down, up, w, *refs):
    away = n_dp - 1
    ups, downs, pieces, sem = refs[:away], refs[away:2 * away], refs[2 * away:-1], refs[-1]
    feat = w.shape[0] // n_mp
    part = feat // n_pair
    copies = []
    for s in range(away):
        site = wanted_site(table, n_dp, s + 1)
        copies.append(pltpu.make_async_copy(up.at[site], ups[s], sem.at[s]))
        copies.append(pltpu.make_async_copy(down.at[site], downs[s], sem.at[away + s]))
    for s in range(1, n_mp):
        row = lax.rem(lax.axis_index("mp") + s, n_mp) * feat + lax.axis_index("pair") * part
        row = pl.multiple_of(row, part)
        copies.append(pltpu.make_async_copy(w.at[pl.ds(row, part)], pieces[s - 1], sem.at[2 * away + s - 1]))
    run(copies)


def gather_maps(n_dp, table, own, gots, wide):
    rank = own.shape[1]
    wide[:rank, :] = own[wanted_site(table, n_dp, 0)]
    for s in range(1, n_dp):
        wide[s * rank:(s + 1) * rank, :] = gots[s - 1][...]


def reduce_kernel(n_dp, owner, table, act, _, own, *refs):
    gots, out, wide = refs[:n_dp - 1], refs[n_dp - 1], refs[n_dp]
    rank = own.shape[1]
    blocks = owner.shape[0]
    rows = act.shape[0] // blocks
    gather_maps(n_dp, table, own, gots, wide)
    full = nt(act[...], wide[...])
    lane_slot = lax.broadcasted_iota(jnp.int32, (rows, n_dp * rank), 1) // rank
    folded = []
    for b in range(blocks):
        kept = jnp.where(lane_slot == slot_of(owner, b, n_dp), full[b * rows:(b + 1) * rows], 0.0)
        total = kept[:, :rank]
        for s in range(1, n_dp):
            total = total + kept[:, s * rank:(s + 1) * rank]
        folded.append(total)
    for j in range(blocks // 2):
        pair = jnp.concatenate([folded[2 * j], folded[2 * j + 1]], axis=1)
        out[j * rows:(j + 1) * rows, :] = pair.astype(BF16)


def grad_kernel(n_dp, n_part, n_behind, owner, act, *refs):
    refs = refs[n_behind:]
    parts, grads, wide = refs[:n_part], refs[n_part:n_part + n_dp], refs[n_part + n_dp]
    rank = wide.shape[1] // n_dp
    blocks = owner.shape[0]
    rows = act.shape[0] // blocks
    total = parts[0][...].astype(F32)
    for part in parts[1:]:
        total = total + part[...].astype(F32)
    lane_slot = lax.broadcasted_iota(jnp.int32, (rows, n_dp * rank), 1) // rank
    for b in range(blocks):
        one = total[(b // 2) * rows:(b // 2 + 1) * rows, (b % 2) * rank:(b % 2 + 1) * rank]
        spread = jnp.concatenate([one] * n_dp, axis=1)
        kept = jnp.where(lane_slot == slot_of(owner, b, n_dp), spread, 0.0)
        wide[b * rows:(b + 1) * rows, :] = kept.astype(BF16)
    full = tn(wide[...], act[...])
    for s in range(n_dp):
        grads[s][...] = full[s * rank:(s + 1) * rank].astype(BF16)


def send_kernel(n_pair, feat, n_mp, _, __, x, *refs):
    n_other = n_mp - 1
    pieces, outs, rows = refs[:n_other * n_pair], refs[n_other * n_pair:n_other * n_pair + n_other], refs[-n_other:]
    part = feat // n_pair

    @pl.when(pl.program_id(0) == 0)
    def _():
        for s in range(n_other):
            for q in range(n_pair):
                at = lax.rem(lax.axis_index("pair") + n_pair - q, n_pair) * part
                rows[s][pl.ds(pl.multiple_of(at, part), part), :] = pieces[s * n_pair + q][...]

    for s in range(n_other):
        outs[s][...] = nn(x[...], rows[s][...]).astype(BF16)


def back_kernel(n_dp, n_mp, table, *refs):
    w, gys, rows, wide, own_down, downs, out, picks, own, maps = (
        refs[0], refs[1:1 + n_mp], refs[1 + n_mp:2 * n_mp], refs[2 * n_mp], refs[2 * n_mp + 1],
        refs[2 * n_mp + 2:-4], refs[-4], refs[-3], refs[-2], refs[-1],
    )
    feat = out.shape[1]

    @pl.when(pl.program_id(0) == 0)
    def _():
        row = lax.broadcasted_iota(jnp.int32, picks.shape, 0)
        sites = jnp.zeros(picks.shape, jnp.int32)
        for k in range(n_dp * lax.axis_size("pair")):
            sites = jnp.where(row == k, wanted_site(table, n_dp, k % n_dp, k // n_dp), sites)
        picks[...] = sites
        own[...] = w[pl.ds(pl.multiple_of(lax.axis_index("mp") * feat, feat), feat), :]
        gather_maps(n_dp, table, own_down, downs, maps)

    total = nt(gys[0][...], own[...]) + SCALE * nn(wide[...], maps[...])
    for gy, row in zip(gys[1:], rows):
        total = total + nt(gy[...], row[...])
    out[...] = total.astype(BF16)


def own_kernel(n_dp, table, w, x, wide, own_up, *refs):
    ups, out, maps = refs[:n_dp - 1], refs[n_dp - 1], refs[n_dp]
    feat = x.shape[1]

    @pl.when(pl.program_id(0) == 0)
    def _():
        gather_maps(n_dp, table, own_up, ups, maps)

    own = w[pl.ds(pl.multiple_of(lax.axis_index("mp") * feat, feat), feat), :]
    out[...] = nn(x[...], own) + SCALE * nn(wide[...], maps[...])


def pick_sum(grads, picks, site):
    total = jnp.zeros(grads[0].shape, F32)
    for k, grad in enumerate(grads):
        total = total + jnp.where(picks[k:k + 1, :1] == site, grad[...].astype(F32), 0.0)
    return total


def site_kernel(picks, _, *refs):
    grads, out = refs[:-1], refs[-1]
    for site in range(out.shape[0]):
        out[site] = pick_sum(grads, picks, site).astype(BF16)


def last_kernel(n_pair, n_ups, n_mp, picks, *refs):
    downs, ups, parts = refs[:n_pair], refs[n_pair:n_pair + n_ups], refs[n_pair + n_ups:n_pair + n_ups + n_mp]
    down, up, y = refs[-3:]
    total = downs[0][0].astype(F32)
    for part in downs[1:]:
        total = total + part[0].astype(F32)
    down[0] = SCALE * total
    up[0] = SCALE * pick_sum(ups, picks, pl.program_id(0))
    total = parts[0][...]
    for part in parts[1:]:
        total = total + part[...].astype(F32)
    y[...] = total.astype(BF16)


def shards(x, w, down, up, gy, owner, table):
    tok, feat = x.shape
    cols = w.shape[1]
    sites, rank = up.shape[:2]
    n_dp, n_mp, n_pair = (lax.axis_size(a) for a in ("dp", "mp", "pair"))
    n_other = n_mp - 1
    down = down.transpose(0, 2, 1)
    part = feat // n_pair
    tile = tok // TILES
    row_block = lambda width: pl.BlockSpec((tile, width), lambda i: (i, 0))
    whole = lambda *dims: pl.BlockSpec(dims, lambda i: (0,) * len(dims))

    away = n_dp - 1
    packed = call(
        functools.partial(pack_kernel, n_dp, n_mp, n_pair), "pack",
        [shape(rank, cols)] * away + [shape(rank, feat)] * away + [shape(part, cols)] * n_other,
        [SMEM, ANY, ANY, ANY], [VMEM] * (2 * away + n_other),
        [pltpu.SemaphoreType.DMA((2 * away + n_other,))], mib=60,
    )(table, down, up, w)
    pieces = [shift(packed[2 * away + s - 1], "mp", s) for s in range(1, n_mp)]
    ups = [swap(packed[s - 1], "dp", s) for s in range(1, n_dp)]
    downs = [swap(after(packed[away + s - 1], ups[1 % away]), "dp", s) for s in range(1, n_dp)]

    def low_rank(act, own, maps, behind, name):
        mine = call(
            functools.partial(reduce_kernel, n_dp), name + "_part",
            shape(tok // 2, 2 * rank), [SMEM, SMEM, VMEM, ANY] + [VMEM] * n_dp, VMEM,
            [pltpu.VMEM((n_dp * rank, act.shape[1]), BF16)],
        )(owner, table, act, behind, own, *maps)
        return [mine] + [shift(mine, "mp", s) for s in range(1, n_mp)]

    def gradient(act, parts, behind, name, flops):
        *grads, wide = call(
            functools.partial(grad_kernel, n_dp, n_mp, len(behind)), name + "_grad",
            [shape(rank, act.shape[1])] * n_dp + [shape(tok, n_dp * rank)],
            [SMEM, VMEM] + [ANY] * len(behind) + [VMEM] * n_mp, [VMEM] * (n_dp + 1), flops=flops,
        )(owner, act, *behind, *parts)
        return [grads[0]] + [swap(grads[s], "dp", s) for s in range(1, n_dp)], wide

    h_parts = low_rank(gy, up, ups, ups[0], "h")
    gy_got = [shift(after(gy, *pieces), "mp", s) for s in range(1, n_mp)]
    down_back, h_wide = gradient(x, h_parts, downs, "down", GRAD_COST)
    u_parts = low_rank(x, down, downs, h_wide, "u")

    parts = []
    for piece in pieces:
        parts += [piece] + [shift(after(piece, h_wide), "pair", q) for q in range(1, n_pair)]
    sent = call(
        functools.partial(send_kernel, n_pair, feat, n_mp), "y_send",
        [shape(tok, cols)] * n_other + [shape(feat, cols)] * n_other,
        [ANY, ANY, row_block(feat)] + [whole(part, cols)] * len(parts),
        [row_block(cols)] * n_other + [whole(feat, cols)] * n_other,
        grid=(TILES,),
    )(u_parts[0], down_back[1], x, *parts)
    w_rows = sent[n_other:]
    y_got = [shift(sent[s - 1], "mp", n_mp - s) for s in range(1, n_mp)]
    back, picks = call(
        functools.partial(back_kernel, n_dp, n_mp), "back",
        [shape(tok, feat), shape(-(-n_dp * n_pair // 8) * 8, 128, dtype=jnp.int32)],
        [SMEM, whole(*w.shape)] + [row_block(cols)] * n_mp + [whole(feat, cols)] * n_other
        + [row_block(n_dp * rank), whole(*down.shape)] + [whole(rank, feat)] * away,
        [row_block(feat), whole(-(-n_dp * n_pair // 8) * 8, 128)],
        [pltpu.VMEM((feat, cols), BF16), pltpu.VMEM((n_dp * rank, feat), BF16)], grid=(TILES,),
    )(table, w, gy, *gy_got, *w_rows, h_wide, down, *downs)
    up_back, u_wide = gradient(gy, u_parts, [picks] + down_back[2:] + gy_got, "up", GRAD_COST)

    y_own = call(
        functools.partial(own_kernel, n_dp), "y_own", shape(tok, cols, dtype=F32),
        [SMEM, whole(*w.shape), row_block(feat), row_block(n_dp * rank), whole(*up.shape)]
        + [whole(rank, cols)] * away,
        row_block(cols), [pltpu.VMEM((n_dp * rank, cols), BF16)], grid=(TILES,), flops=GRAD_COST,
    )(table, w, x, u_wide, up, *ups)

    summed = call(
        site_kernel, "sites", shape(sites, rank, feat), [VMEM, ANY] + [VMEM] * n_dp, VMEM,
    )(picks, up_back[0], *down_back)
    both = [summed] + [shift(summed, "pair", q) for q in range(1, n_pair)]
    up_all = [shift(after(one, y_own), "pair", q) if q else one for q in range(n_pair) for one in up_back]
    rows = tok // sites
    of_site = lambda width: pl.BlockSpec((1, rank, width), lambda i: (i, 0, 0))
    out_rows = pl.BlockSpec((rows, cols), lambda i: (i, 0))
    down_grad, up_grad, y = call(
        functools.partial(last_kernel, n_pair, n_pair * n_dp, n_mp), "last",
        [shape(sites, rank, feat, dtype=F32), shape(sites, rank, cols, dtype=F32), shape(tok, cols)],
        [whole(*picks.shape)] + [of_site(feat)] * n_pair + [whole(rank, cols)] * (n_pair * n_dp) + [out_rows] * n_mp,
        [of_site(feat), of_site(cols), out_rows], grid=(sites,),
    )(picks, *both, *up_all, y_own, *y_got)
    return y, back, down_grad.transpose(0, 2, 1), up_grad


def solution(mesh):
    rows = P(("groups", "dp", "pair"), "mp")
    in_specs = (
        rows,
        P(None, "mp"),
        P(("groups", "dp"), "mp", None),
        P(("groups", "dp"), None, "mp"),
        rows,
        P(("groups", "dp", "pair")),
        P(("groups", "dp"), None, None),
    )
    out_specs = (rows, rows, P(("groups", "dp"), "mp", None), P(("groups", "dp"), None, "mp"))
    return jax.shard_map(shards, mesh=mesh, in_specs=in_specs, out_specs=out_specs, check_vma=False)
```

```python
import functools

import jax
import jax.numpy as jnp
from jax import lax
from jax.experimental import pallas as pl
from jax.experimental.pallas import tpu as pltpu
from jax.sharding import PartitionSpec as P

SCALE = 2.0
TILES = 3
GRAD_COST = 15_000_000_000
F32 = jnp.float32
BF16 = jnp.bfloat16
SMEM = pl.BlockSpec(memory_space=pltpu.SMEM)
VMEM = pl.BlockSpec(memory_space=pltpu.VMEM)
ANY = pl.BlockSpec(memory_space=pl.ANY)


def shape(*dims, dtype=BF16):
    return jax.ShapeDtypeStruct(dims, dtype)


def call(kernel, name, out_shape, in_specs, out_specs, scratch=(), grid=(), mib=32, flops=1):
    return pl.pallas_call(
        kernel, name=name, out_shape=out_shape, grid=grid, in_specs=in_specs, out_specs=out_specs,
        scratch_shapes=scratch,
        compiler_params=pltpu.CompilerParams(vmem_limit_bytes=mib * 1024 * 1024),
        cost_estimate=pl.CostEstimate(flops=flops, bytes_accessed=1, transcendentals=0),
    )


def shift(value, axis, by):
    size = lax.axis_size(axis)
    return lax.ppermute(value, axis, [(i, (i + by) % size) for i in range(size)])


def swap(value, axis, mask):
    return lax.ppermute(value, axis, [(i, i ^ mask) for i in range(lax.axis_size(axis))])


def after(value, *others):
    return lax.optimization_barrier((value, *others))[0]


def nn(a, b):
    return lax.dot_general(a, b, (((1,), (0,)), ((), ())), preferred_element_type=F32)


def nt(a, b):
    return lax.dot_general(a, b, (((1,), (1,)), ((), ())), preferred_element_type=F32)


def tn(a, b):
    return lax.dot_general(a, b, (((0,), (0,)), ((), ())), preferred_element_type=F32)


def run(copies):
    for copy in copies:
        copy.start()
    for copy in copies:
        copy.wait()


def wanted_site(table, n_dp, s, q=0):
    n_pair = lax.axis_size("pair")
    core = lax.rem(lax.axis_index("pair") + n_pair - q, n_pair)
    return table[0, core, lax.bitwise_xor(lax.axis_index("dp"), (n_dp - s) % n_dp)]


def slot_of(owner, b, n_dp):
    return lax.rem(n_dp - lax.bitwise_xor(lax.axis_index("dp"), owner[b]), n_dp)


def pack_kernel(n_dp, n_mp, n_pair, table, down, up, w, *refs):
    away = n_dp - 1
    ups, downs, pieces, sem = refs[:away], refs[away:2 * away], refs[2 * away:-1], refs[-1]
    feat = w.shape[0] // n_mp
    part = feat // n_pair
    copies = []
    for s in range(away):
        site = wanted_site(table, n_dp, s + 1)
        copies.append(pltpu.make_async_copy(up.at[site], ups[s], sem.at[s]))
        copies.append(pltpu.make_async_copy(down.at[site], downs[s], sem.at[away + s]))
    for s in range(1, n_mp):
        row = lax.rem(lax.axis_index("mp") + s, n_mp) * feat + lax.axis_index("pair") * part
        row = pl.multiple_of(row, part)
        copies.append(pltpu.make_async_copy(w.at[pl.ds(row, part)], pieces[s - 1], sem.at[2 * away + s - 1]))
    run(copies)


def gather_maps(n_dp, table, own, gots, wide):
    rank = own.shape[1]
    wide[:rank, :] = own[wanted_site(table, n_dp, 0)]
    for s in range(1, n_dp):
        wide[s * rank:(s + 1) * rank, :] = gots[s - 1][...]


def reduce_kernel(n_dp, owner, table, act, _, own, *refs):
    gots, out, wide = refs[:n_dp - 1], refs[n_dp - 1], refs[n_dp]
    rank = own.shape[1]
    blocks = owner.shape[0]
    rows = act.shape[0] // blocks
    gather_maps(n_dp, table, own, gots, wide)
    full = nt(act[...], wide[...])
    lane_slot = lax.broadcasted_iota(jnp.int32, (rows, n_dp * rank), 1) // rank
    folded = []
    for b in range(blocks):
        kept = jnp.where(lane_slot == slot_of(owner, b, n_dp), full[b * rows:(b + 1) * rows], 0.0)
        total = kept[:, :rank]
        for s in range(1, n_dp):
            total = total + kept[:, s * rank:(s + 1) * rank]
        folded.append(total)
    for j in range(blocks // 2):
        pair = jnp.concatenate([folded[2 * j], folded[2 * j + 1]], axis=1)
        out[j * rows:(j + 1) * rows, :] = pair.astype(BF16)


def grad_kernel(n_dp, n_part, n_behind, owner, act, *refs):
    refs = refs[n_behind:]
    parts, grads, wide = refs[:n_part], refs[n_part:n_part + n_dp], refs[n_part + n_dp]
    rank = wide.shape[1] // n_dp
    blocks = owner.shape[0]
    rows = act.shape[0] // blocks
    total = parts[0][...].astype(F32)
    for part in parts[1:]:
        total = total + part[...].astype(F32)
    lane_slot = lax.broadcasted_iota(jnp.int32, (rows, n_dp * rank), 1) // rank
    for b in range(blocks):
        one = total[(b // 2) * rows:(b // 2 + 1) * rows, (b % 2) * rank:(b % 2 + 1) * rank]
        spread = jnp.concatenate([one] * n_dp, axis=1)
        kept = jnp.where(lane_slot == slot_of(owner, b, n_dp), spread, 0.0)
        wide[b * rows:(b + 1) * rows, :] = kept.astype(BF16)
    full = tn(wide[...], act[...])
    for s in range(n_dp):
        grads[s][...] = full[s * rank:(s + 1) * rank].astype(BF16)


def send_kernel(n_pair, feat, n_mp, _, __, x, *refs):
    n_other = n_mp - 1
    pieces, outs, rows = refs[:n_other * n_pair], refs[n_other * n_pair:n_other * n_pair + n_other], refs[-n_other:]
    part = feat // n_pair

    @pl.when(pl.program_id(0) == 0)
    def _():
        for s in range(n_other):
            for q in range(n_pair):
                at = lax.rem(lax.axis_index("pair") + n_pair - q, n_pair) * part
                rows[s][pl.ds(pl.multiple_of(at, part), part), :] = pieces[s * n_pair + q][...]

    for s in range(n_other):
        outs[s][...] = nn(x[...], rows[s][...]).astype(BF16)


def back_kernel(n_dp, n_mp, table, *refs):
    w, gys, rows, wide, own_down, downs, out, picks, own, maps = (
        refs[0], refs[1:1 + n_mp], refs[1 + n_mp:2 * n_mp], refs[2 * n_mp], refs[2 * n_mp + 1],
        refs[2 * n_mp + 2:-4], refs[-4], refs[-3], refs[-2], refs[-1],
    )
    feat = out.shape[1]

    @pl.when(pl.program_id(0) == 0)
    def _():
        row = lax.broadcasted_iota(jnp.int32, picks.shape, 0)
        sites = jnp.zeros(picks.shape, jnp.int32)
        for k in range(n_dp * lax.axis_size("pair")):
            sites = jnp.where(row == k, wanted_site(table, n_dp, k % n_dp, k // n_dp), sites)
        picks[...] = sites
        own[...] = w[pl.ds(pl.multiple_of(lax.axis_index("mp") * feat, feat), feat), :]
        gather_maps(n_dp, table, own_down, downs, maps)

    total = nt(gys[0][...], own[...]) + SCALE * nn(wide[...], maps[...])
    for gy, row in zip(gys[1:], rows):
        total = total + nt(gy[...], row[...])
    out[...] = total.astype(BF16)


def own_kernel(n_dp, table, w, x, wide, own_up, *refs):
    ups, out, maps = refs[:n_dp - 1], refs[n_dp - 1], refs[n_dp]
    feat = x.shape[1]

    @pl.when(pl.program_id(0) == 0)
    def _():
        gather_maps(n_dp, table, own_up, ups, maps)

    own = w[pl.ds(pl.multiple_of(lax.axis_index("mp") * feat, feat), feat), :]
    out[...] = nn(x[...], own) + SCALE * nn(wide[...], maps[...])


def pick_sum(grads, picks, site):
    total = jnp.zeros(grads[0].shape, F32)
    for k, grad in enumerate(grads):
        total = total + jnp.where(picks[k:k + 1, :1] == site, grad[...].astype(F32), 0.0)
    return total


def site_kernel(picks, _, *refs):
    grads, out = refs[:-1], refs[-1]
    for site in range(out.shape[0]):
        out[site] = pick_sum(grads, picks, site).astype(BF16)


def last_kernel(n_pair, n_ups, n_mp, picks, *refs):
    downs, ups, parts = refs[:n_pair], refs[n_pair:n_pair + n_ups], refs[n_pair + n_ups:n_pair + n_ups + n_mp]
    down, up, y = refs[-3:]
    total = downs[0][0].astype(F32)
    for part in downs[1:]:
        total = total + part[0].astype(F32)
    down[0] = SCALE * total
    up[0] = SCALE * pick_sum(ups, picks, pl.program_id(0))
    total = parts[0][...]
    for part in parts[1:]:
        total = total + part[...].astype(F32)
    y[...] = total.astype(BF16)


def shards(x, w, down, up, gy, owner, table):
    tok, feat = x.shape
    cols = w.shape[1]
    sites, rank = up.shape[:2]
    n_dp, n_mp, n_pair = (lax.axis_size(a) for a in ("dp", "mp", "pair"))
    n_other = n_mp - 1
    down = down.transpose(0, 2, 1)
    part = feat // n_pair
    tile = tok // TILES
    row_block = lambda width: pl.BlockSpec((tile, width), lambda i: (i, 0))
    whole = lambda *dims: pl.BlockSpec(dims, lambda i: (0,) * len(dims))

    away = n_dp - 1
    packed = call(
        functools.partial(pack_kernel, n_dp, n_mp, n_pair), "pack",
        [shape(rank, cols)] * away + [shape(rank, feat)] * away + [shape(part, cols)] * n_other,
        [SMEM, ANY, ANY, ANY], [VMEM] * (2 * away + n_other),
        [pltpu.SemaphoreType.DMA((2 * away + n_other,))], mib=60,
    )(table, down, up, w)
    pieces = [shift(packed[2 * away + s - 1], "mp", s) for s in range(1, n_mp)]
    ups = [swap(packed[s - 1], "dp", n_dp - s) for s in range(1, n_dp)]
    downs = [swap(after(packed[away + s - 1], ups[0]), "dp", n_dp - s) for s in range(1, n_dp)]

    def low_rank(act, own, maps, behind, name):
        mine = call(
            functools.partial(reduce_kernel, n_dp), name + "_part",
            shape(tok // 2, 2 * rank), [SMEM, SMEM, VMEM, ANY] + [VMEM] * n_dp, VMEM,
            [pltpu.VMEM((n_dp * rank, act.shape[1]), BF16)],
        )(owner, table, act, behind, own, *maps)
        return [mine] + [shift(mine, "mp", s) for s in range(1, n_mp)]

    def gradient(act, parts, behind, name, flops):
        *grads, wide = call(
            functools.partial(grad_kernel, n_dp, n_mp, len(behind)), name + "_grad",
            [shape(rank, act.shape[1])] * n_dp + [shape(tok, n_dp * rank)],
            [SMEM, VMEM] + [ANY] * len(behind) + [VMEM] * n_mp, [VMEM] * (n_dp + 1), flops=flops,
        )(owner, act, *behind, *parts)
        return [grads[0]] + [swap(grads[s], "dp", n_dp - s) for s in range(1, n_dp)], wide

    h_parts = low_rank(gy, up, ups, ups[0], "h")
    gy_got = [shift(after(gy, *pieces), "mp", s) for s in range(1, n_mp)]
    down_back, h_wide = gradient(x, h_parts, downs, "down", GRAD_COST)
    u_parts = low_rank(x, down, downs, h_wide, "u")

    parts = []
    for piece in pieces:
        parts += [piece] + [shift(after(piece, h_wide), "pair", q) for q in range(1, n_pair)]
    sent = call(
        functools.partial(send_kernel, n_pair, feat, n_mp), "y_send",
        [shape(tok, cols)] * n_other + [shape(feat, cols)] * n_other,
        [ANY, ANY, row_block(feat)] + [whole(part, cols)] * len(parts),
        [row_block(cols)] * n_other + [whole(feat, cols)] * n_other,
        grid=(TILES,),
    )(u_parts[0], down_back[1], x, *parts)
    w_rows = sent[n_other:]
    y_got = [shift(sent[s - 1], "mp", n_mp - s) for s in range(1, n_mp)]
    back, picks = call(
        functools.partial(back_kernel, n_dp, n_mp), "back",
        [shape(tok, feat), shape(-(-n_dp * n_pair // 8) * 8, 128, dtype=jnp.int32)],
        [SMEM, whole(*w.shape)] + [row_block(cols)] * n_mp + [whole(feat, cols)] * n_other
        + [row_block(n_dp * rank), whole(*down.shape)] + [whole(rank, feat)] * away,
        [row_block(feat), whole(-(-n_dp * n_pair // 8) * 8, 128)],
        [pltpu.VMEM((feat, cols), BF16), pltpu.VMEM((n_dp * rank, feat), BF16)], grid=(TILES,),
    )(table, w, gy, *gy_got, *w_rows, h_wide, down, *downs)
    up_back, u_wide = gradient(gy, u_parts, [picks] + down_back[2:] + gy_got, "up", GRAD_COST)

    y_own = call(
        functools.partial(own_kernel, n_dp), "y_own", shape(tok, cols, dtype=F32),
        [SMEM, whole(*w.shape), row_block(feat), row_block(n_dp * rank), whole(*up.shape)]
        + [whole(rank, cols)] * away,
        row_block(cols), [pltpu.VMEM((n_dp * rank, cols), BF16)], grid=(TILES,), flops=GRAD_COST,
    )(table, w, x, u_wide, up, *ups)

    summed = call(
        site_kernel, "sites", shape(sites, rank, feat), [VMEM, ANY] + [VMEM] * n_dp, VMEM,
    )(picks, up_back[0], *down_back)
    both = [summed] + [shift(summed, "pair", q) for q in range(1, n_pair)]
    up_all = [shift(after(one, y_own), "pair", q) if q else one for q in range(n_pair) for one in up_back]
    rows = tok // sites
    of_site = lambda width: pl.BlockSpec((1, rank, width), lambda i: (i, 0, 0))
    out_rows = pl.BlockSpec((rows, cols), lambda i: (i, 0))
    down_grad, up_grad, y = call(
        functools.partial(last_kernel, n_pair, n_pair * n_dp, n_mp), "last",
        [shape(sites, rank, feat, dtype=F32), shape(sites, rank, cols, dtype=F32), shape(tok, cols)],
        [whole(*picks.shape)] + [of_site(feat)] * n_pair + [whole(rank, cols)] * (n_pair * n_dp) + [out_rows] * n_mp,
        [of_site(feat), of_site(cols), out_rows], grid=(sites,),
    )(picks, *both, *up_all, y_own, *y_got)
    return y, back, down_grad.transpose(0, 2, 1), up_grad


def solution(mesh):
    rows = P(("groups", "dp", "pair"), "mp")
    in_specs = (
        rows,
        P(None, "mp"),
        P(("groups", "dp"), "mp", None),
        P(("groups", "dp"), None, "mp"),
        rows,
        P(("groups", "dp", "pair")),
        P(("groups", "dp"), None, None),
    )
    out_specs = (rows, rows, P(("groups", "dp"), "mp", None), P(("groups", "dp"), None, "mp"))
    return jax.shard_map(shards, mesh=mesh, in_specs=in_specs, out_specs=out_specs, check_vma=False)
```

```python
import functools

import jax
import jax.numpy as jnp
from jax import lax
from jax.experimental import pallas as pl
from jax.experimental.pallas import tpu as pltpu
from jax.sharding import PartitionSpec as P

SCALE = 2.0
TILES = 3
GRAD_COST = 15_000_000_000
F32 = jnp.float32
BF16 = jnp.bfloat16
SMEM = pl.BlockSpec(memory_space=pltpu.SMEM)
VMEM = pl.BlockSpec(memory_space=pltpu.VMEM)
ANY = pl.BlockSpec(memory_space=pl.ANY)


def shape(*dims, dtype=BF16):
    return jax.ShapeDtypeStruct(dims, dtype)


def call(kernel, name, out_shape, in_specs, out_specs, scratch=(), grid=(), mib=32, flops=1):
    return pl.pallas_call(
        kernel, name=name, out_shape=out_shape, grid=grid, in_specs=in_specs, out_specs=out_specs,
        scratch_shapes=scratch,
        compiler_params=pltpu.CompilerParams(vmem_limit_bytes=mib * 1024 * 1024),
        cost_estimate=pl.CostEstimate(flops=flops, bytes_accessed=1, transcendentals=0),
    )


def shift(value, axis, by):
    size = lax.axis_size(axis)
    return lax.ppermute(value, axis, [(i, (i + by) % size) for i in range(size)])


def swap(value, axis, mask):
    return lax.ppermute(value, axis, [(i, i ^ mask) for i in range(lax.axis_size(axis))])


def after(value, *others):
    return lax.optimization_barrier((value, *others))[0]


def nn(a, b):
    return lax.dot_general(a, b, (((1,), (0,)), ((), ())), preferred_element_type=F32)


def nt(a, b):
    return lax.dot_general(a, b, (((1,), (1,)), ((), ())), preferred_element_type=F32)


def tn(a, b):
    return lax.dot_general(a, b, (((0,), (0,)), ((), ())), preferred_element_type=F32)


def run(copies):
    for copy in copies:
        copy.start()
    for copy in copies:
        copy.wait()


def wanted_site(table, n_dp, s, q=0):
    n_pair = lax.axis_size("pair")
    core = lax.rem(lax.axis_index("pair") + n_pair - q, n_pair)
    return table[0, core, lax.bitwise_xor(lax.axis_index("dp"), (n_dp - s) % n_dp)]


def slot_of(owner, b, n_dp):
    return lax.rem(n_dp - lax.bitwise_xor(lax.axis_index("dp"), owner[b]), n_dp)


def pack_kernel(n_dp, n_mp, n_pair, table, down, up, w, *refs):
    away = n_dp - 1
    ups, downs, near = refs[:away - 1], refs[away - 1:2 * away - 2], refs[2 * away - 2]
    pieces, sem = refs[2 * away - 1:-1], refs[-1]
    feat = w.shape[0] // n_mp
    part = feat // n_pair
    copies = []
    for s in range(away):
        site = wanted_site(table, n_dp, s + 1)
        if s < away - 1:
            up_to, down_to = ups[s], downs[s]
        else:
            down_to, up_to = near.at[:, pl.ds(0, feat)], near.at[:, pl.ds(feat, up.shape[2])]
        copies.append(pltpu.make_async_copy(up.at[site], up_to, sem.at[s]))
        copies.append(pltpu.make_async_copy(down.at[site], down_to, sem.at[away + s]))
    for s in range(1, n_mp):
        row = lax.rem(lax.axis_index("mp") + s, n_mp) * feat + lax.axis_index("pair") * part
        row = pl.multiple_of(row, part)
        copies.append(pltpu.make_async_copy(w.at[pl.ds(row, part)], pieces[s - 1], sem.at[2 * away + s - 1]))
    run(copies)


def share(ref, width, tail):
    start = ref.shape[1] - width if tail else 0
    return ref[:, start:start + width]


def gather_maps(n_dp, table, own, gots, wide, tail):
    rank = own.shape[1]
    wide[:rank, :] = own[wanted_site(table, n_dp, 0)]
    for s in range(1, n_dp):
        wide[s * rank:(s + 1) * rank, :] = share(gots[s - 1], wide.shape[1], tail)


def reduce_kernel(n_dp, tail, owner, table, act, _, own, *refs):
    gots, out, wide = refs[:n_dp - 1], refs[n_dp - 1], refs[n_dp]
    rank = own.shape[1]
    blocks = owner.shape[0]
    rows = act.shape[0] // blocks
    gather_maps(n_dp, table, own, gots, wide, tail)
    full = nt(act[...], wide[...])
    lane_slot = lax.broadcasted_iota(jnp.int32, (rows, n_dp * rank), 1) // rank
    folded = []
    for b in range(blocks):
        kept = jnp.where(lane_slot == slot_of(owner, b, n_dp), full[b * rows:(b + 1) * rows], 0.0)
        total = kept[:, :rank]
        for s in range(1, n_dp):
            total = total + kept[:, s * rank:(s + 1) * rank]
        folded.append(total)
    for j in range(blocks // 2):
        pair = jnp.concatenate([folded[2 * j], folded[2 * j + 1]], axis=1)
        out[j * rows:(j + 1) * rows, :] = pair.astype(BF16)


def grad_kernel(n_dp, n_part, n_behind, owner, act, near, *refs):
    refs = refs[n_behind:]
    parts, grads, wide = refs[:n_part], refs[n_part:n_part + n_dp], refs[n_part + n_dp]
    rank = wide.shape[1] // n_dp
    blocks = owner.shape[0]
    rows = act.shape[0] // blocks
    total = parts[0][...].astype(F32)
    for part in parts[1:]:
        total = total + part[...].astype(F32)
    lane_slot = lax.broadcasted_iota(jnp.int32, (rows, n_dp * rank), 1) // rank
    for b in range(blocks):
        one = total[(b // 2) * rows:(b // 2 + 1) * rows, (b % 2) * rank:(b % 2 + 1) * rank]
        spread = jnp.concatenate([one] * n_dp, axis=1)
        kept = jnp.where(lane_slot == slot_of(owner, b, n_dp), spread, 0.0)
        wide[b * rows:(b + 1) * rows, :] = kept.astype(BF16)
    full = tn(wide[...], act[...])
    width = act.shape[1]
    for s in range(n_dp):
        grads[s][:, grads[s].shape[1] - width:] = full[s * rank:(s + 1) * rank].astype(BF16)
    extra = grads[-1].shape[1] - width
    if extra:
        grads[-1][:, :extra] = near[...]


def send_kernel(n_pair, feat, n_mp, _, x, *refs):
    n_other = n_mp - 1
    pieces, outs, rows = refs[:n_other * n_pair], refs[n_other * n_pair:n_other * n_pair + n_other], refs[-n_other:]
    part = feat // n_pair

    @pl.when(pl.program_id(0) == 0)
    def _():
        for s in range(n_other):
            for q in range(n_pair):
                at = lax.rem(lax.axis_index("pair") + n_pair - q, n_pair) * part
                rows[s][pl.ds(pl.multiple_of(at, part), part), :] = pieces[s * n_pair + q][...]

    for s in range(n_other):
        outs[s][...] = nn(x[...], rows[s][...]).astype(BF16)


def back_kernel(n_dp, n_mp, table, *refs):
    w, gys, rows, wide, own_down, downs, out, picks, own, maps = (
        refs[0], refs[1:1 + n_mp], refs[1 + n_mp:2 * n_mp], refs[2 * n_mp], refs[2 * n_mp + 1],
        refs[2 * n_mp + 2:-4], refs[-4], refs[-3], refs[-2], refs[-1],
    )
    feat = out.shape[1]

    @pl.when(pl.program_id(0) == 0)
    def _():
        row = lax.broadcasted_iota(jnp.int32, picks.shape, 0)
        sites = jnp.zeros(picks.shape, jnp.int32)
        for k in range(n_dp * lax.axis_size("pair")):
            sites = jnp.where(row == k, wanted_site(table, n_dp, k % n_dp, k // n_dp), sites)
        picks[...] = sites
        own[...] = w[pl.ds(pl.multiple_of(lax.axis_index("mp") * feat, feat), feat), :]
        gather_maps(n_dp, table, own_down, downs, maps, False)

    total = nt(gys[0][...], own[...]) + SCALE * nn(wide[...], maps[...])
    for gy, row in zip(gys[1:], rows):
        total = total + nt(gy[...], row[...])
    out[...] = total.astype(BF16)


def own_kernel(n_dp, table, w, x, wide, own_up, *refs):
    ups, out, maps = refs[:n_dp - 1], refs[n_dp - 1], refs[n_dp]
    feat = x.shape[1]

    @pl.when(pl.program_id(0) == 0)
    def _():
        gather_maps(n_dp, table, own_up, ups, maps, True)

    own = w[pl.ds(pl.multiple_of(lax.axis_index("mp") * feat, feat), feat), :]
    out[...] = nn(x[...], own) + SCALE * nn(wide[...], maps[...])


def pick_sum(grads, picks, site, width, tail):
    total = jnp.zeros((grads[0].shape[0], width), F32)
    for k, grad in enumerate(grads):
        total = total + jnp.where(picks[k:k + 1, :1] == site, share(grad, width, tail).astype(F32), 0.0)
    return total


def site_kernel(picks, _, *refs):
    grads, out = refs[:-1], refs[-1]
    for site in range(out.shape[0]):
        out[site] = pick_sum(grads, picks, site, out.shape[2], False).astype(BF16)


def last_kernel(n_pair, n_ups, n_mp, picks, *refs):
    downs, ups, parts = refs[:n_pair], refs[n_pair:n_pair + n_ups], refs[n_pair + n_ups:n_pair + n_ups + n_mp]
    down, up, y = refs[-3:]
    total = downs[0][0].astype(F32)
    for part in downs[1:]:
        total = total + part[0].astype(F32)
    down[0] = SCALE * total
    up[0] = SCALE * pick_sum(ups, picks, pl.program_id(0), up.shape[2], True)
    total = parts[0][...]
    for part in parts[1:]:
        total = total + part[...].astype(F32)
    y[...] = total.astype(BF16)


def shards(x, w, down, up, gy, owner, table):
    tok, feat = x.shape
    cols = w.shape[1]
    sites, rank = up.shape[:2]
    n_dp, n_mp, n_pair = (lax.axis_size(a) for a in ("dp", "mp", "pair"))
    n_other = n_mp - 1
    down = down.transpose(0, 2, 1)
    part = feat // n_pair
    tile = tok // TILES
    row_block = lambda width: pl.BlockSpec((tile, width), lambda i: (i, 0))
    whole = lambda *dims: pl.BlockSpec(dims, lambda i: (0,) * len(dims))

    away = n_dp - 1
    far = away - 1
    packed = call(
        functools.partial(pack_kernel, n_dp, n_mp, n_pair), "pack",
        [shape(rank, cols)] * far + [shape(rank, feat)] * far + [shape(rank, feat + cols)] + [shape(part, cols)] * n_other,
        [SMEM, ANY, ANY, ANY], [VMEM] * (2 * far + 1 + n_other),
        [pltpu.SemaphoreType.DMA((2 * away + n_other,))], mib=60,
    )(table, down, up, w)
    pieces = [shift(packed[2 * far + s], "mp", s) for s in range(1, n_mp)]
    near = swap(packed[2 * far], "dp", 1)
    ups = [swap(packed[s - 1], "dp", n_dp - s) for s in range(1, away)] + [near]
    downs = [swap(after(packed[far + s - 1], ups[0]), "dp", n_dp - s) for s in range(1, away)] + [near]

    def low_rank(act, own, maps, behind, tail, name):
        mine = call(
            functools.partial(reduce_kernel, n_dp, tail), name + "_part",
            shape(tok // 2, 2 * rank), [SMEM, SMEM, VMEM, ANY] + [VMEM] * n_dp, VMEM,
            [pltpu.VMEM((n_dp * rank, act.shape[1]), BF16)],
        )(owner, table, act, behind, own, *maps)
        return [mine] + [shift(mine, "mp", s) for s in range(1, n_mp)]

    def gradient(act, parts, near, width, behind, name):
        *grads, wide = call(
            functools.partial(grad_kernel, n_dp, n_mp, len(behind)), name + "_grad",
            [shape(rank, act.shape[1])] * away + [shape(rank, width)] + [shape(tok, n_dp * rank)],
            [SMEM, VMEM, VMEM] + [ANY] * len(behind) + [VMEM] * n_mp, [VMEM] * (n_dp + 1), flops=GRAD_COST,
        )(owner, act, near, *behind, *parts)
        return [grads[0]] + [swap(grads[s], "dp", n_dp - s) for s in range(1, away)], grads[-1], wide

    h_parts = low_rank(gy, up, ups, ups[0], True, "h")
    gy_got = [shift(after(gy, *pieces), "mp", s) for s in range(1, n_mp)]
    down_back, down_near, h_wide = gradient(x, h_parts, h_parts[0], feat, downs, "down")
    u_parts = low_rank(x, down, downs, h_wide, False, "u")

    parts = []
    for piece in pieces:
        parts += [piece] + [shift(after(piece, h_wide), "pair", q) for q in range(1, n_pair)]
    sent = call(
        functools.partial(send_kernel, n_pair, feat, n_mp), "y_send",
        [shape(tok, cols)] * n_other + [shape(feat, cols)] * n_other,
        [ANY, row_block(feat)] + [whole(part, cols)] * len(parts),
        [row_block(cols)] * n_other + [whole(feat, cols)] * n_other,
        grid=(TILES,),
    )(u_parts[0], x, *parts)
    w_rows = sent[n_other:]
    y_got = [shift(sent[s - 1], "mp", n_mp - s) for s in range(1, n_mp)]
    back, picks = call(
        functools.partial(back_kernel, n_dp, n_mp), "back",
        [shape(tok, feat), shape(-(-n_dp * n_pair // 8) * 8, 128, dtype=jnp.int32)],
        [SMEM, whole(*w.shape)] + [row_block(cols)] * n_mp + [whole(feat, cols)] * n_other
        + [row_block(n_dp * rank), whole(*down.shape)] + [whole(*one.shape) for one in downs],
        [row_block(feat), whole(-(-n_dp * n_pair // 8) * 8, 128)],
        [pltpu.VMEM((feat, cols), BF16), pltpu.VMEM((n_dp * rank, feat), BF16)], grid=(TILES,),
    )(table, w, gy, *gy_got, *w_rows, h_wide, down, *downs)
    up_back, both_near, u_wide = gradient(
        gy, u_parts, down_near, feat + cols, [picks] + down_back[1:] + gy_got, "up"
    )
    both_near = swap(both_near, "dp", 1)
    down_back, up_back = down_back + [both_near], up_back + [both_near]

    y_own = call(
        functools.partial(own_kernel, n_dp), "y_own", shape(tok, cols, dtype=F32),
        [SMEM, whole(*w.shape), row_block(feat), row_block(n_dp * rank), whole(*up.shape)]
        + [whole(*one.shape) for one in ups],
        row_block(cols), [pltpu.VMEM((n_dp * rank, cols), BF16)], grid=(TILES,), flops=GRAD_COST,
    )(table, w, x, u_wide, up, *ups)

    summed = call(
        site_kernel, "sites", shape(sites, rank, feat), [VMEM, ANY] + [VMEM] * n_dp, VMEM,
    )(picks, y_own, *down_back)
    both = [summed] + [shift(after(summed, *up_back[1:away]), "pair", q) for q in range(1, n_pair)]
    up_all = [shift(after(one, y_own), "pair", q) if q else one for q in range(n_pair) for one in up_back]
    rows = tok // sites
    of_site = lambda width: pl.BlockSpec((1, rank, width), lambda i: (i, 0, 0))
    out_rows = pl.BlockSpec((rows, cols), lambda i: (i, 0))
    down_grad, up_grad, y = call(
        functools.partial(last_kernel, n_pair, n_pair * n_dp, n_mp), "last",
        [shape(sites, rank, feat, dtype=F32), shape(sites, rank, cols, dtype=F32), shape(tok, cols)],
        [whole(*picks.shape)] + [of_site(feat)] * n_pair + [whole(*one.shape) for one in up_all] + [out_rows] * n_mp,
        [of_site(feat), of_site(cols), out_rows], grid=(sites,),
    )(picks, *both, *up_all, y_own, *y_got)
    return y, back, down_grad.transpose(0, 2, 1), up_grad


def solution(mesh):
    rows = P(("groups", "dp", "pair"), "mp")
    in_specs = (
        rows,
        P(None, "mp"),
        P(("groups", "dp"), "mp", None),
        P(("groups", "dp"), None, "mp"),
        rows,
        P(("groups", "dp", "pair")),
        P(("groups", "dp"), None, None),
    )
    out_specs = (rows, rows, P(("groups", "dp"), "mp", None), P(("groups", "dp"), None, "mp"))
    return jax.shard_map(shards, mesh=mesh, in_specs=in_specs, out_specs=out_specs, check_vma=False)
```

```python
import functools

import jax
import jax.numpy as jnp
from jax import lax
from jax.experimental import pallas as pl
from jax.experimental.pallas import tpu as pltpu
from jax.sharding import PartitionSpec as P

SCALE = 2.0
TILES = 3
GRAD_COST = 15_000_000_000
F32 = jnp.float32
BF16 = jnp.bfloat16
SMEM = pl.BlockSpec(memory_space=pltpu.SMEM)
VMEM = pl.BlockSpec(memory_space=pltpu.VMEM)
ANY = pl.BlockSpec(memory_space=pl.ANY)


def shape(*dims, dtype=BF16):
    return jax.ShapeDtypeStruct(dims, dtype)


def call(kernel, name, out_shape, in_specs, out_specs, scratch=(), grid=(), mib=32, flops=1):
    return pl.pallas_call(
        kernel, name=name, out_shape=out_shape, grid=grid, in_specs=in_specs, out_specs=out_specs,
        scratch_shapes=scratch,
        compiler_params=pltpu.CompilerParams(vmem_limit_bytes=mib * 1024 * 1024),
        cost_estimate=pl.CostEstimate(flops=flops, bytes_accessed=1, transcendentals=0),
    )


def shift(value, axis, by):
    size = lax.axis_size(axis)
    return lax.ppermute(value, axis, [(i, (i + by) % size) for i in range(size)])


def swap(value, axis, mask):
    return lax.ppermute(value, axis, [(i, i ^ mask) for i in range(lax.axis_size(axis))])


def after(value, *others):
    return lax.optimization_barrier((value, *others))[0]


def nn(a, b):
    return lax.dot_general(a, b, (((1,), (0,)), ((), ())), preferred_element_type=F32)


def nt(a, b):
    return lax.dot_general(a, b, (((1,), (1,)), ((), ())), preferred_element_type=F32)


def tn(a, b):
    return lax.dot_general(a, b, (((0,), (0,)), ((), ())), preferred_element_type=F32)


def run(copies):
    for copy in copies:
        copy.start()
    for copy in copies:
        copy.wait()


def wanted_site(table, n_dp, s, q=0):
    n_pair = lax.axis_size("pair")
    core = lax.rem(lax.axis_index("pair") + n_pair - q, n_pair)
    return table[0, core, lax.bitwise_xor(lax.axis_index("dp"), (n_dp - s) % n_dp)]


def slot_of(owner, b, n_dp):
    return lax.rem(n_dp - lax.bitwise_xor(lax.axis_index("dp"), owner[b]), n_dp)


def pack_kernel(n_dp, n_mp, n_share, table, down, up, w, *refs):
    away = n_dp - 1
    ups, downs, pieces, sem = refs[:away], refs[away:2 * away], refs[2 * away:-1], refs[-1]
    feat = w.shape[0] // n_mp
    part = feat // n_share
    place = lax.axis_index("groups") * lax.axis_size("pair") + lax.axis_index("pair")
    copies = []
    for s in range(away):
        site = wanted_site(table, n_dp, s + 1)
        copies.append(pltpu.make_async_copy(up.at[site], ups[s], sem.at[s]))
        copies.append(pltpu.make_async_copy(down.at[site], downs[s], sem.at[away + s]))
    for s in range(1, n_mp):
        row = pl.multiple_of(lax.rem(lax.axis_index("mp") + s, n_mp) * feat + place * part, part)
        copies.append(pltpu.make_async_copy(w.at[pl.ds(row, part)], pieces[s - 1], sem.at[2 * away + s - 1]))
    run(copies)


def gather_maps(n_dp, table, own, gots, wide):
    rank = own.shape[1]
    wide[:rank, :] = own[wanted_site(table, n_dp, 0)]
    for s in range(1, n_dp):
        wide[s * rank:(s + 1) * rank, :] = gots[s - 1][...]


def reduce_kernel(n_dp, owner, table, act, _, own, *refs):
    gots, out, again, wide = refs[:n_dp - 1], refs[n_dp - 1], refs[n_dp:-1], refs[-1]
    rank = own.shape[1]
    blocks = owner.shape[0]
    rows = act.shape[0] // blocks
    for late in again:
        late[...] = act[act.shape[0] - late.shape[0]:, :]
    gather_maps(n_dp, table, own, gots, wide)
    full = nt(act[...], wide[...])
    lane_slot = lax.broadcasted_iota(jnp.int32, (rows, n_dp * rank), 1) // rank
    folded = []
    for b in range(blocks):
        kept = jnp.where(lane_slot == slot_of(owner, b, n_dp), full[b * rows:(b + 1) * rows], 0.0)
        total = kept[:, :rank]
        for s in range(1, n_dp):
            total = total + kept[:, s * rank:(s + 1) * rank]
        folded.append(total)
    for j in range(blocks // 2):
        pair = jnp.concatenate([folded[2 * j], folded[2 * j + 1]], axis=1)
        out[j * rows:(j + 1) * rows, :] = pair.astype(BF16)


def grad_kernel(n_dp, n_part, n_behind, owner, act, *refs):
    refs = refs[n_behind:]
    parts, grads, wide = refs[:n_part], refs[n_part:n_part + n_dp], refs[n_part + n_dp]
    rank = wide.shape[1] // n_dp
    blocks = owner.shape[0]
    rows = act.shape[0] // blocks
    total = parts[0][...].astype(F32)
    for part in parts[1:]:
        total = total + part[...].astype(F32)
    lane_slot = lax.broadcasted_iota(jnp.int32, (rows, n_dp * rank), 1) // rank
    for b in range(blocks):
        one = total[(b // 2) * rows:(b // 2 + 1) * rows, (b % 2) * rank:(b % 2 + 1) * rank]
        spread = jnp.concatenate([one] * n_dp, axis=1)
        kept = jnp.where(lane_slot == slot_of(owner, b, n_dp), spread, 0.0)
        wide[b * rows:(b + 1) * rows, :] = kept.astype(BF16)
    full = tn(wide[...], act[...])
    for s in range(n_dp):
        grads[s][...] = full[s * rank:(s + 1) * rank].astype(BF16)


def send_kernel(n_groups, n_pair, feat, n_mp, _, x, *refs):
    n_other, n_share = n_mp - 1, n_groups * n_pair
    pieces, outs, rows = refs[:n_other * n_share], refs[-2 * n_other:-n_other], refs[-n_other:]
    part = feat // n_share

    @pl.when(pl.program_id(0) == 0)
    def _():
        for s in range(n_other):
            for k in range(n_share):
                group = lax.rem(lax.axis_index("groups") + n_groups - k // n_pair, n_groups)
                core = lax.rem(lax.axis_index("pair") + n_pair - k % n_pair, n_pair)
                at = pl.multiple_of((group * n_pair + core) * part, part)
                rows[s][pl.ds(at, part), :] = pieces[s * n_share + k][...]

    for s in range(n_other):
        outs[s][...] = nn(x[...], rows[s][...]).astype(BF16)


def back_kernel(n_dp, n_mp, table, w, gy, wide, own_down, *refs):
    n_other = n_mp - 1
    early, late, rows = refs[:n_other], refs[n_other:2 * n_other], refs[2 * n_other:3 * n_other]
    downs, out, picks, own, maps = refs[3 * n_other:-4], refs[-4], refs[-3], refs[-2], refs[-1]
    feat = out.shape[1]

    @pl.when(pl.program_id(0) == 0)
    def _():
        row = lax.broadcasted_iota(jnp.int32, picks.shape, 0)
        sites = jnp.zeros(picks.shape, jnp.int32)
        for k in range(n_dp * lax.axis_size("pair")):
            sites = jnp.where(row == k, wanted_site(table, n_dp, k % n_dp, k // n_dp), sites)
        picks[...] = sites
        own[...] = w[pl.ds(pl.multiple_of(lax.axis_index("mp") * feat, feat), feat), :]
        gather_maps(n_dp, table, own_down, downs, maps)

    total = nt(gy[...], own[...]) + SCALE * nn(wide[...], maps[...])
    for first, second, row in zip(early, late, rows):
        got = jnp.where(pl.program_id(0) == 0, first[...], second[...])
        total = total + nt(got, row[...])
    out[...] = total.astype(BF16)


def own_kernel(n_dp, table, w, x, wide, own_up, *refs):
    ups, out, maps = refs[:n_dp - 1], refs[n_dp - 1], refs[n_dp]
    feat = x.shape[1]

    @pl.when(pl.program_id(0) == 0)
    def _():
        gather_maps(n_dp, table, own_up, ups, maps)

    own = w[pl.ds(pl.multiple_of(lax.axis_index("mp") * feat, feat), feat), :]
    out[...] = nn(x[...], own) + SCALE * nn(wide[...], maps[...])


def pick_sum(grads, picks, site):
    total = jnp.zeros(grads[0].shape, F32)
    for k, grad in enumerate(grads):
        total = total + jnp.where(picks[k:k + 1, :1] == site, grad[...].astype(F32), 0.0)
    return total


def site_kernel(picks, _, *refs):
    grads, out = refs[:-1], refs[-1]
    for site in range(out.shape[0]):
        out[site] = pick_sum(grads, picks, site).astype(BF16)


def last_kernel(n_pair, n_ups, n_mp, picks, *refs):
    downs, ups, parts = refs[:n_pair], refs[n_pair:n_pair + n_ups], refs[n_pair + n_ups:n_pair + n_ups + n_mp]
    down, up, y = refs[-3:]
    total = downs[0][0].astype(F32)
    for part in downs[1:]:
        total = total + part[0].astype(F32)
    down[0] = SCALE * total
    up[0] = SCALE * pick_sum(ups, picks, pl.program_id(0))
    total = parts[0][...]
    for part in parts[1:]:
        total = total + part[...].astype(F32)
    y[...] = total.astype(BF16)


def shards(x, w, down, up, gy, owner, table):
    tok, feat = x.shape
    cols = w.shape[1]
    sites, rank = up.shape[:2]
    n_groups, n_dp, n_mp, n_pair = (lax.axis_size(a) for a in ("groups", "dp", "mp", "pair"))
    n_other, n_share = n_mp - 1, n_groups * n_pair
    down = down.transpose(0, 2, 1)
    part = feat // n_share
    half = tok // 2
    tile = tok // TILES
    row_block = lambda width: pl.BlockSpec((tile, width), lambda i: (i, 0))
    whole = lambda *dims: pl.BlockSpec(dims, lambda i: (0,) * len(dims))

    away = n_dp - 1
    packed = call(
        functools.partial(pack_kernel, n_dp, n_mp, n_share), "pack",
        [shape(rank, cols)] * away + [shape(rank, feat)] * away + [shape(part, cols)] * n_other,
        [SMEM, ANY, ANY, ANY], [VMEM] * (2 * away + n_other),
        [pltpu.SemaphoreType.DMA((2 * away + n_other,))], mib=60,
    )(table, down, up, w)
    pieces = [shift(packed[2 * away + s - 1], "mp", s) for s in range(1, n_mp)]
    ups = [swap(packed[s - 1], "dp", n_dp - s) for s in range(1, n_dp)]
    downs = [swap(after(packed[away + s - 1], ups[0]), "dp", n_dp - s) for s in range(1, n_dp)]

    gy_early = [shift(after(gy[:half], packed[0]), "mp", s) for s in range(1, n_mp)]

    def low_rank(act, own, maps, behind, again, name):
        mine, *late = call(
            functools.partial(reduce_kernel, n_dp), name + "_part",
            [shape(tok // 2, 2 * rank)] + again,
            [SMEM, SMEM, VMEM, ANY] + [VMEM] * n_dp, [VMEM] * (1 + len(again)),
            [pltpu.VMEM((n_dp * rank, act.shape[1]), BF16)],
        )(owner, table, act, behind, own, *maps)
        return [mine] + [shift(mine, "mp", s) for s in range(1, n_mp)], late

    def gradient(act, parts, behind, name, flops):
        *grads, wide = call(
            functools.partial(grad_kernel, n_dp, n_mp, len(behind)), name + "_grad",
            [shape(rank, act.shape[1])] * n_dp + [shape(tok, n_dp * rank)],
            [SMEM, VMEM] + [ANY] * len(behind) + [VMEM] * n_mp, [VMEM] * (n_dp + 1), flops=flops,
        )(owner, act, *behind, *parts)
        return [grads[0]] + [swap(grads[s], "dp", n_dp - s) for s in range(1, n_dp)], wide

    h_parts, late = low_rank(gy, up, ups, ups[0], [shape(tok - half, cols)], "h")
    gy_late = [shift(after(late[0], *gy_early), "mp", s) for s in range(1, n_mp)]
    down_back, h_wide = gradient(x, h_parts, downs, "down", GRAD_COST)
    u_parts, _ = low_rank(x, down, downs, h_wide, [], "u")

    parts = []
    for piece in pieces:
        for j in range(n_groups):
            one = shift(after(piece, h_parts[0]), "groups", j) if j else piece
            parts += [shift(after(one, h_wide if j else h_parts[0]), "pair", q) if q else one for q in range(n_pair)]
    sent = call(
        functools.partial(send_kernel, n_groups, n_pair, feat, n_mp), "y_send",
        [shape(tok, cols)] * n_other + [shape(feat, cols)] * n_other,
        [ANY, row_block(feat)] + [whole(part, cols)] * len(parts),
        [row_block(cols)] * n_other + [whole(feat, cols)] * n_other,
        grid=(TILES,),
    )(u_parts[0], x, *parts)
    w_rows = sent[n_other:]
    y_got = [shift(sent[s - 1], "mp", n_mp - s) for s in range(1, n_mp)]
    half_rows = lambda width: pl.BlockSpec((half, width), lambda i: (i, 0))
    back, picks = call(
        functools.partial(back_kernel, n_dp, n_mp), "back",
        [shape(tok, feat), shape(-(-n_dp * n_pair // 8) * 8, 128, dtype=jnp.int32)],
        [SMEM, whole(*w.shape), half_rows(cols), half_rows(n_dp * rank), whole(*down.shape)]
        + [whole(half, cols)] * (2 * n_other) + [whole(feat, cols)] * n_other + [whole(rank, feat)] * away,
        [half_rows(feat), whole(-(-n_dp * n_pair // 8) * 8, 128)],
        [pltpu.VMEM((feat, cols), BF16), pltpu.VMEM((n_dp * rank, feat), BF16)], grid=(2,),
    )(table, w, gy, h_wide, down, *gy_early, *gy_late, *w_rows, *downs)
    up_back, u_wide = gradient(gy, u_parts, [picks] + down_back[1:] + gy_late, "up", GRAD_COST)

    y_own = call(
        functools.partial(own_kernel, n_dp), "y_own", shape(tok, cols, dtype=F32),
        [SMEM, whole(*w.shape), row_block(feat), row_block(n_dp * rank), whole(*up.shape)]
        + [whole(rank, cols)] * away,
        row_block(cols), [pltpu.VMEM((n_dp * rank, cols), BF16)], grid=(TILES,), flops=GRAD_COST,
    )(table, w, x, u_wide, up, *ups)

    summed = call(
        site_kernel, "sites", shape(sites, rank, feat), [VMEM, ANY] + [VMEM] * n_dp, VMEM,
    )(picks, up_back[0], *down_back)
    both = [summed] + [shift(summed, "pair", q) for q in range(1, n_pair)]
    up_all = [shift(after(one, y_own), "pair", q) if q else one for q in range(n_pair) for one in up_back]
    rows = tok // sites
    of_site = lambda width: pl.BlockSpec((1, rank, width), lambda i: (i, 0, 0))
    out_rows = pl.BlockSpec((rows, cols), lambda i: (i, 0))
    down_grad, up_grad, y = call(
        functools.partial(last_kernel, n_pair, n_pair * n_dp, n_mp), "last",
        [shape(sites, rank, feat, dtype=F32), shape(sites, rank, cols, dtype=F32), shape(tok, cols)],
        [whole(*picks.shape)] + [of_site(feat)] * n_pair + [whole(rank, cols)] * (n_pair * n_dp) + [out_rows] * n_mp,
        [of_site(feat), of_site(cols), out_rows], grid=(sites,),
    )(picks, *both, *up_all, y_own, *y_got)
    return y, back, down_grad.transpose(0, 2, 1), up_grad


def solution(mesh):
    rows = P(("groups", "dp", "pair"), "mp")
    in_specs = (
        rows,
        P(None, "mp"),
        P(("groups", "dp"), "mp", None),
        P(("groups", "dp"), None, "mp"),
        rows,
        P(("groups", "dp", "pair")),
        P(("groups", "dp"), None, None),
    )
    out_specs = (rows, rows, P(("groups", "dp"), "mp", None), P(("groups", "dp"), None, "mp"))
    return jax.shard_map(shards, mesh=mesh, in_specs=in_specs, out_specs=out_specs, check_vma=False)
```

```python
import functools

import jax
import jax.numpy as jnp
from jax import lax
from jax.experimental import pallas as pl
from jax.experimental.pallas import tpu as pltpu
from jax.sharding import PartitionSpec as P

SCALE = 2.0
TILES = 3
GRAD_COST = 15_000_000_000
F32 = jnp.float32
BF16 = jnp.bfloat16
SMEM = pl.BlockSpec(memory_space=pltpu.SMEM)
VMEM = pl.BlockSpec(memory_space=pltpu.VMEM)
ANY = pl.BlockSpec(memory_space=pl.ANY)


def shape(*dims, dtype=BF16):
    return jax.ShapeDtypeStruct(dims, dtype)


def call(kernel, name, out_shape, in_specs, out_specs, scratch=(), grid=(), mib=32, flops=1):
    return pl.pallas_call(
        kernel, name=name, out_shape=out_shape, grid=grid, in_specs=in_specs, out_specs=out_specs,
        scratch_shapes=scratch,
        compiler_params=pltpu.CompilerParams(vmem_limit_bytes=mib * 1024 * 1024),
        cost_estimate=pl.CostEstimate(flops=flops, bytes_accessed=1, transcendentals=0),
    )


def shift(value, axis, by):
    size = lax.axis_size(axis)
    return lax.ppermute(value, axis, [(i, (i + by) % size) for i in range(size)])


def swap(value, axis, mask):
    return lax.ppermute(value, axis, [(i, i ^ mask) for i in range(lax.axis_size(axis))])


def after(value, *others):
    return lax.optimization_barrier((value, *others))[0]


def nn(a, b):
    return lax.dot_general(a, b, (((1,), (0,)), ((), ())), preferred_element_type=F32)


def nt(a, b):
    return lax.dot_general(a, b, (((1,), (1,)), ((), ())), preferred_element_type=F32)


def tn(a, b):
    return lax.dot_general(a, b, (((0,), (0,)), ((), ())), preferred_element_type=F32)


def wanted_site(table, n_dp, s, q=0):
    n_pair = lax.axis_size("pair")
    core = lax.rem(lax.axis_index("pair") + n_pair - q, n_pair)
    return table[0, core, lax.bitwise_xor(lax.axis_index("dp"), (n_dp - s) % n_dp)]


def slot_of(owner, b, n_dp):
    return lax.rem(n_dp - lax.bitwise_xor(lax.axis_index("dp"), owner[b]), n_dp)


def pack_kernel(n_dp, n_mp, n_pair, table, down, up, w, *refs):
    away = n_dp - 1
    ups, downs, pieces, rows, sem = refs[:away], refs[away:2 * away], refs[2 * away:-2], refs[-2], refs[-1]
    feat = w.shape[0] // n_mp
    part = feat // n_pair
    fetches, copies = [], []
    for s in range(1, n_mp):
        row = lax.rem(lax.axis_index("mp") + s, n_mp) * feat + lax.axis_index("pair") * part
        row = pl.multiple_of(row, part)
        fetches.append(pltpu.make_async_copy(w.at[pl.ds(row, part)], rows.at[s - 1], sem.at[s - 1]))
        fetches[-1].start()
    for s in range(away):
        site = wanted_site(table, n_dp, s + 1)
        copies.append(pltpu.make_async_copy(up.at[site], ups[s], sem.at[n_mp - 1 + s]))
        copies.append(pltpu.make_async_copy(down.at[site], downs[s], sem.at[n_mp - 1 + away + s]))
    for copy in copies:
        copy.start()
    for s, fetch in enumerate(fetches):
        fetch.wait()
        copies.append(pltpu.make_async_copy(rows.at[s], pieces[s], sem.at[n_mp - 1 + 2 * away + s]))
        copies[-1].start()
    for copy in copies:
        copy.wait()


def gather_maps(n_dp, table, own, gots, wide):
    rank = own.shape[1]
    wide[:rank, :] = own[wanted_site(table, n_dp, 0)]
    for s in range(1, n_dp):
        wide[s * rank:(s + 1) * rank, :] = gots[s - 1][...]


def reduce_kernel(n_dp, owner, table, act, _, own, *refs):
    gots, out, wide = refs[:n_dp - 1], refs[n_dp - 1], refs[n_dp]
    rank = own.shape[1]
    blocks = owner.shape[0]
    rows = act.shape[0] // blocks
    gather_maps(n_dp, table, own, gots, wide)
    full = nt(act[...], wide[...])
    lane_slot = lax.broadcasted_iota(jnp.int32, (rows, n_dp * rank), 1) // rank
    folded = []
    for b in range(blocks):
        kept = jnp.where(lane_slot == slot_of(owner, b, n_dp), full[b * rows:(b + 1) * rows], 0.0)
        total = kept[:, :rank]
        for s in range(1, n_dp):
            total = total + kept[:, s * rank:(s + 1) * rank]
        folded.append(total)
    for j in range(blocks // 2):
        pair = jnp.concatenate([folded[2 * j], folded[2 * j + 1]], axis=1)
        out[j * rows:(j + 1) * rows, :] = pair.astype(BF16)


def grad_kernel(n_dp, n_part, n_behind, owner, act, *refs):
    refs = refs[n_behind:]
    parts, grads, wide = refs[:n_part], refs[n_part:n_part + n_dp], refs[n_part + n_dp]
    rank = wide.shape[1] // n_dp
    blocks = owner.shape[0]
    rows = act.shape[0] // blocks
    total = parts[0][...].astype(F32)
    for part in parts[1:]:
        total = total + part[...].astype(F32)
    lane_slot = lax.broadcasted_iota(jnp.int32, (rows, n_dp * rank), 1) // rank
    for b in range(blocks):
        one = total[(b // 2) * rows:(b // 2 + 1) * rows, (b % 2) * rank:(b % 2 + 1) * rank]
        spread = jnp.concatenate([one] * n_dp, axis=1)
        kept = jnp.where(lane_slot == slot_of(owner, b, n_dp), spread, 0.0)
        wide[b * rows:(b + 1) * rows, :] = kept.astype(BF16)
    full = tn(wide[...], act[...])
    for s in range(n_dp):
        grads[s][...] = full[s * rank:(s + 1) * rank].astype(BF16)


def send_kernel(n_pair, feat, n_mp, _, __, x, *refs):
    n_other = n_mp - 1
    pieces, outs, rows = refs[:n_other * n_pair], refs[n_other * n_pair:n_other * n_pair + n_other], refs[-n_other:]
    part = feat // n_pair

    @pl.when(pl.program_id(0) == 0)
    def _():
        for s in range(n_other):
            for q in range(n_pair):
                at = lax.rem(lax.axis_index("pair") + n_pair - q, n_pair) * part
                rows[s][pl.ds(pl.multiple_of(at, part), part), :] = pieces[s * n_pair + q][...]

    for s in range(n_other):
        outs[s][...] = nn(x[...], rows[s][...]).astype(BF16)


def back_kernel(n_dp, n_mp, table, *refs):
    w, gys, rows, wide, own_down, downs, out, picks, own, maps = (
        refs[0], refs[1:1 + n_mp], refs[1 + n_mp:2 * n_mp], refs[2 * n_mp], refs[2 * n_mp + 1],
        refs[2 * n_mp + 2:-4], refs[-4], refs[-3], refs[-2], refs[-1],
    )
    feat = out.shape[1]

    @pl.when(pl.program_id(0) == 0)
    def _():
        row = lax.broadcasted_iota(jnp.int32, picks.shape, 0)
        sites = jnp.zeros(picks.shape, jnp.int32)
        for k in range(n_dp * lax.axis_size("pair")):
            sites = jnp.where(row == k, wanted_site(table, n_dp, k % n_dp, k // n_dp), sites)
        picks[...] = sites
        own[...] = w[pl.ds(pl.multiple_of(lax.axis_index("mp") * feat, feat), feat), :]
        gather_maps(n_dp, table, own_down, downs, maps)

    total = nt(gys[0][...], own[...]) + SCALE * nn(wide[...], maps[...])
    for gy, row in zip(gys[1:], rows):
        total = total + nt(gy[...], row[...])
    out[...] = total.astype(BF16)


def own_kernel(n_dp, table, w, x, wide, own_up, *refs):
    ups, out, maps = refs[:n_dp - 1], refs[n_dp - 1], refs[n_dp]
    feat = x.shape[1]

    @pl.when(pl.program_id(0) == 0)
    def _():
        gather_maps(n_dp, table, own_up, ups, maps)

    own = w[pl.ds(pl.multiple_of(lax.axis_index("mp") * feat, feat), feat), :]
    out[...] = (nn(x[...], own) + SCALE * nn(wide[...], maps[...])).astype(BF16)


def pick_sum(grads, picks, site):
    total = jnp.zeros(grads[0].shape, F32)
    for k, grad in enumerate(grads):
        total = total + jnp.where(picks[k:k + 1, :1] == site, grad[...].astype(F32), 0.0)
    return total


def site_kernel(picks, _, *refs):
    grads, out = refs[:-1], refs[-1]
    for site in range(out.shape[0]):
        out[site] = pick_sum(grads, picks, site).astype(BF16)


def last_kernel(n_pair, n_ups, n_mp, picks, *refs):
    downs, ups, parts = refs[:n_pair], refs[n_pair:n_pair + n_ups], refs[n_pair + n_ups:n_pair + n_ups + n_mp]
    down, up, y = refs[-3:]
    total = downs[0][0].astype(F32)
    for part in downs[1:]:
        total = total + part[0].astype(F32)
    down[0] = SCALE * total
    up[0] = SCALE * pick_sum(ups, picks, pl.program_id(0))
    total = parts[0][...].astype(F32)
    for part in parts[1:]:
        total = total + part[...].astype(F32)
    y[...] = total.astype(BF16)


def shards(x, w, down, up, gy, owner, table):
    tok, feat = x.shape
    cols = w.shape[1]
    sites, rank = up.shape[:2]
    n_dp, n_mp, n_pair = (lax.axis_size(a) for a in ("dp", "mp", "pair"))
    n_other = n_mp - 1
    down = down.transpose(0, 2, 1)
    part = feat // n_pair
    tile = tok // TILES
    row_block = lambda width: pl.BlockSpec((tile, width), lambda i: (i, 0))
    whole = lambda *dims: pl.BlockSpec(dims, lambda i: (0,) * len(dims))

    away = n_dp - 1
    packed = call(
        functools.partial(pack_kernel, n_dp, n_mp, n_pair), "pack",
        [shape(rank, cols)] * away + [shape(rank, feat)] * away + [shape(part, cols)] * n_other,
        [SMEM, VMEM, VMEM, ANY], [ANY] * (2 * away + n_other),
        [pltpu.VMEM((n_other, part, cols), BF16), pltpu.SemaphoreType.DMA((2 * away + 2 * n_other,))], mib=60,
    )(table, down, up, w)
    pieces = [shift(packed[2 * away + s - 1], "mp", s) for s in range(1, n_mp)]
    ups = [swap(packed[s - 1], "dp", n_dp - s) for s in range(1, n_dp)]
    downs = [swap(after(packed[away + s - 1], ups[0]), "dp", n_dp - s) for s in range(1, n_dp)]

    def low_rank(act, own, maps, behind, name):
        mine = call(
            functools.partial(reduce_kernel, n_dp), name + "_part",
            shape(tok // 2, 2 * rank), [SMEM, SMEM, VMEM, ANY] + [VMEM] * n_dp, VMEM,
            [pltpu.VMEM((n_dp * rank, act.shape[1]), BF16)],
        )(owner, table, act, behind, own, *maps)
        return [mine] + [shift(mine, "mp", s) for s in range(1, n_mp)]

    def gradient(act, parts, behind, name, flops):
        *grads, wide = call(
            functools.partial(grad_kernel, n_dp, n_mp, len(behind)), name + "_grad",
            [shape(rank, act.shape[1])] * n_dp + [shape(tok, n_dp * rank)],
            [SMEM, VMEM] + [ANY] * len(behind) + [VMEM] * n_mp, [VMEM] * (n_dp + 1), flops=flops,
        )(owner, act, *behind, *parts)
        return [grads[0]] + [swap(grads[s], "dp", n_dp - s) for s in range(1, n_dp)], wide

    h_parts = low_rank(gy, up, ups, ups[0], "h")
    gy_got = [shift(after(gy, *pieces), "mp", s) for s in range(1, n_mp)]
    down_back, h_wide = gradient(x, h_parts, downs, "down", GRAD_COST)
    u_parts = low_rank(x, down, downs, h_wide, "u")

    parts = []
    for piece in pieces:
        parts += [piece] + [shift(after(piece, h_wide), "pair", q) for q in range(1, n_pair)]
    sent = call(
        functools.partial(send_kernel, n_pair, feat, n_mp), "y_send",
        [shape(tok, cols)] * n_other + [shape(feat, cols)] * n_other,
        [ANY, ANY, row_block(feat)] + [whole(part, cols)] * len(parts),
        [row_block(cols)] * n_other + [whole(feat, cols)] * n_other,
        grid=(TILES,),
    )(u_parts[0], down_back[away], x, *parts)
    w_rows = sent[n_other:]
    y_got = [shift(sent[s - 1], "mp", n_mp - s) for s in range(1, n_mp)]
    back, picks = call(
        functools.partial(back_kernel, n_dp, n_mp), "back",
        [shape(tok, feat), shape(-(-n_dp * n_pair // 8) * 8, 128, dtype=jnp.int32)],
        [SMEM, whole(*w.shape)] + [row_block(cols)] * n_mp + [whole(feat, cols)] * n_other
        + [row_block(n_dp * rank), whole(*down.shape)] + [whole(rank, feat)] * away,
        [row_block(feat), whole(-(-n_dp * n_pair // 8) * 8, 128)],
        [pltpu.VMEM((feat, cols), BF16), pltpu.VMEM((n_dp * rank, feat), BF16)], grid=(TILES,),
    )(table, w, gy, *gy_got, *w_rows, h_wide, down, *downs)
    up_back, u_wide = gradient(gy, u_parts, [picks] + down_back[1:] + gy_got, "up", GRAD_COST)

    y_own = call(
        functools.partial(own_kernel, n_dp), "y_own", shape(tok, cols),
        [SMEM, whole(*w.shape), row_block(feat), row_block(n_dp * rank), whole(*up.shape)]
        + [whole(rank, cols)] * away,
        row_block(cols), [pltpu.VMEM((n_dp * rank, cols), BF16)], grid=(TILES,), flops=GRAD_COST,
    )(table, w, x, u_wide, up, *ups)

    summed = call(
        site_kernel, "sites", shape(sites, rank, feat), [VMEM, ANY] + [VMEM] * n_dp, VMEM,
    )(picks, up_back[0], *down_back)
    both = [summed] + [shift(summed, "pair", q) for q in range(1, n_pair)]
    up_all = [shift(after(one, y_own), "pair", q) if q else one for q in range(n_pair) for one in up_back]
    rows = tok // sites
    of_site = lambda width: pl.BlockSpec((1, rank, width), lambda i: (i, 0, 0))
    out_rows = pl.BlockSpec((rows, cols), lambda i: (i, 0))
    down_grad, up_grad, y = call(
        functools.partial(last_kernel, n_pair, n_pair * n_dp, n_mp), "last",
        [shape(sites, rank, feat, dtype=F32), shape(sites, rank, cols, dtype=F32), shape(tok, cols)],
        [whole(*picks.shape)] + [of_site(feat)] * n_pair + [whole(rank, cols)] * (n_pair * n_dp) + [out_rows] * n_mp,
        [of_site(feat), of_site(cols), out_rows], grid=(sites,),
    )(picks, *both, *up_all, y_own, *y_got)
    return y, back, down_grad.transpose(0, 2, 1), up_grad


def solution(mesh):
    rows = P(("groups", "dp", "pair"), "mp")
    in_specs = (
        rows,
        P(None, "mp"),
        P(("groups", "dp"), "mp", None),
        P(("groups", "dp"), None, "mp"),
        rows,
        P(("groups", "dp", "pair")),
        P(("groups", "dp"), None, None),
    )
    out_specs = (rows, rows, P(("groups", "dp"), "mp", None), P(("groups", "dp"), None, "mp"))
    return jax.shard_map(shards, mesh=mesh, in_specs=in_specs, out_specs=out_specs, check_vma=False)
```

```python
import functools

import jax
import jax.numpy as jnp
from jax import lax
from jax.experimental import pallas as pl
from jax.experimental.pallas import tpu as pltpu
from jax.sharding import PartitionSpec as P

SCALE = 2.0
TILES = 3
GRAD_COST = 15_000_000_000
F32 = jnp.float32
BF16 = jnp.bfloat16
SMEM = pl.BlockSpec(memory_space=pltpu.SMEM)
VMEM = pl.BlockSpec(memory_space=pltpu.VMEM)
ANY = pl.BlockSpec(memory_space=pl.ANY)


def shape(*dims, dtype=BF16):
    return jax.ShapeDtypeStruct(dims, dtype)


def call(kernel, name, out_shape, in_specs, out_specs, scratch=(), grid=(), mib=32, flops=1):
    return pl.pallas_call(
        kernel, name=name, out_shape=out_shape, grid=grid, in_specs=in_specs, out_specs=out_specs,
        scratch_shapes=scratch,
        compiler_params=pltpu.CompilerParams(vmem_limit_bytes=mib * 1024 * 1024),
        cost_estimate=pl.CostEstimate(flops=flops, bytes_accessed=1, transcendentals=0),
    )


def shift(value, axis, by):
    size = lax.axis_size(axis)
    return lax.ppermute(value, axis, [(i, (i + by) % size) for i in range(size)])


def swap(value, axis, mask):
    return lax.ppermute(value, axis, [(i, i ^ mask) for i in range(lax.axis_size(axis))])


def after(value, *others):
    return lax.optimization_barrier((value, *others))[0]


def nn(a, b):
    return lax.dot_general(a, b, (((1,), (0,)), ((), ())), preferred_element_type=F32)


def nt(a, b):
    return lax.dot_general(a, b, (((1,), (1,)), ((), ())), preferred_element_type=F32)


def tn(a, b):
    return lax.dot_general(a, b, (((0,), (0,)), ((), ())), preferred_element_type=F32)


def wanted_site(table, n_dp, s, q=0):
    n_pair = lax.axis_size("pair")
    core = lax.rem(lax.axis_index("pair") + n_pair - q, n_pair)
    return table[0, core, lax.bitwise_xor(lax.axis_index("dp"), s)]


def slot_of(owner, b, n_dp):
    return lax.bitwise_xor(lax.axis_index("dp"), owner[b])


def pack_kernel(n_dp, n_mp, n_pair, table, down, up, w, *refs):
    away = n_dp - 1
    ups, downs, pieces, rows, sem = refs[:away], refs[away:2 * away], refs[2 * away:-2], refs[-2], refs[-1]
    feat = w.shape[0] // n_mp
    part = feat // n_pair
    fetches, copies = [], []
    for s in range(1, n_mp):
        row = lax.rem(lax.axis_index("mp") + s, n_mp) * feat + lax.axis_index("pair") * part
        row = pl.multiple_of(row, part)
        fetches.append(pltpu.make_async_copy(w.at[pl.ds(row, part)], rows.at[s - 1], sem.at[s - 1]))
        fetches[-1].start()
    for s in range(away):
        site = wanted_site(table, n_dp, s + 1)
        copies.append(pltpu.make_async_copy(up.at[site], ups[s], sem.at[n_mp - 1 + s]))
        copies.append(pltpu.make_async_copy(down.at[site], downs[s], sem.at[n_mp - 1 + away + s]))
    for copy in copies:
        copy.start()
    for s, fetch in enumerate(fetches):
        fetch.wait()
        copies.append(pltpu.make_async_copy(rows.at[s], pieces[s], sem.at[n_mp - 1 + 2 * away + s]))
        copies[-1].start()
    for copy in copies:
        copy.wait()


def gather_maps(n_dp, table, own, gots, wide):
    rank = own.shape[1]
    wide[:rank, :] = own[wanted_site(table, n_dp, 0)]
    for s in range(1, n_dp):
        wide[s * rank:(s + 1) * rank, :] = gots[s - 1][...]


def reduce_kernel(n_dp, owner, table, act, _, own, *refs):
    gots, out, wide = refs[:n_dp - 1], refs[n_dp - 1], refs[n_dp]
    rank = own.shape[1]
    blocks = owner.shape[0]
    rows = act.shape[0] // blocks
    gather_maps(n_dp, table, own, gots, wide)
    full = nt(act[...], wide[...])
    lane_slot = lax.broadcasted_iota(jnp.int32, (rows, n_dp * rank), 1) // rank
    folded = []
    for b in range(blocks):
        kept = jnp.where(lane_slot == slot_of(owner, b, n_dp), full[b * rows:(b + 1) * rows], 0.0)
        total = kept[:, :rank]
        for s in range(1, n_dp):
            total = total + kept[:, s * rank:(s + 1) * rank]
        folded.append(total)
    for j in range(blocks // 2):
        pair = jnp.concatenate([folded[2 * j], folded[2 * j + 1]], axis=1)
        out[j * rows:(j + 1) * rows, :] = pair.astype(BF16)


def grad_kernel(n_dp, n_part, n_behind, owner, act, *refs):
    refs = refs[n_behind:]
    parts, grads, wide = refs[:n_part], refs[n_part:n_part + n_dp], refs[n_part + n_dp]
    rank = wide.shape[1] // n_dp
    blocks = owner.shape[0]
    rows = act.shape[0] // blocks
    total = parts[0][...].astype(F32)
    for part in parts[1:]:
        total = total + part[...].astype(F32)
    lane_slot = lax.broadcasted_iota(jnp.int32, (rows, n_dp * rank), 1) // rank
    for b in range(blocks):
        one = total[(b // 2) * rows:(b // 2 + 1) * rows, (b % 2) * rank:(b % 2 + 1) * rank]
        spread = jnp.concatenate([one] * n_dp, axis=1)
        kept = jnp.where(lane_slot == slot_of(owner, b, n_dp), spread, 0.0)
        wide[b * rows:(b + 1) * rows, :] = kept.astype(BF16)
    full = tn(wide[...], act[...])
    for s in range(n_dp):
        grads[s][...] = full[s * rank:(s + 1) * rank].astype(BF16)


def send_kernel(n_pair, feat, n_mp, _, __, x, *refs):
    n_other = n_mp - 1
    pieces, outs, rows = refs[:n_other * n_pair], refs[n_other * n_pair:n_other * n_pair + n_other], refs[-n_other:]
    part = feat // n_pair

    @pl.when(pl.program_id(0) == 0)
    def _():
        for s in range(n_other):
            for q in range(n_pair):
                at = lax.rem(lax.axis_index("pair") + n_pair - q, n_pair) * part
                rows[s][pl.ds(pl.multiple_of(at, part), part), :] = pieces[s * n_pair + q][...]

    for s in range(n_other):
        outs[s][...] = nn(x[...], rows[s][...]).astype(BF16)


def back_kernel(n_dp, n_mp, table, *refs):
    w, gys, rows, wide, own_down, downs, out, picks, own, maps = (
        refs[0], refs[1:1 + n_mp], refs[1 + n_mp:2 * n_mp], refs[2 * n_mp], refs[2 * n_mp + 1],
        refs[2 * n_mp + 2:-4], refs[-4], refs[-3], refs[-2], refs[-1],
    )
    feat = out.shape[1]

    @pl.when(pl.program_id(0) == 0)
    def _():
        row = lax.broadcasted_iota(jnp.int32, picks.shape, 0)
        sites = jnp.zeros(picks.shape, jnp.int32)
        for k in range(n_dp * lax.axis_size("pair")):
            sites = jnp.where(row == k, wanted_site(table, n_dp, k % n_dp, k // n_dp), sites)
        picks[...] = sites
        own[...] = w[pl.ds(pl.multiple_of(lax.axis_index("mp") * feat, feat), feat), :]
        gather_maps(n_dp, table, own_down, downs, maps)

    total = nt(gys[0][...], own[...]) + SCALE * nn(wide[...], maps[...])
    for gy, row in zip(gys[1:], rows):
        total = total + nt(gy[...], row[...])
    out[...] = total.astype(BF16)


def own_kernel(n_dp, table, w, x, wide, own_up, *refs):
    ups, out, maps = refs[:n_dp - 1], refs[n_dp - 1], refs[n_dp]
    feat = x.shape[1]

    @pl.when(pl.program_id(0) == 0)
    def _():
        gather_maps(n_dp, table, own_up, ups, maps)

    own = w[pl.ds(pl.multiple_of(lax.axis_index("mp") * feat, feat), feat), :]
    out[...] = (nn(x[...], own) + SCALE * nn(wide[...], maps[...])).astype(BF16)


def pick_sum(grads, picks, site):
    total = jnp.zeros(grads[0].shape, F32)
    for k, grad in enumerate(grads):
        total = total + jnp.where(picks[k:k + 1, :1] == site, grad[...].astype(F32), 0.0)
    return total


def site_kernel(picks, _, *refs):
    grads, out = refs[:-1], refs[-1]
    for site in range(out.shape[0]):
        out[site] = pick_sum(grads, picks, site).astype(BF16)


def last_kernel(n_pair, n_ups, n_mp, picks, *refs):
    downs, ups, parts = refs[:n_pair], refs[n_pair:n_pair + n_ups], refs[n_pair + n_ups:n_pair + n_ups + n_mp]
    down, up, y = refs[-3:]
    total = downs[0][0].astype(F32)
    for part in downs[1:]:
        total = total + part[0].astype(F32)
    down[0] = SCALE * total
    up[0] = SCALE * pick_sum(ups, picks, pl.program_id(0))
    total = parts[0][...].astype(F32)
    for part in parts[1:]:
        total = total + part[...].astype(F32)
    y[...] = total.astype(BF16)


def shards(x, w, down, up, gy, owner, table):
    tok, feat = x.shape
    cols = w.shape[1]
    sites, rank = up.shape[:2]
    n_dp, n_mp, n_pair = (lax.axis_size(a) for a in ("dp", "mp", "pair"))
    n_other = n_mp - 1
    down = down.transpose(0, 2, 1)
    part = feat // n_pair
    tile = tok // TILES
    row_block = lambda width: pl.BlockSpec((tile, width), lambda i: (i, 0))
    whole = lambda *dims: pl.BlockSpec(dims, lambda i: (0,) * len(dims))

    away = n_dp - 1
    packed = call(
        functools.partial(pack_kernel, n_dp, n_mp, n_pair), "pack",
        [shape(rank, cols)] * away + [shape(rank, feat)] * away + [shape(part, cols)] * n_other,
        [SMEM, VMEM, VMEM, ANY], [ANY] * (2 * away + n_other),
        [pltpu.VMEM((n_other, part, cols), BF16), pltpu.SemaphoreType.DMA((2 * away + 2 * n_other,))], mib=60,
    )(table, down, up, w)
    pieces = [shift(packed[2 * away + s - 1], "mp", s) for s in range(1, n_mp)]
    ups = [swap(packed[s - 1], "dp", s) for s in range(1, n_dp)]
    downs = [swap(after(packed[away + s - 1], ups[away - 1]), "dp", s) for s in range(1, n_dp)]

    def low_rank(act, own, maps, behind, name):
        mine = call(
            functools.partial(reduce_kernel, n_dp), name + "_part",
            shape(tok // 2, 2 * rank), [SMEM, SMEM, VMEM, ANY] + [VMEM] * n_dp, VMEM,
            [pltpu.VMEM((n_dp * rank, act.shape[1]), BF16)],
        )(owner, table, act, behind, own, *maps)
        return [mine] + [shift(mine, "mp", s) for s in range(1, n_mp)]

    def gradient(act, parts, behind, name, flops):
        *grads, wide = call(
            functools.partial(grad_kernel, n_dp, n_mp, len(behind)), name + "_grad",
            [shape(rank, act.shape[1])] * n_dp + [shape(tok, n_dp * rank)],
            [SMEM, VMEM] + [ANY] * len(behind) + [VMEM] * n_mp, [VMEM] * (n_dp + 1), flops=flops,
        )(owner, act, *behind, *parts)
        return [grads[0]] + [swap(grads[s], "dp", s) for s in range(1, n_dp)], wide

    h_parts = low_rank(gy, up, ups, ups[0], "h")
    gy_got = [shift(after(gy, *pieces), "mp", s) for s in range(1, n_mp)]
    down_back, h_wide = gradient(x, h_parts, downs, "down", GRAD_COST)
    u_parts = low_rank(x, down, downs, h_wide, "u")

    parts = []
    for piece in pieces:
        parts += [piece] + [shift(after(piece, h_wide), "pair", q) for q in range(1, n_pair)]
    sent = call(
        functools.partial(send_kernel, n_pair, feat, n_mp), "y_send",
        [shape(tok, cols)] * n_other + [shape(feat, cols)] * n_other,
        [ANY, ANY, row_block(feat)] + [whole(part, cols)] * len(parts),
        [row_block(cols)] * n_other + [whole(feat, cols)] * n_other,
        grid=(TILES,),
    )(u_parts[0], down_back[1], x, *parts)
    w_rows = sent[n_other:]
    y_got = [shift(sent[s - 1], "mp", n_mp - s) for s in range(1, n_mp)]
    back, picks = call(
        functools.partial(back_kernel, n_dp, n_mp), "back",
        [shape(tok, feat), shape(-(-n_dp * n_pair // 8) * 8, 128, dtype=jnp.int32)],
        [SMEM, whole(*w.shape)] + [row_block(cols)] * n_mp + [whole(feat, cols)] * n_other
        + [row_block(n_dp * rank), whole(*down.shape)] + [whole(rank, feat)] * away,
        [row_block(feat), whole(-(-n_dp * n_pair // 8) * 8, 128)],
        [pltpu.VMEM((feat, cols), BF16), pltpu.VMEM((n_dp * rank, feat), BF16)], grid=(TILES,),
    )(table, w, gy, *gy_got, *w_rows, h_wide, down, *downs)
    up_back, u_wide = gradient(gy, u_parts, [picks] + down_back[1:] + gy_got, "up", GRAD_COST)

    y_own = call(
        functools.partial(own_kernel, n_dp), "y_own", shape(tok, cols),
        [SMEM, whole(*w.shape), row_block(feat), row_block(n_dp * rank), whole(*up.shape)]
        + [whole(rank, cols)] * away,
        row_block(cols), [pltpu.VMEM((n_dp * rank, cols), BF16)], grid=(TILES,), flops=GRAD_COST,
    )(table, w, x, u_wide, up, *ups)

    summed = call(
        site_kernel, "sites", shape(sites, rank, feat), [VMEM, ANY] + [VMEM] * n_dp, VMEM,
    )(picks, up_back[0], *down_back)
    both = [summed] + [shift(summed, "pair", q) for q in range(1, n_pair)]
    up_all = [shift(after(one, y_own), "pair", q) if q else one for q in range(n_pair) for one in up_back]
    rows = tok // sites
    of_site = lambda width: pl.BlockSpec((1, rank, width), lambda i: (i, 0, 0))
    out_rows = pl.BlockSpec((rows, cols), lambda i: (i, 0))
    down_grad, up_grad, y = call(
        functools.partial(last_kernel, n_pair, n_pair * n_dp, n_mp), "last",
        [shape(sites, rank, feat, dtype=F32), shape(sites, rank, cols, dtype=F32), shape(tok, cols)],
        [whole(*picks.shape)] + [of_site(feat)] * n_pair + [whole(rank, cols)] * (n_pair * n_dp) + [out_rows] * n_mp,
        [of_site(feat), of_site(cols), out_rows], grid=(sites,),
    )(picks, *both, *up_all, y_own, *y_got)
    return y, back, down_grad.transpose(0, 2, 1), up_grad


def solution(mesh):
    rows = P(("groups", "dp", "pair"), "mp")
    in_specs = (
        rows,
        P(None, "mp"),
        P(("groups", "dp"), "mp", None),
        P(("groups", "dp"), None, "mp"),
        rows,
        P(("groups", "dp", "pair")),
        P(("groups", "dp"), None, None),
    )
    out_specs = (rows, rows, P(("groups", "dp"), "mp", None), P(("groups", "dp"), None, "mp"))
    return jax.shard_map(shards, mesh=mesh, in_specs=in_specs, out_specs=out_specs, check_vma=False)
```

```python
import functools

import jax
import jax.numpy as jnp
from jax import lax
from jax.experimental import pallas as pl
from jax.experimental.pallas import tpu as pltpu
from jax.sharding import PartitionSpec as P

SCALE = 2.0
TILES = 3
GRAD_COST = 15_000_000_000
F32 = jnp.float32
BF16 = jnp.bfloat16
SMEM = pl.BlockSpec(memory_space=pltpu.SMEM)
VMEM = pl.BlockSpec(memory_space=pltpu.VMEM)
ANY = pl.BlockSpec(memory_space=pl.ANY)


def shape(*dims, dtype=BF16):
    return jax.ShapeDtypeStruct(dims, dtype)


def call(kernel, name, out_shape, in_specs, out_specs, scratch=(), grid=(), mib=32, flops=1):
    return pl.pallas_call(
        kernel, name=name, out_shape=out_shape, grid=grid, in_specs=in_specs, out_specs=out_specs,
        scratch_shapes=scratch,
        compiler_params=pltpu.CompilerParams(vmem_limit_bytes=mib * 1024 * 1024),
        cost_estimate=pl.CostEstimate(flops=flops, bytes_accessed=1, transcendentals=0),
    )


def shift(value, axis, by):
    size = lax.axis_size(axis)
    return lax.ppermute(value, axis, [(i, (i + by) % size) for i in range(size)])


def swap(value, axis, mask):
    return lax.ppermute(value, axis, [(i, i ^ mask) for i in range(lax.axis_size(axis))])


def after(value, *others):
    return lax.optimization_barrier((value, *others))[0]


def nn(a, b):
    return lax.dot_general(a, b, (((1,), (0,)), ((), ())), preferred_element_type=F32)


def nt(a, b):
    return lax.dot_general(a, b, (((1,), (1,)), ((), ())), preferred_element_type=F32)


def tn(a, b):
    return lax.dot_general(a, b, (((0,), (0,)), ((), ())), preferred_element_type=F32)


def wanted_site(table, n_dp, s, q=0):
    n_pair = lax.axis_size("pair")
    core = lax.rem(lax.axis_index("pair") + n_pair - q, n_pair)
    return table[0, core, lax.bitwise_xor(lax.axis_index("dp"), s)]


def slot_of(owner, b, n_dp):
    return lax.bitwise_xor(lax.axis_index("dp"), owner[b])


def pack_kernel(n_dp, n_mp, n_pair, table, down, up, w, *refs):
    away = n_dp - 1
    ups, downs, pieces, rows, sem = refs[:away], refs[away:2 * away], refs[2 * away:-2], refs[-2], refs[-1]
    feat = w.shape[0] // n_mp
    part = feat // n_pair
    fetches, copies = [], []
    for s in range(1, n_mp):
        row = lax.rem(lax.axis_index("mp") + s, n_mp) * feat + lax.axis_index("pair") * part
        row = pl.multiple_of(row, part)
        fetches.append(pltpu.make_async_copy(w.at[pl.ds(row, part)], rows.at[s - 1], sem.at[s - 1]))
        fetches[-1].start()
    for s in range(away):
        site = wanted_site(table, n_dp, s + 1)
        copies.append(pltpu.make_async_copy(up.at[site], ups[s], sem.at[n_mp - 1 + s]))
        copies.append(pltpu.make_async_copy(down.at[site], downs[s], sem.at[n_mp - 1 + away + s]))
    for copy in copies:
        copy.start()
    for s, fetch in enumerate(fetches):
        fetch.wait()
        copies.append(pltpu.make_async_copy(rows.at[s], pieces[s], sem.at[n_mp - 1 + 2 * away + s]))
        copies[-1].start()
    for copy in copies:
        copy.wait()


def gather_maps(n_dp, table, own, gots, wide):
    rank = own.shape[1]
    wide[:rank, :] = own[wanted_site(table, n_dp, 0)]
    for s in range(1, n_dp):
        wide[s * rank:(s + 1) * rank, :] = gots[s - 1][...]


def reduce_kernel(n_dp, owner, table, act, _, own, *refs):
    gots, out, wide = refs[:n_dp - 1], refs[n_dp - 1], refs[n_dp]
    rank = own.shape[1]
    blocks = owner.shape[0]
    rows = act.shape[0] // blocks
    gather_maps(n_dp, table, own, gots, wide)
    full = nt(act[...], wide[...])
    lane_slot = lax.broadcasted_iota(jnp.int32, (rows, n_dp * rank), 1) // rank
    folded = []
    for b in range(blocks):
        kept = jnp.where(lane_slot == slot_of(owner, b, n_dp), full[b * rows:(b + 1) * rows], 0.0)
        total = kept[:, :rank]
        for s in range(1, n_dp):
            total = total + kept[:, s * rank:(s + 1) * rank]
        folded.append(total)
    for j in range(blocks // 2):
        pair = jnp.concatenate([folded[2 * j], folded[2 * j + 1]], axis=1)
        out[j * rows:(j + 1) * rows, :] = pair.astype(BF16)


def grad_kernel(n_dp, n_part, n_behind, owner, act, *refs):
    refs = refs[n_behind:]
    parts, grads, wide = refs[:n_part], refs[n_part:n_part + n_dp], refs[n_part + n_dp]
    rank = wide.shape[1] // n_dp
    blocks = owner.shape[0]
    rows = act.shape[0] // blocks
    total = parts[0][...].astype(F32)
    for part in parts[1:]:
        total = total + part[...].astype(F32)
    lane_slot = lax.broadcasted_iota(jnp.int32, (rows, n_dp * rank), 1) // rank
    for b in range(blocks):
        one = total[(b // 2) * rows:(b // 2 + 1) * rows, (b % 2) * rank:(b % 2 + 1) * rank]
        spread = jnp.concatenate([one] * n_dp, axis=1)
        kept = jnp.where(lane_slot == slot_of(owner, b, n_dp), spread, 0.0)
        wide[b * rows:(b + 1) * rows, :] = kept.astype(BF16)
    full = tn(wide[...], act[...])
    for s in range(n_dp):
        grads[s][...] = full[s * rank:(s + 1) * rank].astype(BF16)


def send_kernel(n_pair, feat, n_mp, _, __, x, *refs):
    n_other = n_mp - 1
    pieces, outs, rows = refs[:n_other * n_pair], refs[n_other * n_pair:n_other * n_pair + n_other], refs[-n_other:]
    part = feat // n_pair

    @pl.when(pl.program_id(0) == 0)
    def _():
        for s in range(n_other):
            for q in range(n_pair):
                at = lax.rem(lax.axis_index("pair") + n_pair - q, n_pair) * part
                rows[s][pl.ds(pl.multiple_of(at, part), part), :] = pieces[s * n_pair + q][...]

    for s in range(n_other):
        outs[s][...] = nn(x[...], rows[s][...]).astype(BF16)


def back_kernel(n_dp, n_mp, table, *refs):
    w, gys, rows, wide, own_down, downs, out, picks, own, maps = (
        refs[0], refs[1:1 + n_mp], refs[1 + n_mp:2 * n_mp], refs[2 * n_mp], refs[2 * n_mp + 1],
        refs[2 * n_mp + 2:-4], refs[-4], refs[-3], refs[-2], refs[-1],
    )
    feat = out.shape[1]

    @pl.when(pl.program_id(0) == 0)
    def _():
        row = lax.broadcasted_iota(jnp.int32, picks.shape, 0)
        sites = jnp.zeros(picks.shape, jnp.int32)
        for k in range(n_dp * lax.axis_size("pair")):
            sites = jnp.where(row == k, wanted_site(table, n_dp, k % n_dp, k // n_dp), sites)
        picks[...] = sites
        own[...] = w[pl.ds(pl.multiple_of(lax.axis_index("mp") * feat, feat), feat), :]
        gather_maps(n_dp, table, own_down, downs, maps)

    total = nt(gys[0][...], own[...]) + SCALE * nn(wide[...], maps[...])
    for gy, row in zip(gys[1:], rows):
        total = total + nt(gy[...], row[...])
    out[...] = total.astype(BF16)


def own_kernel(n_dp, table, w, x, wide, own_up, *refs):
    ups, out, maps = refs[:n_dp - 1], refs[n_dp - 1], refs[n_dp]
    feat = x.shape[1]

    @pl.when(pl.program_id(0) == 0)
    def _():
        gather_maps(n_dp, table, own_up, ups, maps)

    own = w[pl.ds(pl.multiple_of(lax.axis_index("mp") * feat, feat), feat), :]
    out[...] = (nn(x[...], own) + SCALE * nn(wide[...], maps[...])).astype(BF16)


def pick_sum(grads, picks, site):
    total = jnp.zeros(grads[0].shape, F32)
    for k, grad in enumerate(grads):
        total = total + jnp.where(picks[k:k + 1, :1] == site, grad[...].astype(F32), 0.0)
    return total


def site_kernel(picks, _, *refs):
    grads, out = refs[:-1], refs[-1]
    for site in range(out.shape[0]):
        out[site] = pick_sum(grads, picks, site).astype(BF16)


def last_kernel(n_pair, n_ups, n_mp, picks, *refs):
    downs, ups, parts = refs[:n_pair], refs[n_pair:n_pair + n_ups], refs[n_pair + n_ups:n_pair + n_ups + n_mp]
    down, up, y = refs[-3:]
    total = downs[0][0].astype(F32)
    for part in downs[1:]:
        total = total + part[0].astype(F32)
    down[0] = SCALE * total
    up[0] = SCALE * pick_sum(ups, picks, pl.program_id(0))
    total = parts[0][...].astype(F32)
    for part in parts[1:]:
        total = total + part[...].astype(F32)
    y[...] = total.astype(BF16)


def shards(x, w, down, up, gy, owner, table):
    tok, feat = x.shape
    cols = w.shape[1]
    sites, rank = up.shape[:2]
    n_dp, n_mp, n_pair = (lax.axis_size(a) for a in ("dp", "mp", "pair"))
    n_other = n_mp - 1
    down = down.transpose(0, 2, 1)
    part = feat // n_pair
    tile = tok // TILES
    row_block = lambda width: pl.BlockSpec((tile, width), lambda i: (i, 0))
    whole = lambda *dims: pl.BlockSpec(dims, lambda i: (0,) * len(dims))

    away = n_dp - 1
    packed = call(
        functools.partial(pack_kernel, n_dp, n_mp, n_pair), "pack",
        [shape(rank, cols)] * away + [shape(rank, feat)] * away + [shape(part, cols)] * n_other,
        [SMEM, VMEM, VMEM, ANY], [ANY] * (2 * away + n_other),
        [pltpu.VMEM((n_other, part, cols), BF16), pltpu.SemaphoreType.DMA((2 * away + 2 * n_other,))], mib=60,
    )(table, down, up, w)
    pieces = [shift(packed[2 * away + s - 1], "mp", s) for s in range(1, n_mp)]
    ups = [swap(packed[s - 1], "dp", s) for s in range(1, n_dp)]
    downs = [swap(after(packed[away + s - 1], ups[away - 1]), "dp", s) for s in range(1, n_dp)]

    def low_rank(act, own, maps, behind, name):
        mine = call(
            functools.partial(reduce_kernel, n_dp), name + "_part",
            shape(tok // 2, 2 * rank), [SMEM, SMEM, VMEM, ANY] + [VMEM] * n_dp, VMEM,
            [pltpu.VMEM((n_dp * rank, act.shape[1]), BF16)],
        )(owner, table, act, behind, own, *maps)
        return [mine] + [shift(mine, "mp", s) for s in range(1, n_mp)]

    def gradient(act, parts, behind, name, flops):
        *grads, wide = call(
            functools.partial(grad_kernel, n_dp, n_mp, len(behind)), name + "_grad",
            [shape(rank, act.shape[1])] * n_dp + [shape(tok, n_dp * rank)],
            [SMEM, VMEM] + [ANY] * len(behind) + [VMEM] * n_mp, [VMEM] * (n_dp + 1), flops=flops,
        )(owner, act, *behind, *parts)
        return [grads[0]] + [swap(grads[s], "dp", s) for s in range(1, n_dp)], wide

    h_parts = low_rank(gy, up, ups, ups[0], "h")
    gy_got = [shift(after(gy, *pieces), "mp", s) for s in range(1, n_mp)]
    down_back, h_wide = gradient(x, h_parts, downs, "down", GRAD_COST)
    parts = []
    for piece in pieces:
        parts += [piece] + [shift(after(piece, h_wide), "pair", q) for q in range(1, n_pair)]
    u_parts = low_rank(x, down, downs, parts[-1], "u")


    sent = call(
        functools.partial(send_kernel, n_pair, feat, n_mp), "y_send",
        [shape(tok, cols)] * n_other + [shape(feat, cols)] * n_other,
        [ANY, ANY, row_block(feat)] + [whole(part, cols)] * len(parts),
        [row_block(cols)] * n_other + [whole(feat, cols)] * n_other,
        grid=(TILES,),
    )(u_parts[0], h_wide, x, *parts)
    w_rows = sent[n_other:]
    y_got = [shift(after(sent[s - 1], down_back[1]), "mp", n_mp - s) for s in range(1, n_mp)]
    back, picks = call(
        functools.partial(back_kernel, n_dp, n_mp), "back",
        [shape(tok, feat), shape(-(-n_dp * n_pair // 8) * 8, 128, dtype=jnp.int32)],
        [SMEM, whole(*w.shape)] + [row_block(cols)] * n_mp + [whole(feat, cols)] * n_other
        + [row_block(n_dp * rank), whole(*down.shape)] + [whole(rank, feat)] * away,
        [row_block(feat), whole(-(-n_dp * n_pair // 8) * 8, 128)],
        [pltpu.VMEM((feat, cols), BF16), pltpu.VMEM((n_dp * rank, feat), BF16)], grid=(TILES,),
    )(table, w, gy, *gy_got, *w_rows, h_wide, down, *downs)
    up_back, u_wide = gradient(gy, u_parts, [picks] + down_back[1:] + gy_got, "up", GRAD_COST)

    y_own = call(
        functools.partial(own_kernel, n_dp), "y_own", shape(tok, cols),
        [SMEM, whole(*w.shape), row_block(feat), row_block(n_dp * rank), whole(*up.shape)]
        + [whole(rank, cols)] * away,
        row_block(cols), [pltpu.VMEM((n_dp * rank, cols), BF16)], grid=(TILES,), flops=GRAD_COST,
    )(table, w, x, u_wide, up, *ups)

    summed = call(
        site_kernel, "sites", shape(sites, rank, feat), [VMEM, ANY] + [VMEM] * n_dp, VMEM,
    )(picks, up_back[0], *down_back)
    both = [summed] + [shift(summed, "pair", q) for q in range(1, n_pair)]
    up_all = [shift(after(one, y_own), "pair", q) if q else one for q in range(n_pair) for one in up_back]
    rows = tok // sites
    of_site = lambda width: pl.BlockSpec((1, rank, width), lambda i: (i, 0, 0))
    out_rows = pl.BlockSpec((rows, cols), lambda i: (i, 0))
    down_grad, up_grad, y = call(
        functools.partial(last_kernel, n_pair, n_pair * n_dp, n_mp), "last",
        [shape(sites, rank, feat, dtype=F32), shape(sites, rank, cols, dtype=F32), shape(tok, cols)],
        [whole(*picks.shape)] + [of_site(feat)] * n_pair + [whole(rank, cols)] * (n_pair * n_dp) + [out_rows] * n_mp,
        [of_site(feat), of_site(cols), out_rows], grid=(sites,),
    )(picks, *both, *up_all, y_own, *y_got)
    return y, back, down_grad.transpose(0, 2, 1), up_grad


def solution(mesh):
    rows = P(("groups", "dp", "pair"), "mp")
    in_specs = (
        rows,
        P(None, "mp"),
        P(("groups", "dp"), "mp", None),
        P(("groups", "dp"), None, "mp"),
        rows,
        P(("groups", "dp", "pair")),
        P(("groups", "dp"), None, None),
    )
    out_specs = (rows, rows, P(("groups", "dp"), "mp", None), P(("groups", "dp"), None, "mp"))
    return jax.shard_map(shards, mesh=mesh, in_specs=in_specs, out_specs=out_specs, check_vma=False)
```

```python
import functools

import jax
import jax.numpy as jnp
from jax import lax
from jax.experimental import pallas as pl
from jax.experimental.pallas import tpu as pltpu
from jax.sharding import PartitionSpec as P

SCALE = 2.0
TILES = 3
GRAD_COST = 15_000_000_000
F32 = jnp.float32
BF16 = jnp.bfloat16
SMEM = pl.BlockSpec(memory_space=pltpu.SMEM)
VMEM = pl.BlockSpec(memory_space=pltpu.VMEM)
ANY = pl.BlockSpec(memory_space=pl.ANY)


def shape(*dims, dtype=BF16):
    return jax.ShapeDtypeStruct(dims, dtype)


def call(kernel, name, out_shape, in_specs, out_specs, scratch=(), grid=(), mib=32, flops=1):
    return pl.pallas_call(
        kernel, name=name, out_shape=out_shape, grid=grid, in_specs=in_specs, out_specs=out_specs,
        scratch_shapes=scratch,
        compiler_params=pltpu.CompilerParams(vmem_limit_bytes=mib * 1024 * 1024),
        cost_estimate=pl.CostEstimate(flops=flops, bytes_accessed=1, transcendentals=0),
    )


def shift(value, axis, by):
    size = lax.axis_size(axis)
    return lax.ppermute(value, axis, [(i, (i + by) % size) for i in range(size)])


def swap(value, axis, mask):
    return lax.ppermute(value, axis, [(i, i ^ mask) for i in range(lax.axis_size(axis))])


def after(value, *others):
    return lax.optimization_barrier((value, *others))[0]


def nn(a, b):
    return lax.dot_general(a, b, (((1,), (0,)), ((), ())), preferred_element_type=F32)


def nt(a, b):
    return lax.dot_general(a, b, (((1,), (1,)), ((), ())), preferred_element_type=F32)


def tn(a, b):
    return lax.dot_general(a, b, (((0,), (0,)), ((), ())), preferred_element_type=F32)


def wanted_site(table, n_dp, s, q=0):
    n_pair = lax.axis_size("pair")
    core = lax.rem(lax.axis_index("pair") + n_pair - q, n_pair)
    return table[0, core, lax.bitwise_xor(lax.axis_index("dp"), s)]


def slot_of(owner, b, n_dp):
    return lax.bitwise_xor(lax.axis_index("dp"), owner[b])


def pack_kernel(n_dp, n_mp, table, down, up, *refs):
    away, n_other = n_dp - 1, n_mp - 1
    rows, refs, sem = refs[:n_other], refs[n_other:-1], refs[-1]
    ups, downs, pieces = refs[:away], refs[away:2 * away], refs[2 * away:]
    copies = [pltpu.make_async_copy(rows[s], pieces[s], sem.at[s]) for s in range(n_other)]
    for s in range(away):
        site = wanted_site(table, n_dp, s + 1)
        copies.append(pltpu.make_async_copy(up.at[site], ups[s], sem.at[n_other + s]))
        copies.append(pltpu.make_async_copy(down.at[site], downs[s], sem.at[n_other + away + s]))
    for copy in copies:
        copy.start()
    for copy in copies:
        copy.wait()


def gather_maps(n_dp, table, own, gots, wide):
    rank = own.shape[1]
    wide[:rank, :] = own[wanted_site(table, n_dp, 0)]
    for s in range(1, n_dp):
        wide[s * rank:(s + 1) * rank, :] = gots[s - 1][...]


def reduce_kernel(n_dp, owner, table, act, _, own, *refs):
    gots, out, wide = refs[:n_dp - 1], refs[n_dp - 1], refs[n_dp]
    rank = own.shape[1]
    blocks = owner.shape[0]
    rows = act.shape[0] // blocks
    gather_maps(n_dp, table, own, gots, wide)
    full = nt(act[...], wide[...])
    lane_slot = lax.broadcasted_iota(jnp.int32, (rows, n_dp * rank), 1) // rank
    folded = []
    for b in range(blocks):
        kept = jnp.where(lane_slot == slot_of(owner, b, n_dp), full[b * rows:(b + 1) * rows], 0.0)
        total = kept[:, :rank]
        for s in range(1, n_dp):
            total = total + kept[:, s * rank:(s + 1) * rank]
        folded.append(total)
    for j in range(blocks // 2):
        pair = jnp.concatenate([folded[2 * j], folded[2 * j + 1]], axis=1)
        out[j * rows:(j + 1) * rows, :] = pair.astype(BF16)


def grad_kernel(n_dp, n_part, n_behind, owner, act, *refs):
    refs = refs[n_behind:]
    parts, grads, wide = refs[:n_part], refs[n_part:n_part + n_dp], refs[n_part + n_dp]
    rank = wide.shape[1] // n_dp
    blocks = owner.shape[0]
    rows = act.shape[0] // blocks
    total = parts[0][...].astype(F32)
    for part in parts[1:]:
        total = total + part[...].astype(F32)
    lane_slot = lax.broadcasted_iota(jnp.int32, (rows, n_dp * rank), 1) // rank
    for b in range(blocks):
        one = total[(b // 2) * rows:(b // 2 + 1) * rows, (b % 2) * rank:(b % 2 + 1) * rank]
        spread = jnp.concatenate([one] * n_dp, axis=1)
        kept = jnp.where(lane_slot == slot_of(owner, b, n_dp), spread, 0.0)
        wide[b * rows:(b + 1) * rows, :] = kept.astype(BF16)
    full = tn(wide[...], act[...])
    for s in range(n_dp):
        grads[s][...] = full[s * rank:(s + 1) * rank].astype(BF16)


def send_kernel(n_pair, feat, n_mp, _, __, x, *refs):
    n_other = n_mp - 1
    pieces, outs, rows = refs[:n_other * n_pair], refs[n_other * n_pair:n_other * n_pair + n_other], refs[-n_other:]
    part = feat // n_pair

    @pl.when(pl.program_id(0) == 0)
    def _():
        for s in range(n_other):
            for q in range(n_pair):
                at = lax.rem(lax.axis_index("pair") + n_pair - q, n_pair) * part
                rows[s][pl.ds(pl.multiple_of(at, part), part), :] = pieces[s * n_pair + q][...]

    for s in range(n_other):
        outs[s][...] = nn(x[...], rows[s][...]).astype(BF16)


def back_kernel(n_dp, n_mp, table, *refs):
    w, gys, rows, wide, own_down, downs, out, picks, own, maps = (
        refs[0], refs[1:1 + n_mp], refs[1 + n_mp:2 * n_mp], refs[2 * n_mp], refs[2 * n_mp + 1],
        refs[2 * n_mp + 2:-4], refs[-4], refs[-3], refs[-2], refs[-1],
    )
    feat = out.shape[1]

    @pl.when(pl.program_id(0) == 0)
    def _():
        row = lax.broadcasted_iota(jnp.int32, picks.shape, 0)
        sites = jnp.zeros(picks.shape, jnp.int32)
        for k in range(n_dp * lax.axis_size("pair")):
            sites = jnp.where(row == k, wanted_site(table, n_dp, k % n_dp, k // n_dp), sites)
        picks[...] = sites
        own[...] = w[pl.ds(pl.multiple_of(lax.axis_index("mp") * feat, feat), feat), :]
        gather_maps(n_dp, table, own_down, downs, maps)

    total = nt(gys[0][...], own[...]) + SCALE * nn(wide[...], maps[...])
    for gy, row in zip(gys[1:], rows):
        total = total + nt(gy[...], row[...])
    out[...] = total.astype(BF16)


def own_kernel(n_dp, table, w, x, wide, own_up, *refs):
    ups, out, maps = refs[:n_dp - 1], refs[n_dp - 1], refs[n_dp]
    feat = x.shape[1]

    @pl.when(pl.program_id(0) == 0)
    def _():
        gather_maps(n_dp, table, own_up, ups, maps)

    own = w[pl.ds(pl.multiple_of(lax.axis_index("mp") * feat, feat), feat), :]
    out[...] = (nn(x[...], own) + SCALE * nn(wide[...], maps[...])).astype(BF16)


def pick_sum(grads, picks, site):
    total = jnp.zeros(grads[0].shape, F32)
    for k, grad in enumerate(grads):
        total = total + jnp.where(picks[k:k + 1, :1] == site, grad[...].astype(F32), 0.0)
    return total


def site_kernel(picks, _, *refs):
    grads, out = refs[:-1], refs[-1]
    for site in range(out.shape[0]):
        out[site] = pick_sum(grads, picks, site).astype(BF16)


def last_kernel(n_pair, n_ups, n_mp, picks, *refs):
    downs, ups, parts = refs[:n_pair], refs[n_pair:n_pair + n_ups], refs[n_pair + n_ups:n_pair + n_ups + n_mp]
    down, up, y = refs[-3:]
    total = downs[0][0].astype(F32)
    for part in downs[1:]:
        total = total + part[0].astype(F32)
    down[0] = SCALE * total
    up[0] = SCALE * pick_sum(ups, picks, pl.program_id(0))
    total = parts[0][...].astype(F32)
    for part in parts[1:]:
        total = total + part[...].astype(F32)
    y[...] = total.astype(BF16)


def shards(x, w, down, up, gy, owner, table):
    tok, feat = x.shape
    cols = w.shape[1]
    sites, rank = up.shape[:2]
    n_dp, n_mp, n_pair = (lax.axis_size(a) for a in ("dp", "mp", "pair"))
    n_other = n_mp - 1
    down = down.transpose(0, 2, 1)
    part = feat // n_pair
    tile = tok // TILES
    row_block = lambda width: pl.BlockSpec((tile, width), lambda i: (i, 0))
    whole = lambda *dims: pl.BlockSpec(dims, lambda i: (0,) * len(dims))

    away = n_dp - 1
    def sent_rows(s):
        return lambda i: (lax.rem(lax.axis_index("mp") + s, n_mp) * n_pair + lax.axis_index("pair"), 0)

    packed = call(
        functools.partial(pack_kernel, n_dp, n_mp), "pack",
        [shape(rank, cols)] * away + [shape(rank, feat)] * away + [shape(part, cols)] * n_other,
        [SMEM, whole(*down.shape), whole(*up.shape)] + [pl.BlockSpec((part, cols), sent_rows(s)) for s in range(1, n_mp)],
        [ANY] * (2 * away + n_other),
        [pltpu.SemaphoreType.DMA((2 * away + n_other,))], mib=60, grid=(1,),
    )(table, down, up, *[w] * n_other)
    pieces = [shift(packed[2 * away + s - 1], "mp", s) for s in range(1, n_mp)]
    ups = [swap(packed[s - 1], "dp", s) for s in range(1, n_dp)]
    downs = [swap(after(packed[away + s - 1], ups[away - 1]), "dp", s) for s in range(1, n_dp)]

    def low_rank(act, own, maps, behind, name):
        mine = call(
            functools.partial(reduce_kernel, n_dp), name + "_part",
            shape(tok // 2, 2 * rank), [SMEM, SMEM, VMEM, ANY] + [VMEM] * n_dp, VMEM,
            [pltpu.VMEM((n_dp * rank, act.shape[1]), BF16)],
        )(owner, table, act, behind, own, *maps)
        return [mine] + [shift(mine, "mp", s) for s in range(1, n_mp)]

    def gradient(act, parts, behind, name, flops):
        *grads, wide = call(
            functools.partial(grad_kernel, n_dp, n_mp, len(behind)), name + "_grad",
            [shape(rank, act.shape[1])] * n_dp + [shape(tok, n_dp * rank)],
            [SMEM, VMEM] + [ANY] * len(behind) + [VMEM] * n_mp, [VMEM] * (n_dp + 1), flops=flops,
        )(owner, act, *behind, *parts)
        return [grads[0]] + [swap(grads[s], "dp", s) for s in range(1, n_dp)], wide

    h_parts = low_rank(gy, up, ups, ups[0], "h")
    gy_got = [shift(after(gy, *pieces), "mp", s) for s in range(1, n_mp)]
    down_back, h_wide = gradient(x, h_parts, downs, "down", GRAD_COST)
    parts = []
    for piece in pieces:
        parts += [piece] + [shift(after(piece, h_wide), "pair", q) for q in range(1, n_pair)]
    u_parts = low_rank(x, down, downs, parts[-1], "u")


    sent = call(
        functools.partial(send_kernel, n_pair, feat, n_mp), "y_send",
        [shape(tok, cols)] * n_other + [shape(feat, cols)] * n_other,
        [ANY, ANY, row_block(feat)] + [whole(part, cols)] * len(parts),
        [row_block(cols)] * n_other + [whole(feat, cols)] * n_other,
        grid=(TILES,),
    )(u_parts[0], h_wide, x, *parts)
    w_rows = sent[n_other:]
    y_got = [shift(after(sent[s - 1], down_back[1]), "mp", n_mp - s) for s in range(1, n_mp)]
    back, picks = call(
        functools.partial(back_kernel, n_dp, n_mp), "back",
        [shape(tok, feat), shape(-(-n_dp * n_pair // 8) * 8, 128, dtype=jnp.int32)],
        [SMEM, whole(*w.shape)] + [row_block(cols)] * n_mp + [whole(feat, cols)] * n_other
        + [row_block(n_dp * rank), whole(*down.shape)] + [whole(rank, feat)] * away,
        [row_block(feat), whole(-(-n_dp * n_pair // 8) * 8, 128)],
        [pltpu.VMEM((feat, cols), BF16), pltpu.VMEM((n_dp * rank, feat), BF16)], grid=(TILES,),
    )(table, w, gy, *gy_got, *w_rows, h_wide, down, *downs)
    up_back, u_wide = gradient(gy, u_parts, [picks] + down_back[1:] + gy_got, "up", GRAD_COST)

    y_own = call(
        functools.partial(own_kernel, n_dp), "y_own", shape(tok, cols),
        [SMEM, whole(*w.shape), row_block(feat), row_block(n_dp * rank), whole(*up.shape)]
        + [whole(rank, cols)] * away,
        row_block(cols), [pltpu.VMEM((n_dp * rank, cols), BF16)], grid=(TILES,), flops=GRAD_COST,
    )(table, w, x, u_wide, up, *ups)

    summed = call(
        site_kernel, "sites", shape(sites, rank, feat), [VMEM, ANY] + [VMEM] * n_dp, VMEM,
    )(picks, up_back[0], *down_back)
    both = [summed] + [shift(summed, "pair", q) for q in range(1, n_pair)]
    up_all = [shift(after(one, y_own), "pair", q) if q else one for q in range(n_pair) for one in up_back]
    rows = tok // sites
    of_site = lambda width: pl.BlockSpec((1, rank, width), lambda i: (i, 0, 0))
    out_rows = pl.BlockSpec((rows, cols), lambda i: (i, 0))
    down_grad, up_grad, y = call(
        functools.partial(last_kernel, n_pair, n_pair * n_dp, n_mp), "last",
        [shape(sites, rank, feat, dtype=F32), shape(sites, rank, cols, dtype=F32), shape(tok, cols)],
        [whole(*picks.shape)] + [of_site(feat)] * n_pair + [whole(rank, cols)] * (n_pair * n_dp) + [out_rows] * n_mp,
        [of_site(feat), of_site(cols), out_rows], grid=(sites,),
    )(picks, *both, *up_all, y_own, *y_got)
    return y, back, down_grad.transpose(0, 2, 1), up_grad


def solution(mesh):
    rows = P(("groups", "dp", "pair"), "mp")
    in_specs = (
        rows,
        P(None, "mp"),
        P(("groups", "dp"), "mp", None),
        P(("groups", "dp"), None, "mp"),
        rows,
        P(("groups", "dp", "pair")),
        P(("groups", "dp"), None, None),
    )
    out_specs = (rows, rows, P(("groups", "dp"), "mp", None), P(("groups", "dp"), None, "mp"))
    return jax.shard_map(shards, mesh=mesh, in_specs=in_specs, out_specs=out_specs, check_vma=False)
```

```python
import functools

import jax
import jax.numpy as jnp
from jax import lax
from jax.experimental import pallas as pl
from jax.experimental.pallas import tpu as pltpu
from jax.sharding import PartitionSpec as P

SCALE = 2.0
TILES = 3
GRAD_COST = 15_000_000_000
F32 = jnp.float32
BF16 = jnp.bfloat16
SMEM = pl.BlockSpec(memory_space=pltpu.SMEM)
VMEM = pl.BlockSpec(memory_space=pltpu.VMEM)
ANY = pl.BlockSpec(memory_space=pl.ANY)


def shape(*dims, dtype=BF16):
    return jax.ShapeDtypeStruct(dims, dtype)


def call(kernel, name, out_shape, in_specs, out_specs, scratch=(), grid=(), mib=32, flops=1):
    return pl.pallas_call(
        kernel, name=name, out_shape=out_shape, grid=grid, in_specs=in_specs, out_specs=out_specs,
        scratch_shapes=scratch,
        compiler_params=pltpu.CompilerParams(vmem_limit_bytes=mib * 1024 * 1024),
        cost_estimate=pl.CostEstimate(flops=flops, bytes_accessed=1, transcendentals=0),
    )


def shift(value, axis, by):
    size = lax.axis_size(axis)
    return lax.ppermute(value, axis, [(i, (i + by) % size) for i in range(size)])


def swap(value, axis, mask):
    return lax.ppermute(value, axis, [(i, i ^ mask) for i in range(lax.axis_size(axis))])


def after(value, *others):
    return lax.optimization_barrier((value, *others))[0]


def nn(a, b):
    return lax.dot_general(a, b, (((1,), (0,)), ((), ())), preferred_element_type=F32)


def nt(a, b):
    return lax.dot_general(a, b, (((1,), (1,)), ((), ())), preferred_element_type=F32)


def tn(a, b):
    return lax.dot_general(a, b, (((0,), (0,)), ((), ())), preferred_element_type=F32)


def wanted_site(table, n_dp, s, q=0):
    n_pair = lax.axis_size("pair")
    core = lax.rem(lax.axis_index("pair") + n_pair - q, n_pair)
    return table[0, core, lax.bitwise_xor(lax.axis_index("dp"), s)]


def slot_of(owner, b, n_dp):
    return lax.bitwise_xor(lax.axis_index("dp"), owner[b])


def pack_kernel(n_dp, n_mp, table, down, up, *refs):
    away, n_other = n_dp - 1, n_mp - 1
    rows, refs, sem = refs[:n_other], refs[n_other:-1], refs[-1]
    ups, downs, pieces = refs[:away], refs[away:2 * away], refs[2 * away:]
    copies = [pltpu.make_async_copy(rows[s], pieces[s], sem.at[s]) for s in range(n_other)]
    for s in range(away):
        site = wanted_site(table, n_dp, s + 1)
        copies.append(pltpu.make_async_copy(up.at[site], ups[s], sem.at[n_other + s]))
        copies.append(pltpu.make_async_copy(down.at[site], downs[s], sem.at[n_other + away + s]))
    for copy in copies:
        copy.start()
    for copy in copies:
        copy.wait()


def gather_maps(n_dp, table, own, gots, wide):
    rank = own.shape[1]
    wide[:rank, :] = own[wanted_site(table, n_dp, 0)]
    for s in range(1, n_dp):
        wide[s * rank:(s + 1) * rank, :] = gots[s - 1][...]


def reduce_kernel(n_dp, owner, table, act, _, own, *refs):
    gots, out, wide = refs[:n_dp - 1], refs[n_dp - 1], refs[n_dp]
    rank = own.shape[1]
    blocks = owner.shape[0]
    rows = act.shape[0] // blocks
    gather_maps(n_dp, table, own, gots, wide)
    full = nt(act[...], wide[...])
    lane_slot = lax.broadcasted_iota(jnp.int32, (rows, n_dp * rank), 1) // rank
    folded = []
    for b in range(blocks):
        kept = jnp.where(lane_slot == slot_of(owner, b, n_dp), full[b * rows:(b + 1) * rows], 0.0)
        total = kept[:, :rank]
        for s in range(1, n_dp):
            total = total + kept[:, s * rank:(s + 1) * rank]
        folded.append(total)
    for j in range(blocks // 2):
        pair = jnp.concatenate([folded[2 * j], folded[2 * j + 1]], axis=1)
        out[j * rows:(j + 1) * rows, :] = pair.astype(BF16)


def grad_kernel(n_dp, n_part, n_behind, owner, act, *refs):
    refs = refs[n_behind:]
    parts, grads, wide = refs[:n_part], refs[n_part:n_part + n_dp], refs[n_part + n_dp]
    rank = wide.shape[1] // n_dp
    blocks = owner.shape[0]
    rows = act.shape[0] // blocks
    total = parts[0][...].astype(F32)
    for part in parts[1:]:
        total = total + part[...].astype(F32)
    lane_slot = lax.broadcasted_iota(jnp.int32, (rows, n_dp * rank), 1) // rank
    for b in range(blocks):
        one = total[(b // 2) * rows:(b // 2 + 1) * rows, (b % 2) * rank:(b % 2 + 1) * rank]
        spread = jnp.concatenate([one] * n_dp, axis=1)
        kept = jnp.where(lane_slot == slot_of(owner, b, n_dp), spread, 0.0)
        wide[b * rows:(b + 1) * rows, :] = kept.astype(BF16)
    full = tn(wide[...], act[...])
    for s in range(n_dp):
        grads[s][...] = full[s * rank:(s + 1) * rank].astype(BF16)


def send_kernel(n_pair, feat, n_mp, _, __, x, *refs):
    n_other = n_mp - 1
    pieces, outs, rows = refs[:n_other * n_pair], refs[n_other * n_pair:n_other * n_pair + n_other], refs[-n_other:]
    part = feat // n_pair

    @pl.when(pl.program_id(0) == 0)
    def _():
        for s in range(n_other):
            for q in range(n_pair):
                at = lax.rem(lax.axis_index("pair") + n_pair - q, n_pair) * part
                rows[s][pl.ds(pl.multiple_of(at, part), part), :] = pieces[s * n_pair + q][...]

    for s in range(n_other):
        outs[s][...] = nn(x[...], rows[s][...]).astype(BF16)


def back_kernel(n_dp, n_mp, table, *refs):
    w, gys, rows, wide, own_down, downs, out, picks, own, maps = (
        refs[0], refs[1:1 + n_mp], refs[1 + n_mp:2 * n_mp], refs[2 * n_mp], refs[2 * n_mp + 1],
        refs[2 * n_mp + 2:-4], refs[-4], refs[-3], refs[-2], refs[-1],
    )
    feat = out.shape[1]

    @pl.when(pl.program_id(0) == 0)
    def _():
        row = lax.broadcasted_iota(jnp.int32, picks.shape, 0)
        sites = jnp.zeros(picks.shape, jnp.int32)
        for k in range(n_dp * lax.axis_size("pair")):
            sites = jnp.where(row == k, wanted_site(table, n_dp, k % n_dp, k // n_dp), sites)
        picks[...] = sites
        own[...] = w[pl.ds(pl.multiple_of(lax.axis_index("mp") * feat, feat), feat), :]
        gather_maps(n_dp, table, own_down, downs, maps)

    total = nt(gys[0][...], own[...]) + SCALE * nn(wide[...], maps[...])
    for gy, row in zip(gys[1:], rows):
        total = total + nt(gy[...], row[...])
    out[...] = total.astype(BF16)


def own_kernel(n_dp, table, w, x, wide, own_up, *refs):
    ups, out, maps = refs[:n_dp - 1], refs[n_dp - 1], refs[n_dp]
    feat = x.shape[1]

    @pl.when(pl.program_id(0) == 0)
    def _():
        gather_maps(n_dp, table, own_up, ups, maps)

    own = w[pl.ds(pl.multiple_of(lax.axis_index("mp") * feat, feat), feat), :]
    out[...] = (nn(x[...], own) + SCALE * nn(wide[...], maps[...])).astype(BF16)


def pick_sum(grads, picks, site):
    total = jnp.zeros(grads[0].shape, F32)
    for k, grad in enumerate(grads):
        total = total + jnp.where(picks[k:k + 1, :1] == site, grad[...].astype(F32), 0.0)
    return total


def site_kernel(picks, _, *refs):
    grads, out = refs[:-1], refs[-1]
    for site in range(out.shape[0]):
        out[site] = pick_sum(grads, picks, site).astype(BF16)


def last_kernel(cuts, n_pair, n_ups, n_mp, picks, *refs):
    downs, ups, parts = refs[:n_pair], refs[n_pair:n_pair + n_ups], refs[n_pair + n_ups:n_pair + n_ups + n_mp]
    down, up, y = refs[-3:]
    total = downs[0][0].astype(F32)
    for part in downs[1:]:
        total = total + part[0].astype(F32)
    down[0] = SCALE * total
    up[0] = SCALE * pick_sum(ups, picks, pl.program_id(0) // cuts)
    total = parts[0][...].astype(F32)
    for part in parts[1:]:
        total = total + part[...].astype(F32)
    y[...] = total.astype(BF16)


def shards(x, w, down, up, gy, owner, table):
    tok, feat = x.shape
    cols = w.shape[1]
    sites, rank = up.shape[:2]
    n_dp, n_mp, n_pair = (lax.axis_size(a) for a in ("dp", "mp", "pair"))
    n_other = n_mp - 1
    down = down.transpose(0, 2, 1)
    part = feat // n_pair
    tile = tok // TILES
    row_block = lambda width: pl.BlockSpec((tile, width), lambda i: (i, 0))
    whole = lambda *dims: pl.BlockSpec(dims, lambda i: (0,) * len(dims))

    away = n_dp - 1
    def sent_rows(s):
        return lambda i: (lax.rem(lax.axis_index("mp") + s, n_mp) * n_pair + lax.axis_index("pair"), 0)

    packed = call(
        functools.partial(pack_kernel, n_dp, n_mp), "pack",
        [shape(rank, cols)] * away + [shape(rank, feat)] * away + [shape(part, cols)] * n_other,
        [SMEM, whole(*down.shape), whole(*up.shape)] + [pl.BlockSpec((part, cols), sent_rows(s)) for s in range(1, n_mp)],
        [ANY] * (2 * away + n_other),
        [pltpu.SemaphoreType.DMA((2 * away + n_other,))], mib=60, grid=(1,),
    )(table, down, up, *[w] * n_other)
    pieces = [shift(packed[2 * away + s - 1], "mp", s) for s in range(1, n_mp)]
    ups = [swap(packed[s - 1], "dp", s) for s in range(1, n_dp)]
    downs = [swap(after(packed[away + s - 1], ups[away - 1]), "dp", s) for s in range(1, n_dp)]

    def low_rank(act, own, maps, behind, name):
        mine = call(
            functools.partial(reduce_kernel, n_dp), name + "_part",
            shape(tok // 2, 2 * rank), [SMEM, SMEM, VMEM, ANY] + [VMEM] * n_dp, VMEM,
            [pltpu.VMEM((n_dp * rank, act.shape[1]), BF16)],
        )(owner, table, act, behind, own, *maps)
        return [mine] + [shift(mine, "mp", s) for s in range(1, n_mp)]

    def gradient(act, parts, behind, name, flops):
        *grads, wide = call(
            functools.partial(grad_kernel, n_dp, n_mp, len(behind)), name + "_grad",
            [shape(rank, act.shape[1])] * n_dp + [shape(tok, n_dp * rank)],
            [SMEM, VMEM] + [ANY] * len(behind) + [VMEM] * n_mp, [VMEM] * (n_dp + 1), flops=flops,
        )(owner, act, *behind, *parts)
        return [grads[0]] + [swap(grads[s], "dp", s) for s in range(1, n_dp)], wide

    h_parts = low_rank(gy, up, ups, ups[0], "h")
    gy_got = [shift(after(gy, *pieces), "mp", s) for s in range(1, n_mp)]
    down_back, h_wide = gradient(x, h_parts, downs, "down", GRAD_COST)
    parts = []
    for piece in pieces:
        parts += [piece] + [shift(after(piece, h_wide), "pair", q) for q in range(1, n_pair)]
    u_parts = low_rank(x, down, downs, parts[-1], "u")


    sent = call(
        functools.partial(send_kernel, n_pair, feat, n_mp), "y_send",
        [shape(tok, cols)] * n_other + [shape(feat, cols)] * n_other,
        [ANY, ANY, row_block(feat)] + [whole(part, cols)] * len(parts),
        [row_block(cols)] * n_other + [whole(feat, cols)] * n_other,
        grid=(TILES,),
    )(u_parts[0], h_wide, x, *parts)
    w_rows = sent[n_other:]
    y_got = [shift(after(sent[s - 1], down_back[1]), "mp", n_mp - s) for s in range(1, n_mp)]
    back, picks = call(
        functools.partial(back_kernel, n_dp, n_mp), "back",
        [shape(tok, feat), shape(-(-n_dp * n_pair // 8) * 8, 128, dtype=jnp.int32)],
        [SMEM, whole(*w.shape)] + [row_block(cols)] * n_mp + [whole(feat, cols)] * n_other
        + [row_block(n_dp * rank), whole(*down.shape)] + [whole(rank, feat)] * away,
        [row_block(feat), whole(-(-n_dp * n_pair // 8) * 8, 128)],
        [pltpu.VMEM((feat, cols), BF16), pltpu.VMEM((n_dp * rank, feat), BF16)], grid=(TILES,),
    )(table, w, gy, *gy_got, *w_rows, h_wide, down, *downs)
    up_back, u_wide = gradient(gy, u_parts, [picks] + down_back[1:] + gy_got, "up", GRAD_COST)

    y_own = call(
        functools.partial(own_kernel, n_dp), "y_own", shape(tok, cols),
        [SMEM, whole(*w.shape), row_block(feat), row_block(n_dp * rank), whole(*up.shape)]
        + [whole(rank, cols)] * away,
        row_block(cols), [pltpu.VMEM((n_dp * rank, cols), BF16)], grid=(TILES,), flops=GRAD_COST,
    )(table, w, x, u_wide, up, *ups)

    summed = call(
        site_kernel, "sites", shape(sites, rank, feat), [VMEM, ANY] + [VMEM] * n_dp, VMEM,
    )(picks, up_back[0], *down_back)
    both = [summed] + [shift(summed, "pair", q) for q in range(1, n_pair)]
    up_all = [shift(after(one, y_own), "pair", q) if q else one for q in range(n_pair) for one in up_back]
    cuts = 2
    rows = tok // (sites * cuts)
    of_site = lambda width: pl.BlockSpec((1, rank // cuts, width), lambda i: (i // cuts, i % cuts, 0))
    of_slot = pl.BlockSpec((rank // cuts, cols), lambda i: (i % cuts, 0))
    out_rows = pl.BlockSpec((rows, cols), lambda i: (i, 0))
    down_grad, up_grad, y = call(
        functools.partial(last_kernel, cuts, n_pair, n_pair * n_dp, n_mp), "last",
        [shape(sites, rank, feat, dtype=F32), shape(sites, rank, cols, dtype=F32), shape(tok, cols)],
        [whole(*picks.shape)] + [of_site(feat)] * n_pair + [of_slot] * (n_pair * n_dp) + [out_rows] * n_mp,
        [of_site(feat), of_site(cols), out_rows], grid=(sites * cuts,),
    )(picks, *both, *up_all, y_own, *y_got)
    return y, back, down_grad.transpose(0, 2, 1), up_grad


def solution(mesh):
    rows = P(("groups", "dp", "pair"), "mp")
    in_specs = (
        rows,
        P(None, "mp"),
        P(("groups", "dp"), "mp", None),
        P(("groups", "dp"), None, "mp"),
        rows,
        P(("groups", "dp", "pair")),
        P(("groups", "dp"), None, None),
    )
    out_specs = (rows, rows, P(("groups", "dp"), "mp", None), P(("groups", "dp"), None, "mp"))
    return jax.shard_map(shards, mesh=mesh, in_specs=in_specs, out_specs=out_specs, check_vma=False)
```

```python
import functools

import jax
import jax.numpy as jnp
from jax import lax
from jax.experimental import pallas as pl
from jax.experimental.pallas import tpu as pltpu
from jax.sharding import PartitionSpec as P

SCALE = 2.0
TILES = 3
GRAD_COST = 15_000_000_000
F32 = jnp.float32
BF16 = jnp.bfloat16
SMEM = pl.BlockSpec(memory_space=pltpu.SMEM)
VMEM = pl.BlockSpec(memory_space=pltpu.VMEM)
ANY = pl.BlockSpec(memory_space=pl.ANY)


def shape(*dims, dtype=BF16):
    return jax.ShapeDtypeStruct(dims, dtype)


def call(kernel, name, out_shape, in_specs, out_specs, scratch=(), grid=(), mib=32, flops=1):
    return pl.pallas_call(
        kernel, name=name, out_shape=out_shape, grid=grid, in_specs=in_specs, out_specs=out_specs,
        scratch_shapes=scratch,
        compiler_params=pltpu.CompilerParams(vmem_limit_bytes=mib * 1024 * 1024),
        cost_estimate=pl.CostEstimate(flops=flops, bytes_accessed=1, transcendentals=0),
    )


def shift(value, axis, by):
    size = lax.axis_size(axis)
    return lax.ppermute(value, axis, [(i, (i + by) % size) for i in range(size)])


def swap(value, axis, mask):
    return lax.ppermute(value, axis, [(i, i ^ mask) for i in range(lax.axis_size(axis))])


def after(value, *others):
    return lax.optimization_barrier((value, *others))[0]


def nn(a, b):
    return lax.dot_general(a, b, (((1,), (0,)), ((), ())), preferred_element_type=F32)


def nt(a, b):
    return lax.dot_general(a, b, (((1,), (1,)), ((), ())), preferred_element_type=F32)


def tn(a, b):
    return lax.dot_general(a, b, (((0,), (0,)), ((), ())), preferred_element_type=F32)


def wanted_site(table, n_dp, s, q=0):
    n_pair = lax.axis_size("pair")
    core = lax.rem(lax.axis_index("pair") + n_pair - q, n_pair)
    return table[0, core, lax.bitwise_xor(lax.axis_index("dp"), s)]


def slot_of(owner, b, n_dp):
    return lax.bitwise_xor(lax.axis_index("dp"), owner[b])


def pack_kernel(n_dp, n_mp, table, down, up, *refs):
    away, n_other = n_dp - 1, n_mp - 1
    rows, refs, sem = refs[:n_other], refs[n_other:-1], refs[-1]
    ups, downs, pieces = refs[:away], refs[away:2 * away], refs[2 * away:]
    copies = [pltpu.make_async_copy(rows[s], pieces[s], sem.at[s]) for s in range(n_other)]
    for s in range(away):
        site = wanted_site(table, n_dp, s + 1)
        copies.append(pltpu.make_async_copy(up.at[site], ups[s], sem.at[n_other + s]))
        copies.append(pltpu.make_async_copy(down.at[site], downs[s], sem.at[n_other + away + s]))
    for copy in copies:
        copy.start()
    for copy in copies:
        copy.wait()


def gather_maps(n_dp, table, own, gots, wide):
    rank = own.shape[1]
    wide[:rank, :] = own[wanted_site(table, n_dp, 0)]
    for s in range(1, n_dp):
        wide[s * rank:(s + 1) * rank, :] = gots[s - 1][...]


def reduce_kernel(n_dp, owner, table, act, _, own, *refs):
    gots, out, wide = refs[:n_dp - 1], refs[n_dp - 1], refs[n_dp]
    rank = own.shape[1]
    blocks = owner.shape[0]
    rows = act.shape[0] // blocks
    gather_maps(n_dp, table, own, gots, wide)
    full = nt(act[...], wide[...])
    lane_slot = lax.broadcasted_iota(jnp.int32, (rows, n_dp * rank), 1) // rank
    folded = []
    for b in range(blocks):
        kept = jnp.where(lane_slot == slot_of(owner, b, n_dp), full[b * rows:(b + 1) * rows], 0.0)
        total = kept[:, :rank]
        for s in range(1, n_dp):
            total = total + kept[:, s * rank:(s + 1) * rank]
        folded.append(total)
    for j in range(blocks // 2):
        pair = jnp.concatenate([folded[2 * j], folded[2 * j + 1]], axis=1)
        out[j * rows:(j + 1) * rows, :] = pair.astype(BF16)


def grad_kernel(n_dp, n_part, n_behind, owner, act, *refs):
    refs = refs[n_behind:]
    parts, grads, wide = refs[:n_part], refs[n_part:n_part + n_dp], refs[n_part + n_dp]
    rank = wide.shape[1] // n_dp
    blocks = owner.shape[0]
    rows = act.shape[0] // blocks
    total = parts[0][...].astype(F32)
    for part in parts[1:]:
        total = total + part[...].astype(F32)
    lane_slot = lax.broadcasted_iota(jnp.int32, (rows, n_dp * rank), 1) // rank
    for b in range(blocks):
        one = total[(b // 2) * rows:(b // 2 + 1) * rows, (b % 2) * rank:(b % 2 + 1) * rank]
        spread = jnp.concatenate([one] * n_dp, axis=1)
        kept = jnp.where(lane_slot == slot_of(owner, b, n_dp), spread, 0.0)
        wide[b * rows:(b + 1) * rows, :] = kept.astype(BF16)
    full = tn(wide[...], act[...])
    for s in range(n_dp):
        grads[s][...] = full[s * rank:(s + 1) * rank].astype(BF16)


def send_kernel(n_pair, feat, n_mp, _, __, x, *refs):
    n_other = n_mp - 1
    pieces, outs, rows = refs[:n_other * n_pair], refs[n_other * n_pair:n_other * n_pair + n_other], refs[-n_other:]
    part = feat // n_pair

    @pl.when(pl.program_id(0) == 0)
    def _():
        for s in range(n_other):
            for q in range(n_pair):
                at = lax.rem(lax.axis_index("pair") + n_pair - q, n_pair) * part
                rows[s][pl.ds(pl.multiple_of(at, part), part), :] = pieces[s * n_pair + q][...]

    for s in range(n_other):
        outs[s][...] = nn(x[...], rows[s][...]).astype(BF16)


def back_kernel(n_dp, n_mp, table, *refs):
    w, gys, rows, wide, own_down, downs, out, picks, own, maps = (
        refs[0], refs[1:1 + n_mp], refs[1 + n_mp:2 * n_mp], refs[2 * n_mp], refs[2 * n_mp + 1],
        refs[2 * n_mp + 2:-4], refs[-4], refs[-3], refs[-2], refs[-1],
    )
    feat = out.shape[1]

    @pl.when(pl.program_id(0) == 0)
    def _():
        row = lax.broadcasted_iota(jnp.int32, picks.shape, 0)
        sites = jnp.zeros(picks.shape, jnp.int32)
        for k in range(n_dp * lax.axis_size("pair")):
            sites = jnp.where(row == k, wanted_site(table, n_dp, k % n_dp, k // n_dp), sites)
        picks[...] = sites
        own[...] = w[pl.ds(pl.multiple_of(lax.axis_index("mp") * feat, feat), feat), :]
        gather_maps(n_dp, table, own_down, downs, maps)

    total = nt(gys[0][...], own[...]) + SCALE * nn(wide[...], maps[...])
    for gy, row in zip(gys[1:], rows):
        total = total + nt(gy[...], row[...])
    out[...] = total.astype(BF16)


def own_kernel(n_dp, table, w, x, wide, own_up, *refs):
    ups, out, maps = refs[:n_dp - 1], refs[n_dp - 1], refs[n_dp]
    feat = x.shape[1]

    @pl.when(pl.program_id(0) == 0)
    def _():
        gather_maps(n_dp, table, own_up, ups, maps)

    own = w[pl.ds(pl.multiple_of(lax.axis_index("mp") * feat, feat), feat), :]
    out[...] = (nn(x[...], own) + SCALE * nn(wide[...], maps[...])).astype(BF16)


def pick_sum(grads, picks, site):
    total = jnp.zeros(grads[0].shape, F32)
    for k, grad in enumerate(grads):
        total = total + jnp.where(picks[k:k + 1, :1] == site, grad[...].astype(F32), 0.0)
    return total


def site_kernel(picks, _, *refs):
    grads, out = refs[:-1], refs[-1]
    for site in range(out.shape[0]):
        out[site] = pick_sum(grads, picks, site).astype(BF16)


def last_kernel(n_pair, n_ups, n_mp, picks, *refs):
    downs, ups, parts = refs[:n_pair], refs[n_pair:n_pair + n_ups], refs[n_pair + n_ups:n_pair + n_ups + n_mp]
    down, up, y = refs[-3:]
    for site in range(up.shape[0]):
        total = downs[0][site].astype(F32)
        for part in downs[1:]:
            total = total + part[site].astype(F32)
        down[site] = SCALE * total
        up[site] = SCALE * pick_sum(ups, picks, site)
    total = parts[0][...].astype(F32)
    for part in parts[1:]:
        total = total + part[...].astype(F32)
    y[...] = total.astype(BF16)


def shards(x, w, down, up, gy, owner, table):
    tok, feat = x.shape
    cols = w.shape[1]
    sites, rank = up.shape[:2]
    n_dp, n_mp, n_pair = (lax.axis_size(a) for a in ("dp", "mp", "pair"))
    n_other = n_mp - 1
    down = down.transpose(0, 2, 1)
    part = feat // n_pair
    tile = tok // TILES
    row_block = lambda width: pl.BlockSpec((tile, width), lambda i: (i, 0))
    whole = lambda *dims: pl.BlockSpec(dims, lambda i: (0,) * len(dims))

    away = n_dp - 1
    def sent_rows(s):
        return lambda i: (lax.rem(lax.axis_index("mp") + s, n_mp) * n_pair + lax.axis_index("pair"), 0)

    packed = call(
        functools.partial(pack_kernel, n_dp, n_mp), "pack",
        [shape(rank, cols)] * away + [shape(rank, feat)] * away + [shape(part, cols)] * n_other,
        [SMEM, whole(*down.shape), whole(*up.shape)] + [pl.BlockSpec((part, cols), sent_rows(s)) for s in range(1, n_mp)],
        [ANY] * (2 * away + n_other),
        [pltpu.SemaphoreType.DMA((2 * away + n_other,))], mib=60, grid=(1,),
    )(table, down, up, *[w] * n_other)
    pieces = [shift(packed[2 * away + s - 1], "mp", s) for s in range(1, n_mp)]
    ups = [swap(packed[s - 1], "dp", s) for s in range(1, n_dp)]
    downs = [swap(after(packed[away + s - 1], ups[away - 1]), "dp", s) for s in range(1, n_dp)]

    def low_rank(act, own, maps, behind, name):
        mine = call(
            functools.partial(reduce_kernel, n_dp), name + "_part",
            shape(tok // 2, 2 * rank), [SMEM, SMEM, VMEM, ANY] + [VMEM] * n_dp, VMEM,
            [pltpu.VMEM((n_dp * rank, act.shape[1]), BF16)],
        )(owner, table, act, behind, own, *maps)
        return [mine] + [shift(mine, "mp", s) for s in range(1, n_mp)]

    def gradient(act, parts, behind, name, flops):
        *grads, wide = call(
            functools.partial(grad_kernel, n_dp, n_mp, len(behind)), name + "_grad",
            [shape(rank, act.shape[1])] * n_dp + [shape(tok, n_dp * rank)],
            [SMEM, VMEM] + [ANY] * len(behind) + [VMEM] * n_mp, [VMEM] * (n_dp + 1), flops=flops,
        )(owner, act, *behind, *parts)
        return [grads[0]] + [swap(grads[s], "dp", s) for s in range(1, n_dp)], wide

    h_parts = low_rank(gy, up, ups, ups[0], "h")
    gy_got = [shift(after(gy, *pieces), "mp", s) for s in range(1, n_mp)]
    down_back, h_wide = gradient(x, h_parts, downs, "down", GRAD_COST)
    parts = []
    for piece in pieces:
        parts += [piece] + [shift(after(piece, h_wide), "pair", q) for q in range(1, n_pair)]
    u_parts = low_rank(x, down, downs, parts[-1], "u")


    sent = call(
        functools.partial(send_kernel, n_pair, feat, n_mp), "y_send",
        [shape(tok, cols)] * n_other + [shape(feat, cols)] * n_other,
        [ANY, ANY, row_block(feat)] + [whole(part, cols)] * len(parts),
        [row_block(cols)] * n_other + [whole(feat, cols)] * n_other,
        grid=(TILES,),
    )(u_parts[0], h_wide, x, *parts)
    w_rows = sent[n_other:]
    y_got = [shift(after(sent[s - 1], down_back[1]), "mp", n_mp - s) for s in range(1, n_mp)]
    back, picks = call(
        functools.partial(back_kernel, n_dp, n_mp), "back",
        [shape(tok, feat), shape(-(-n_dp * n_pair // 8) * 8, 128, dtype=jnp.int32)],
        [SMEM, whole(*w.shape)] + [row_block(cols)] * n_mp + [whole(feat, cols)] * n_other
        + [row_block(n_dp * rank), whole(*down.shape)] + [whole(rank, feat)] * away,
        [row_block(feat), whole(-(-n_dp * n_pair // 8) * 8, 128)],
        [pltpu.VMEM((feat, cols), BF16), pltpu.VMEM((n_dp * rank, feat), BF16)], grid=(TILES,),
    )(table, w, gy, *gy_got, *w_rows, h_wide, down, *downs)
    up_back, u_wide = gradient(gy, u_parts, [picks] + down_back[1:] + gy_got, "up", GRAD_COST)

    y_own = call(
        functools.partial(own_kernel, n_dp), "y_own", shape(tok, cols),
        [SMEM, whole(*w.shape), row_block(feat), row_block(n_dp * rank), whole(*up.shape)]
        + [whole(rank, cols)] * away,
        row_block(cols), [pltpu.VMEM((n_dp * rank, cols), BF16)], grid=(TILES,), flops=GRAD_COST,
    )(table, w, x, u_wide, up, *ups)

    summed = call(
        site_kernel, "sites", shape(sites, rank, feat), [VMEM, ANY] + [VMEM] * n_dp, VMEM,
    )(picks, up_back[0], *down_back)
    both = [summed] + [shift(summed, "pair", q) for q in range(1, n_pair)]
    up_all = [shift(after(one, y_own), "pair", q) if q else one for q in range(n_pair) for one in up_back]
    down_grad, up_grad, y = call(
        functools.partial(last_kernel, n_pair, n_pair * n_dp, n_mp), "last",
        [shape(sites, rank, feat, dtype=F32), shape(sites, rank, cols, dtype=F32), shape(tok, cols)],
        [VMEM] * (1 + n_pair + n_pair * n_dp + n_mp), [VMEM] * 3,
    )(picks, *both, *up_all, y_own, *y_got)
    return y, back, down_grad.transpose(0, 2, 1), up_grad


def solution(mesh):
    rows = P(("groups", "dp", "pair"), "mp")
    in_specs = (
        rows,
        P(None, "mp"),
        P(("groups", "dp"), "mp", None),
        P(("groups", "dp"), None, "mp"),
        rows,
        P(("groups", "dp", "pair")),
        P(("groups", "dp"), None, None),
    )
    out_specs = (rows, rows, P(("groups", "dp"), "mp", None), P(("groups", "dp"), None, "mp"))
    return jax.shard_map(shards, mesh=mesh, in_specs=in_specs, out_specs=out_specs, check_vma=False)
```

```python
import functools

import jax
import jax.numpy as jnp
from jax import lax
from jax.experimental import pallas as pl
from jax.experimental.pallas import tpu as pltpu
from jax.sharding import PartitionSpec as P

SCALE = 2.0
TILES = 2
GRAD_COST = 15_000_000_000
F32 = jnp.float32
BF16 = jnp.bfloat16
SMEM = pl.BlockSpec(memory_space=pltpu.SMEM)
VMEM = pl.BlockSpec(memory_space=pltpu.VMEM)
ANY = pl.BlockSpec(memory_space=pl.ANY)


def shape(*dims, dtype=BF16):
    return jax.ShapeDtypeStruct(dims, dtype)


def call(kernel, name, out_shape, in_specs, out_specs, scratch=(), grid=(), mib=32, flops=1):
    return pl.pallas_call(
        kernel, name=name, out_shape=out_shape, grid=grid, in_specs=in_specs, out_specs=out_specs,
        scratch_shapes=scratch,
        compiler_params=pltpu.CompilerParams(vmem_limit_bytes=mib * 1024 * 1024),
        cost_estimate=pl.CostEstimate(flops=flops, bytes_accessed=1, transcendentals=0),
    )


def shift(value, axis, by):
    size = lax.axis_size(axis)
    return lax.ppermute(value, axis, [(i, (i + by) % size) for i in range(size)])


def swap(value, axis, mask):
    return lax.ppermute(value, axis, [(i, i ^ mask) for i in range(lax.axis_size(axis))])


def after(value, *others):
    return lax.optimization_barrier((value, *others))[0]


def nn(a, b):
    return lax.dot_general(a, b, (((1,), (0,)), ((), ())), preferred_element_type=F32)


def nt(a, b):
    return lax.dot_general(a, b, (((1,), (1,)), ((), ())), preferred_element_type=F32)


def tn(a, b):
    return lax.dot_general(a, b, (((0,), (0,)), ((), ())), preferred_element_type=F32)


def wanted_site(table, n_dp, s, q=0):
    n_pair = lax.axis_size("pair")
    core = lax.rem(lax.axis_index("pair") + n_pair - q, n_pair)
    return table[0, core, lax.bitwise_xor(lax.axis_index("dp"), s)]


def slot_of(owner, b, n_dp):
    return lax.bitwise_xor(lax.axis_index("dp"), owner[b])


def pack_kernel(n_dp, n_mp, table, down, up, *refs):
    away, n_other = n_dp - 1, n_mp - 1
    rows, refs, sem = refs[:n_other], refs[n_other:-1], refs[-1]
    ups, downs, pieces = refs[:away], refs[away:2 * away], refs[2 * away:]
    copies = [pltpu.make_async_copy(rows[s], pieces[s], sem.at[s]) for s in range(n_other)]
    for s in range(away):
        site = wanted_site(table, n_dp, s + 1)
        copies.append(pltpu.make_async_copy(up.at[site], ups[s], sem.at[n_other + s]))
        copies.append(pltpu.make_async_copy(down.at[site], downs[s], sem.at[n_other + away + s]))
    for copy in copies:
        copy.start()
    for copy in copies:
        copy.wait()


def gather_maps(n_dp, table, own, gots, wide):
    rank = own.shape[1]
    wide[:rank, :] = own[wanted_site(table, n_dp, 0)]
    for s in range(1, n_dp):
        wide[s * rank:(s + 1) * rank, :] = gots[s - 1][...]


def reduce_kernel(n_dp, owner, table, act, _, own, *refs):
    gots, out, wide = refs[:n_dp - 1], refs[n_dp - 1], refs[n_dp]
    rank = own.shape[1]
    blocks = owner.shape[0]
    rows = act.shape[0] // blocks
    gather_maps(n_dp, table, own, gots, wide)
    full = nt(act[...], wide[...])
    lane_slot = lax.broadcasted_iota(jnp.int32, (rows, n_dp * rank), 1) // rank
    folded = []
    for b in range(blocks):
        kept = jnp.where(lane_slot == slot_of(owner, b, n_dp), full[b * rows:(b + 1) * rows], 0.0)
        total = kept[:, :rank]
        for s in range(1, n_dp):
            total = total + kept[:, s * rank:(s + 1) * rank]
        folded.append(total)
    for j in range(blocks // 2):
        pair = jnp.concatenate([folded[2 * j], folded[2 * j + 1]], axis=1)
        out[j * rows:(j + 1) * rows, :] = pair.astype(BF16)


def grad_kernel(n_dp, n_part, n_behind, owner, act, *refs):
    refs = refs[n_behind:]
    parts, grads, wide = refs[:n_part], refs[n_part:n_part + n_dp], refs[n_part + n_dp]
    rank = wide.shape[1] // n_dp
    blocks = owner.shape[0]
    rows = act.shape[0] // blocks
    total = parts[0][...].astype(F32)
    for part in parts[1:]:
        total = total + part[...].astype(F32)
    lane_slot = lax.broadcasted_iota(jnp.int32, (rows, n_dp * rank), 1) // rank
    for b in range(blocks):
        one = total[(b // 2) * rows:(b // 2 + 1) * rows, (b % 2) * rank:(b % 2 + 1) * rank]
        spread = jnp.concatenate([one] * n_dp, axis=1)
        kept = jnp.where(lane_slot == slot_of(owner, b, n_dp), spread, 0.0)
        wide[b * rows:(b + 1) * rows, :] = kept.astype(BF16)
    full = tn(wide[...], act[...])
    for s in range(n_dp):
        grads[s][...] = full[s * rank:(s + 1) * rank].astype(BF16)


def send_kernel(n_pair, feat, n_mp, _, __, x, *refs):
    n_other = n_mp - 1
    pieces, outs, rows = refs[:n_other * n_pair], refs[n_other * n_pair:n_other * n_pair + n_other], refs[-n_other:]
    part = feat // n_pair

    @pl.when(pl.program_id(0) == 0)
    def _():
        for s in range(n_other):
            for q in range(n_pair):
                at = lax.rem(lax.axis_index("pair") + n_pair - q, n_pair) * part
                rows[s][pl.ds(pl.multiple_of(at, part), part), :] = pieces[s * n_pair + q][...]

    for s in range(n_other):
        outs[s][...] = nn(x[...], rows[s][...]).astype(BF16)


def back_kernel(n_dp, n_mp, table, *refs):
    w, gys, rows, wide, own_down, downs, out, picks, own, maps = (
        refs[0], refs[1:1 + n_mp], refs[1 + n_mp:2 * n_mp], refs[2 * n_mp], refs[2 * n_mp + 1],
        refs[2 * n_mp + 2:-4], refs[-4], refs[-3], refs[-2], refs[-1],
    )
    feat = out.shape[1]

    @pl.when(pl.program_id(0) == 0)
    def _():
        row = lax.broadcasted_iota(jnp.int32, picks.shape, 0)
        sites = jnp.zeros(picks.shape, jnp.int32)
        for k in range(n_dp * lax.axis_size("pair")):
            sites = jnp.where(row == k, wanted_site(table, n_dp, k % n_dp, k // n_dp), sites)
        picks[...] = sites
        own[...] = w[pl.ds(pl.multiple_of(lax.axis_index("mp") * feat, feat), feat), :]
        gather_maps(n_dp, table, own_down, downs, maps)

    total = nt(gys[0][...], own[...]) + SCALE * nn(wide[...], maps[...])
    for gy, row in zip(gys[1:], rows):
        total = total + nt(gy[...], row[...])
    out[...] = total.astype(BF16)


def own_kernel(n_dp, table, w, x, wide, own_up, *refs):
    ups, out, maps = refs[:n_dp - 1], refs[n_dp - 1], refs[n_dp]
    feat = x.shape[1]

    @pl.when(pl.program_id(0) == 0)
    def _():
        gather_maps(n_dp, table, own_up, ups, maps)

    own = w[pl.ds(pl.multiple_of(lax.axis_index("mp") * feat, feat), feat), :]
    out[...] = (nn(x[...], own) + SCALE * nn(wide[...], maps[...])).astype(BF16)


def pick_sum(grads, picks, site):
    total = jnp.zeros(grads[0].shape, F32)
    for k, grad in enumerate(grads):
        total = total + jnp.where(picks[k:k + 1, :1] == site, grad[...].astype(F32), 0.0)
    return total


def site_kernel(picks, _, *refs):
    grads, out = refs[:-1], refs[-1]
    for site in range(out.shape[0]):
        out[site] = pick_sum(grads, picks, site).astype(BF16)


def last_kernel(n_pair, n_ups, n_mp, picks, *refs):
    downs, ups, parts = refs[:n_pair], refs[n_pair:n_pair + n_ups], refs[n_pair + n_ups:n_pair + n_ups + n_mp]
    down, up, y = refs[-3:]
    total = downs[0][0].astype(F32)
    for part in downs[1:]:
        total = total + part[0].astype(F32)
    down[0] = SCALE * total
    up[0] = SCALE * pick_sum(ups, picks, pl.program_id(0))
    total = parts[0][...].astype(F32)
    for part in parts[1:]:
        total = total + part[...].astype(F32)
    y[...] = total.astype(BF16)


def shards(x, w, down, up, gy, owner, table):
    tok, feat = x.shape
    cols = w.shape[1]
    sites, rank = up.shape[:2]
    n_dp, n_mp, n_pair = (lax.axis_size(a) for a in ("dp", "mp", "pair"))
    n_other = n_mp - 1
    down = down.transpose(0, 2, 1)
    part = feat // n_pair
    tile = tok // TILES
    row_block = lambda width: pl.BlockSpec((tile, width), lambda i: (i, 0))
    whole = lambda *dims: pl.BlockSpec(dims, lambda i: (0,) * len(dims))

    away = n_dp - 1
    def sent_rows(s):
        return lambda i: (lax.rem(lax.axis_index("mp") + s, n_mp) * n_pair + lax.axis_index("pair"), 0)

    packed = call(
        functools.partial(pack_kernel, n_dp, n_mp), "pack",
        [shape(rank, cols)] * away + [shape(rank, feat)] * away + [shape(part, cols)] * n_other,
        [SMEM, whole(*down.shape), whole(*up.shape)] + [pl.BlockSpec((part, cols), sent_rows(s)) for s in range(1, n_mp)],
        [ANY] * (2 * away + n_other),
        [pltpu.SemaphoreType.DMA((2 * away + n_other,))], mib=60, grid=(1,),
    )(table, down, up, *[w] * n_other)
    pieces = [shift(packed[2 * away + s - 1], "mp", s) for s in range(1, n_mp)]
    ups = [swap(packed[s - 1], "dp", s) for s in range(1, n_dp)]
    downs = [swap(after(packed[away + s - 1], ups[away - 1]), "dp", s) for s in range(1, n_dp)]

    def low_rank(act, own, maps, behind, name):
        mine = call(
            functools.partial(reduce_kernel, n_dp), name + "_part",
            shape(tok // 2, 2 * rank), [SMEM, SMEM, VMEM, ANY] + [VMEM] * n_dp, VMEM,
            [pltpu.VMEM((n_dp * rank, act.shape[1]), BF16)],
        )(owner, table, act, behind, own, *maps)
        return [mine] + [shift(mine, "mp", s) for s in range(1, n_mp)]

    def gradient(act, parts, behind, name, flops):
        *grads, wide = call(
            functools.partial(grad_kernel, n_dp, n_mp, len(behind)), name + "_grad",
            [shape(rank, act.shape[1])] * n_dp + [shape(tok, n_dp * rank)],
            [SMEM, VMEM] + [ANY] * len(behind) + [VMEM] * n_mp, [VMEM] * (n_dp + 1), flops=flops,
        )(owner, act, *behind, *parts)
        return [grads[0]] + [swap(grads[s], "dp", s) for s in range(1, n_dp)], wide

    h_parts = low_rank(gy, up, ups, ups[0], "h")
    gy_got = [shift(after(gy, *pieces), "mp", s) for s in range(1, n_mp)]
    down_back, h_wide = gradient(x, h_parts, downs, "down", GRAD_COST)
    parts = []
    for piece in pieces:
        parts += [piece] + [shift(after(piece, h_wide), "pair", q) for q in range(1, n_pair)]
    u_parts = low_rank(x, down, downs, parts[-1], "u")


    sent = call(
        functools.partial(send_kernel, n_pair, feat, n_mp), "y_send",
        [shape(tok, cols)] * n_other + [shape(feat, cols)] * n_other,
        [ANY, ANY, row_block(feat)] + [whole(part, cols)] * len(parts),
        [row_block(cols)] * n_other + [whole(feat, cols)] * n_other,
        grid=(TILES,),
    )(u_parts[0], h_wide, x, *parts)
    w_rows = sent[n_other:]
    y_got = [shift(after(sent[s - 1], down_back[1]), "mp", n_mp - s) for s in range(1, n_mp)]
    back, picks = call(
        functools.partial(back_kernel, n_dp, n_mp), "back",
        [shape(tok, feat), shape(-(-n_dp * n_pair // 8) * 8, 128, dtype=jnp.int32)],
        [SMEM, whole(*w.shape)] + [row_block(cols)] * n_mp + [whole(feat, cols)] * n_other
        + [row_block(n_dp * rank), whole(*down.shape)] + [whole(rank, feat)] * away,
        [row_block(feat), whole(-(-n_dp * n_pair // 8) * 8, 128)],
        [pltpu.VMEM((feat, cols), BF16), pltpu.VMEM((n_dp * rank, feat), BF16)], grid=(TILES,),
    )(table, w, gy, *gy_got, *w_rows, h_wide, down, *downs)
    up_back, u_wide = gradient(gy, u_parts, [picks] + down_back[1:] + gy_got, "up", GRAD_COST)

    y_own = call(
        functools.partial(own_kernel, n_dp), "y_own", shape(tok, cols),
        [SMEM, whole(*w.shape), row_block(feat), row_block(n_dp * rank), whole(*up.shape)]
        + [whole(rank, cols)] * away,
        row_block(cols), [pltpu.VMEM((n_dp * rank, cols), BF16)], grid=(TILES,), flops=GRAD_COST,
    )(table, w, x, u_wide, up, *ups)

    summed = call(
        site_kernel, "sites", shape(sites, rank, feat), [VMEM, ANY] + [VMEM] * n_dp, VMEM,
    )(picks, up_back[0], *down_back)
    both = [summed] + [shift(summed, "pair", q) for q in range(1, n_pair)]
    up_all = [shift(after(one, y_own), "pair", q) if q else one for q in range(n_pair) for one in up_back]
    rows = tok // sites
    of_site = lambda width: pl.BlockSpec((1, rank, width), lambda i: (i, 0, 0))
    out_rows = pl.BlockSpec((rows, cols), lambda i: (i, 0))
    down_grad, up_grad, y = call(
        functools.partial(last_kernel, n_pair, n_pair * n_dp, n_mp), "last",
        [shape(sites, rank, feat, dtype=F32), shape(sites, rank, cols, dtype=F32), shape(tok, cols)],
        [whole(*picks.shape)] + [of_site(feat)] * n_pair + [whole(rank, cols)] * (n_pair * n_dp) + [out_rows] * n_mp,
        [of_site(feat), of_site(cols), out_rows], grid=(sites,),
    )(picks, *both, *up_all, y_own, *y_got)
    return y, back, down_grad.transpose(0, 2, 1), up_grad


def solution(mesh):
    rows = P(("groups", "dp", "pair"), "mp")
    in_specs = (
        rows,
        P(None, "mp"),
        P(("groups", "dp"), "mp", None),
        P(("groups", "dp"), None, "mp"),
        rows,
        P(("groups", "dp", "pair")),
        P(("groups", "dp"), None, None),
    )
    out_specs = (rows, rows, P(("groups", "dp"), "mp", None), P(("groups", "dp"), None, "mp"))
    return jax.shard_map(shards, mesh=mesh, in_specs=in_specs, out_specs=out_specs, check_vma=False)
```
